256 devices in a mesh: dp: 16 (over x, y_hi, core), expert: 16 (over y_lo, z).
Axes of the slice: x: 4, y: 4 (y_hi: 2, y_lo: 2; y = y_hi * 2 + y_lo), z: 8, core: 2. Of those that a mesh axis runs over, the one named last changes fastest.
Arguments:
- tokens: bfloat16 [32768, 1024], P(('dp', 'expert')), may hold values from -6 to 6
- expert_ids: int32 [32768, 8], P(('dp', 'expert')), may hold values from 0 to 63, all different within a row; in each aligned block of 128 rows (0 to 127, 128 to 255, ...) at most 24 rows name the same one
- upstream: bfloat16 [32768, 1024], P(('dp', 'expert')), may hold values from -6 to 6
- router_weight: bfloat16 [1024, 64], replicated, may hold values from -0.1875 to 0.1875
- gate_matrix: bfloat16 [64, 384, 1024], P('expert'), may hold values from -0.1875 to 0.1875
- up_matrix: bfloat16 [64, 384, 1024], P('expert'), may hold values from -0.1875 to 0.1875
- down_matrix: bfloat16 [64, 384, 1024], P('expert'), may hold values from -0.3125 to 0.3125
Outputs:
- mixture: bfloat16 [32768, 1024], P(('dp', 'expert'))
- input_grad: bfloat16 [32768, 1024], P(('dp', 'expert'))
- router_grad: float32 [1024, 64], replicated
- gate_grad: float32 [64, 384, 1024], P('expert', 'dp')
- up_grad: float32 [64, 384, 1024], P('expert', 'dp')
- down_grad: float32 [64, 384, 1024], P('expert', 'dp')
The draws below stay inside these ranges and needn't reach their ends.
Inputs may be any that keep to these rules, and one draw needn't show every extreme that they name: `expert_ids`: each row names 8 different experts. Among the rows of one device no expert is named more than 24 times, a bound that some block reaches.
All inputs are finite; a program needn't handle non-finite values.
Results may differ from the reference program's by a relative error of at most 0.0063.
Values may be sent and summed in bfloat16 or wider, within the bound.
No kernel may reach another device: no remote copies, remote signals or barrier semaphores. Data moves between devices by JAX's collectives and lax.ppermute only.
A program may use at most 320 MiB of HBM per device.

```python
import math
import jax
import jax.numpy as jnp
import numpy as np
from jax import lax

D = 1024
FF = 384
TOP = 8
TOK_DEV = 128
EXPERTS = 64
CAP = 24
TOKENS = 32768


def block_scale(key, extent, pieces, low, top_value):
    gain, own = 1.0, jax.random.fold_in(key, 6)
    for axis_at, blocks in pieces:
        draws = jnp.exp(jax.random.uniform(jax.random.fold_in(own, axis_at), (blocks,), jnp.float32, low / len(pieces), top_value / len(pieces)))
        gain = gain * jnp.repeat(draws, extent[axis_at] // blocks).reshape([-1 if axis == axis_at else 1 for axis in range(len(extent))])
    return gain


def shared_out(rng, own, number, rows, amount, top, limit, skew):
    order = jax.random.permutation(rng, amount)
    crowded, usual = shares(amount, rows * top, limit, skew, True), shares(amount, rows * top, limit, skew, False)
    places = jnp.arange(amount)

    def named(sizes, rotation):
        used = int((sizes > 0).sum())
        fixed = max(1, used // 4)
        passed = fixed + (places - fixed + rotation * (used - fixed)) % max(1, amount - fixed)
        return jnp.zeros((amount,), jnp.int32).at[order[jnp.where(places < fixed, places, passed)]].set(jnp.asarray(sizes, jnp.int32))

    sizes = jnp.where(number % 4 == 0, named(crowded, number // 4), named(usual, number - number // 4 - 1))
    mixed = jax.random.permutation(jax.random.fold_in(own, 3), amount)
    source_of, taker = mixed[0:amount // 2 * 2:2], mixed[1:amount // 2 * 2:2]
    room = jnp.minimum(sizes[source_of] - 1, limit - sizes[taker]) // 2
    room = jnp.where((source_of == order[0]) | (taker == order[0]) | (sizes[taker] == 0), 0, jnp.maximum(room, 0))
    passed = jax.random.randint(jax.random.fold_in(own, 4), (amount // 2,), 0, 1 << 20) % (room + 1)
    sizes = sizes.at[source_of].add(-passed).at[taker].add(passed)
    labels = jnp.searchsorted(jnp.cumsum(sizes), jnp.arange(rows * top), side="right").astype(jnp.int32)
    grid = labels.reshape(top, rows).T
    grid = grid[jax.random.permutation(jax.random.fold_in(own, 1), rows)]
    rotation = jax.random.randint(jax.random.fold_in(own, 2), (rows, 1), 0, top)
    return jnp.take_along_axis(grid, (jnp.arange(top)[None, :] + rotation) % top, axis=1)


def shares(number_of, total, most, slope, full):
    loads = [(1 << 20) // math.isqrt(standing ** slope) + 1 for standing in range(1, number_of + 1)]
    largest = most if full else min(most, max(-(-total // number_of), total * loads[0] // sum(loads)))
    least = 1 if total - largest >= number_of - 1 else 0
    holding, spare = [largest] + [least] * (number_of - 1), total - largest - least * (number_of - 1)
    while spare > 0:
        free = [i for i in range(1, number_of) if holding[i] < largest] or [i for i in range(1, number_of) if holding[i] < most]
        whole, remaining = sum([loads[i] for i in free]), spare
        for i in free:
            more = min(most - holding[i], max(1, remaining * loads[i] // whole), spare)
            holding[i] = holding[i] + more
            spare = spare - more
    return np.array(holding)


def gaussian(stream_key, dims, deviation, bound, cuts=(), kind=jnp.bfloat16):
    loudness = block_scale(stream_key, dims, cuts, -0.22, 0.18) if cuts else 1.0
    values = jax.random.normal(stream_key, dims, jnp.float32) * deviation * loudness
    return jnp.minimum(jnp.maximum(values, -bound), bound).astype(kind)


def setup_inputs(seed: int = 0) -> dict:
    streams_of = jax.random.split(jax.random.key(seed), 8)
    tokens = gaussian(streams_of[0], (TOKENS, D), 1.0, 6.0, ((0, 256),))
    expert_ids_keys = jax.random.split(jax.random.fold_in(streams_of[1], 1), TOKENS // TOK_DEV)
    expert_ids_turns = jax.random.permutation(jax.random.fold_in(streams_of[1], 3), TOKENS // TOK_DEV)
    expert_ids = jax.vmap(lambda own, number: shared_out(jax.random.fold_in(streams_of[1], 2), own, number, TOK_DEV, EXPERTS, TOP, CAP, 2))(expert_ids_keys, expert_ids_turns).reshape((TOKENS, TOP))
    upstream = gaussian(streams_of[2], (TOKENS, D), 1.0, 6.0, ((0, 256),))
    router_weight = gaussian(streams_of[3], (D, EXPERTS), D ** -0.5, 0.1875)
    gate_matrix = gaussian(streams_of[4], (EXPERTS, FF, D), D ** -0.5, 0.1875, ((0, 16),))
    up_matrix = gaussian(streams_of[5], (EXPERTS, FF, D), D ** -0.5, 0.1875, ((0, 16),))
    down_matrix = gaussian(streams_of[6], (EXPERTS, FF, D), FF ** -0.5, 0.3125, ((0, 16),))
    return {"tokens": tokens, "expert_ids": expert_ids, "upstream": upstream, "router_weight": router_weight, "gate_matrix": gate_matrix, "up_matrix": up_matrix, "down_matrix": down_matrix}


def reference(tokens, expert_ids, upstream, router_weight, gate_matrix, up_matrix, down_matrix):
    devices = TOKENS // TOK_DEV
    per_dev = TOK_DEV * TOP
    id_blocks = expert_ids.reshape(devices, TOK_DEV, TOP)

    def slot_table(block, device_index):
        flat_ids = block.reshape(-1)
        onehot = (flat_ids[:, None] == jnp.arange(EXPERTS, dtype=jnp.int32)[None, :]).astype(jnp.int32)
        ranking = jnp.cumsum(onehot, axis=0) - 1
        slot_numbers = jnp.sum(ranking * onehot, axis=1)
        positions = flat_ids * CAP + slot_numbers
        ids_here = jnp.arange(per_dev, dtype=jnp.int32) + device_index * per_dev
        return jnp.full((EXPERTS * CAP,), -1, jnp.int32).at[positions].set(ids_here)

    tables = jax.vmap(slot_table)(id_blocks, jnp.arange(devices, dtype=jnp.int32))
    tables = tables.reshape(devices, EXPERTS, CAP).transpose(1, 0, 2).reshape(EXPERTS, devices * CAP)

    logits = jnp.dot(tokens, router_weight, preferred_element_type=jnp.float32)
    chosen = jnp.take_along_axis(logits, expert_ids, axis=1)
    raised = jnp.exp(chosen)
    gate_probs = raised / jnp.sum(raised, axis=1, keepdims=True)
    gate_flat = gate_probs.reshape(-1)
    cotangent = upstream.astype(jnp.float32)

    def per_expert(running, inputs_here):
        mix_acc, grad_acc, prob_acc = running
        sources, gate_here, up_here, down_here = inputs_here
        occupied = sources >= 0
        assign = jnp.maximum(sources, 0)
        token_index = assign // TOP
        picked = tokens[token_index]
        row_data = jnp.where(occupied[:, None], picked, jnp.zeros_like(picked))
        pre_gate = jnp.dot(row_data, gate_here.T, preferred_element_type=jnp.float32)
        pre_up = jnp.dot(row_data, up_here.T, preferred_element_type=jnp.float32)
        logistic = jax.nn.sigmoid(pre_gate)
        swished = pre_gate * logistic
        activated = (swished * pre_up).astype(jnp.bfloat16)
        produced = jnp.dot(activated, down_here, preferred_element_type=jnp.float32).astype(jnp.bfloat16)
        prob_here = jnp.where(occupied, gate_flat[assign], 0.0)
        cot_rows = cotangent[token_index]
        out_grad = (prob_here[:, None] * cot_rows).astype(jnp.bfloat16)
        prob_vals = jnp.sum(cot_rows * produced.astype(jnp.float32), axis=1)
        act_grad = jnp.dot(out_grad, down_here.T, preferred_element_type=jnp.float32)
        gate_back = (act_grad * pre_up * logistic * (1.0 + pre_gate * (1.0 - logistic))).astype(jnp.bfloat16)
        up_back = (act_grad * swished).astype(jnp.bfloat16)
        row_grad = (jnp.dot(gate_back, gate_here, preferred_element_type=jnp.float32)
                    + jnp.dot(up_back, up_here, preferred_element_type=jnp.float32)).astype(jnp.bfloat16)
        target = jnp.where(occupied, token_index, TOKENS)
        mix_acc = mix_acc.at[target].add(prob_here[:, None] * produced.astype(jnp.float32), mode="drop")
        grad_acc = grad_acc.at[target].add(row_grad.astype(jnp.float32), mode="drop")
        prob_acc = prob_acc.at[jnp.where(occupied, assign, TOKENS * TOP)].set(prob_vals, mode="drop")
        weight_terms = (jnp.dot(gate_back.T, row_data, preferred_element_type=jnp.float32),
                        jnp.dot(up_back.T, row_data, preferred_element_type=jnp.float32),
                        jnp.dot(activated.T, out_grad, preferred_element_type=jnp.float32))
        return (mix_acc, grad_acc, prob_acc), weight_terms

    zero_tok = jnp.zeros((TOKENS, D), jnp.float32)
    start_state = (zero_tok, zero_tok, jnp.zeros((TOKENS * TOP,), jnp.float32))
    (mix_acc, grad_acc, prob_acc), weight_terms = lax.scan(
        per_expert, start_state, (tables, gate_matrix, up_matrix, down_matrix))
    mixture = mix_acc.astype(jnp.bfloat16)
    prob_grad = prob_acc.reshape(TOKENS, TOP)
    centered = prob_grad - jnp.sum(gate_probs * prob_grad, axis=1, keepdims=True)
    chosen_grad = gate_probs * centered
    row_numbers = jnp.arange(TOKENS, dtype=jnp.int32)[:, None]
    logit_grad = jnp.zeros((TOKENS, EXPERTS), jnp.float32).at[row_numbers, expert_ids].add(chosen_grad)
    router_grad = jnp.dot(tokens.astype(jnp.float32).T, logit_grad, precision=lax.Precision.HIGHEST)
    router_input = jnp.dot(logit_grad, router_weight.astype(jnp.float32).T, precision=lax.Precision.HIGHEST)
    input_grad = (grad_acc + router_input).astype(jnp.bfloat16)
    return (mixture, input_grad, router_grad, weight_terms[0], weight_terms[1], weight_terms[2])
```

```python
import functools

import jax
import jax.numpy as jnp
from jax import lax
from jax.experimental import pallas as pl
from jax.experimental.pallas import tpu as pltpu
from jax.sharding import PartitionSpec as P

BF = jnp.bfloat16
F32 = jnp.float32
EXPERT = ("yl", "z")
DP = ("x", "yh", "core")
ALL = DP + EXPERT


def nt(a, b):
    return lax.dot_general(a, b, (((1,), (1,)), ((), ())), preferred_element_type=F32)


def tn(a, b):
    return lax.dot_general(a, b, (((0,), (0,)), ((), ())), preferred_element_type=F32)


def nn(a, b):
    return jnp.dot(a, b, preferred_element_type=F32)


def pack_kernel(tokens, ids, upstream, router, payload):
    rows = tokens.shape[0]
    experts = router.shape[0]
    payload[0:rows] = tokens[...]
    payload[rows : 2 * rows] = upstream[...]
    logits = nt(router[...], tokens[...])
    names = lax.broadcasted_iota(jnp.int32, (experts, rows), 0)
    chosen = names == ids[0:1, :]
    for k in range(1, ids.shape[0]):
        chosen = chosen | (names == ids[k : k + 1, :])
    raised = jnp.where(chosen, jnp.exp(logits), 0.0)
    probs = raised / jnp.sum(raised, axis=0, keepdims=True)
    wide = jnp.concatenate([probs[8 * b : 8 * b + 8, :] for b in range(experts // 8)], axis=1)
    high = wide.astype(BF).astype(F32)
    payload[2 * rows : 2 * rows + 16] = jnp.concatenate([high, wide - high], axis=0).astype(BF)


def expert_kernel(
    first,
    payload,
    gate,
    up,
    down,
    router,
    out,
    grads,
    router_part,
    x_rows,
    u_rows,
    picks,
    spreads,
    probs,
    local,
    weight,
    scores,
    produced,
    row_grads,
    down_kept,
    *,
    cap,
):
    e = pl.program_id(0)
    sources, _, width = payload.shape
    mine = local.shape[1]
    pairs, slots, pair_rows = picks.shape
    rows = pair_rows // 2
    experts = router.shape[0]
    two = 2 * cap
    at_first = first[0]

    def pair_of(p, start):
        return jnp.concatenate(
            [payload[2 * p, start : start + rows], payload[2 * p + 1, start : start + rows]], axis=0
        )

    @pl.when(e == 0)
    def _():
        t_from = lax.broadcasted_iota(jnp.int32, (rows, rows), 0)
        t_to = lax.broadcasted_iota(jnp.int32, (rows, rows), 1)
        before = jnp.where(t_from < t_to, 1.0, 0.0).astype(BF)
        names = lax.broadcasted_iota(jnp.int32, (experts, pair_rows), 0)
        slot_down = lax.broadcasted_iota(jnp.int32, (two, pair_rows), 0).astype(F32)
        slot_across = lax.broadcasted_iota(jnp.int32, (pair_rows, slots), 1).astype(F32)

        @pl.loop(0, pairs)
        def _(p):
            halves = []
            for h in range(2):
                ext = payload[2 * p + h, 2 * rows : 2 * rows + 16].astype(F32)
                wide = ext[0:8] + ext[8:16]
                halves.append(
                    jnp.concatenate(
                        [wide[:, rows * b : rows * b + rows] for b in range(experts // 8)], axis=0
                    )
                )
            all_probs = jnp.concatenate(halves, axis=1)
            probs[p] = all_probs
            own = [
                jnp.sum(jnp.where(names == at_first + j, all_probs, 0.0), axis=0, keepdims=True)
                for j in range(mine)
            ]
            own = jnp.concatenate(own + [jnp.zeros((8 - mine, pair_rows), F32)], axis=0)
            local[p] = own[0:mine]
            taken = jnp.where(own > 0.0, 1.0, 0.0)
            rank = jnp.concatenate(
                [
                    nn(taken[:, 0:rows].astype(BF), before),
                    nn(taken[:, rows:].astype(BF), before) + float(cap),
                ],
                axis=1,
            )
            slot = jnp.where(taken > 0.0, rank, -1000.0)
            parts = []
            for j in range(mine):
                hit = slot_down == slot[j : j + 1, :]
                parts.append(jnp.where(hit, 1.0, 0.0))
                weight[j, pl.ds(pl.multiple_of(p * two, two), two), :] = jnp.sum(
                    jnp.where(hit, own[j : j + 1, :], 0.0), axis=1, keepdims=True
                )
            pick = jnp.concatenate(parts, axis=0).astype(BF)
            picks[p] = pick
            slot_t = jnp.transpose(slot)
            spread = jnp.zeros((pair_rows, slots), F32)
            for j in range(mine):
                spread = jnp.where(
                    slot_across == slot_t[:, j : j + 1] + float(j * two),
                    jnp.where(slot_t[:, j : j + 1] >= 0.0, 1.0, 0.0), spread
                )
            spreads[p] = spread.astype(BF)
            here = pl.ds(pl.multiple_of(p * two, two), two)
            got = nn(pick, pair_of(p, 0)).astype(BF)
            for j in range(mine):
                x_rows[j, here, :] = got[j * two : j * two + two]
            got = nn(pick, pair_of(p, rows)).astype(BF)
            for j in range(mine):
                u_rows[j, here, :] = got[j * two : j * two + two]

    x = x_rows[e]
    u = u_rows[e]
    pre_gate = nt(x, gate[0])
    pre_up = nt(x, up[0])
    raw = nt(u, down[0])
    g = weight[e]
    logistic = jax.nn.sigmoid(pre_gate)
    swished = pre_gate * logistic
    activated = swished * pre_up
    scores[e] = jnp.sum(activated * raw, axis=1, keepdims=True)
    act_grad = raw * g
    scaled = (activated * g).astype(BF)
    gate_back = (act_grad * pre_up * logistic * (1.0 + pre_gate * (1.0 - logistic))).astype(BF)
    up_back = (act_grad * swished).astype(BF)
    at = pl.ds(pl.multiple_of(e * two, two), two)
    made = nn(scaled, down[0]).astype(BF)
    back = (nn(gate_back, gate[0]) + nn(up_back, up[0])).astype(BF)
    for p in range(pairs):
        produced[p, at, :] = made[p * two : p * two + two]
        row_grads[p, at, :] = back[p * two : p * two + two]
    chunks = grads.shape[0]
    gate_grad = tn(gate_back, x)
    up_grad = tn(up_back, x)
    piece = gate_grad.shape[0] // chunks
    for d in range(chunks):
        cut = slice(d * piece, d * piece + piece)
        grads[d, pl.ds(pl.multiple_of(e * 2 * piece, 2 * piece), 2 * piece), :] = jnp.concatenate(
            [gate_grad[cut], up_grad[cut]], axis=0
        ).astype(BF)
    down_grad = tn(scaled, u)

    @pl.when(e % 2 == 0)
    def _():
        down_kept[...] = down_grad

    @pl.when(e % 2 == 1)
    def _():
        base = mine * 2 * piece + (e // 2) * 2 * piece
        for d in range(chunks):
            cut = slice(d * piece, d * piece + piece)
            grads[d, pl.ds(pl.multiple_of(base, 2 * piece), 2 * piece), :] = jnp.concatenate(
                [down_kept[cut], down_grad[cut]], axis=0
            ).astype(BF)

    @pl.when(e == mine - 1)
    def _():
        names = lax.broadcasted_iota(jnp.int32, (experts, pair_rows), 0)
        router_part[...] = jnp.zeros_like(router_part)

        @pl.loop(0, pairs)
        def _(p):
            spread = spreads[p]
            mix = nn(spread, produced[p]).astype(BF)
            out[2 * p, 0:rows] = mix[0:rows]
            out[2 * p + 1, 0:rows] = mix[rows:]
            pick = picks[p].astype(F32)
            own = local[p]
            total = jnp.zeros((1, pair_rows), F32)
            placed = jnp.zeros((experts, pair_rows), F32)
            for j in range(mine):
                score = scores[j, pl.ds(pl.multiple_of(p * two, two), two), :]
                grad = own[j : j + 1] * jnp.sum(
                    pick[j * two : j * two + two] * score, axis=0, keepdims=True
                )
                total = total + grad
                placed = jnp.where(names == at_first + j, grad, placed)
            logit_grad = placed - probs[p] * total
            high = logit_grad.astype(BF)
            low = (logit_grad - high.astype(F32)).astype(BF)
            both = nn(jnp.concatenate([high, low], axis=0), pair_of(p, 0))
            router_part[...] += both[0:experts] + both[experts:]
            back = (nn(spread, row_grads[p]) + tn(high, router[...])).astype(BF)
            out[2 * p, rows : 2 * rows] = back[0:rows]
            out[2 * p + 1, rows : 2 * rows] = back[rows:]


def run_experts(first, payload, gate, up, down, router, cap, chunks):
    sources, payload_rows, width = payload.shape
    mine, hidden, _ = gate.shape
    experts = router.shape[0]
    rows = (payload_rows - 16) // 2
    pairs, slots, total = sources // 2, 2 * mine * cap, sources * cap
    whole = functools.partial(pl.BlockSpec, pipeline_mode=pl.Buffered(1))
    one = lambda: pl.BlockSpec((1, hidden, width), lambda e: (e, 0, 0))
    grad_rows = 3 * mine * hidden // chunks
    return pl.pallas_call(
        functools.partial(expert_kernel, cap=cap),
        grid=(mine,),
        out_shape=(
            jax.ShapeDtypeStruct((sources, 2 * rows, width), BF),
            jax.ShapeDtypeStruct((chunks, grad_rows, width), BF),
            jax.ShapeDtypeStruct((experts, width), F32),
        ),
        in_specs=[
            pl.BlockSpec(memory_space=pltpu.SMEM),
            whole((sources, payload_rows, width), lambda e: (0, 0, 0)),
            one(),
            one(),
            one(),
            whole((experts, width), lambda e: (0, 0)),
        ],
        out_specs=(
            whole((sources, 2 * rows, width), lambda e: (0, 0, 0)),
            whole((chunks, grad_rows, width), lambda e: (0, 0, 0)),
            whole((experts, width), lambda e: (0, 0)),
        ),
        scratch_shapes=[
            pltpu.VMEM((mine, total, width), BF),
            pltpu.VMEM((mine, total, width), BF),
            pltpu.VMEM((pairs, slots, 2 * rows), BF),
            pltpu.VMEM((pairs, 2 * rows, slots), BF),
            pltpu.VMEM((pairs, experts, 2 * rows), F32),
            pltpu.VMEM((pairs, mine, 2 * rows), F32),
            pltpu.VMEM((mine, total, 1), F32),
            pltpu.VMEM((mine, total, 1), F32),
            pltpu.VMEM((pairs, slots, width), BF),
            pltpu.VMEM((pairs, slots, width), BF),
            pltpu.VMEM((hidden, width), F32),
        ],
        compiler_params=pltpu.CompilerParams(vmem_limit_bytes=60 * 2**20),
        cost_estimate=pl.CostEstimate(
            flops=16 * 10**9, bytes_accessed=32 * 2**20, transcendentals=10**6
        ),
    )(first, payload, gate, up, down, router)


def body(tokens, expert_ids, upstream, router_weight, gate_matrix, up_matrix, down_matrix):
    rows, width = tokens.shape
    top = expert_ids.shape[1]
    mine, hidden, _ = gate_matrix.shape
    peers = lax.axis_size(EXPERT)
    groups = lax.axis_size(DP)
    experts = peers * mine
    cap = rows * top * 3 // (2 * experts)
    router = router_weight.T
    payload = pl.pallas_call(
        pack_kernel,
        out_shape=jax.ShapeDtypeStruct((2 * rows + 16, width), BF),
    )(tokens, expert_ids.T, upstream, router)
    gathered = lax.all_gather(payload, EXPERT, axis=0, tiled=False)
    first = (lax.axis_index(EXPERT) * mine).reshape(1).astype(jnp.int32)
    out, grads, router_part = run_experts(
        first, gathered, gate_matrix, up_matrix, down_matrix, router, cap, groups
    )
    router_grad = lax.psum(router_part, ALL).T
    grads = lax.psum_scatter(grads, DP, scatter_dimension=0, tiled=False)
    out = lax.psum_scatter(out, EXPERT, scatter_dimension=0, tiled=False)
    piece = hidden // groups
    both = grads[0 : 2 * mine * piece].astype(F32).reshape(mine, 2, piece, width)
    down_grad = grads[2 * mine * piece :].astype(F32).reshape(mine, piece, width)
    return out[0:rows], out[rows:], router_grad, both[:, 0], both[:, 1], down_grad


def solution(mesh):
    shape = {"x": 4, "yh": 2, "core": 2, "yl": 2, "z": 8}
    fine = jax.sharding.Mesh(mesh.devices.reshape(tuple(shape.values())), tuple(shape))
    in_specs = (
        P(ALL, None),
        P(ALL, None),
        P(ALL, None),
        P(),
        P(EXPERT, None, None),
        P(EXPERT, None, None),
        P(EXPERT, None, None),
    )
    out_specs = (
        P(ALL, None),
        P(ALL, None),
        P(),
        P(EXPERT, DP, None),
        P(EXPERT, DP, None),
        P(EXPERT, DP, None),
    )
    return jax.shard_map(body, mesh=fine, in_specs=in_specs, out_specs=out_specs, check_vma=False)
```

```python
import functools

import jax
import jax.numpy as jnp
from jax import lax
from jax.experimental import pallas as pl
from jax.experimental.pallas import tpu as pltpu
from jax.sharding import PartitionSpec as P

BF = jnp.bfloat16
F32 = jnp.float32
EXPERT = ("yl", "z")
DP = ("x", "yh", "core")
ALL = DP + EXPERT


def nt(a, b):
    return lax.dot_general(a, b, (((1,), (1,)), ((), ())), preferred_element_type=F32)


def tn(a, b):
    return lax.dot_general(a, b, (((0,), (0,)), ((), ())), preferred_element_type=F32)


def nn(a, b):
    return jnp.dot(a, b, preferred_element_type=F32)


def pack_kernel(tokens, ids, upstream, router, payload):
    rows = tokens.shape[0]
    experts = router.shape[0]
    payload[0:rows] = tokens[...]
    payload[rows : 2 * rows] = upstream[...]
    logits = nt(router[...], tokens[...])
    names = lax.broadcasted_iota(jnp.int32, (experts, rows), 0)
    chosen = names == ids[0:1, :]
    for k in range(1, ids.shape[0]):
        chosen = chosen | (names == ids[k : k + 1, :])
    raised = jnp.where(chosen, jnp.exp(logits), 0.0)
    probs = raised / jnp.sum(raised, axis=0, keepdims=True)
    wide = jnp.concatenate([probs[8 * b : 8 * b + 8, :] for b in range(experts // 8)], axis=1)
    high = wide.astype(BF).astype(F32)
    payload[2 * rows : 2 * rows + 16] = jnp.concatenate([high, wide - high], axis=0).astype(BF)


def expert_kernel(
    first,
    payload,
    gate,
    up,
    down,
    router,
    out,
    grads,
    router_part,
    x_rows,
    u_rows,
    picks,
    spreads,
    probs,
    local,
    weight,
    scores,
    produced,
    row_grads,
    down_kept,
    *,
    cap,
):
    e = pl.program_id(0)
    sources, _, width = payload.shape
    mine = local.shape[1]
    pairs, slots, pair_rows = picks.shape
    rows = pair_rows // 2
    experts = router.shape[0]
    two = 2 * cap
    at_first = first[0]

    def pair_of(p, start):
        return jnp.concatenate(
            [payload[2 * p, start : start + rows], payload[2 * p + 1, start : start + rows]], axis=0
        )

    @pl.when(e == 0)
    def _():
        t_from = lax.broadcasted_iota(jnp.int32, (rows, rows), 0)
        t_to = lax.broadcasted_iota(jnp.int32, (rows, rows), 1)
        before = jnp.where(t_from < t_to, 1.0, 0.0).astype(BF)
        names = lax.broadcasted_iota(jnp.int32, (experts, pair_rows), 0)
        slot_down = lax.broadcasted_iota(jnp.int32, (two, pair_rows), 0).astype(F32)
        slot_across = lax.broadcasted_iota(jnp.int32, (pair_rows, slots), 1).astype(F32)

        @pl.loop(0, pairs)
        def _(p):
            halves = []
            for h in range(2):
                ext = payload[2 * p + h, 2 * rows : 2 * rows + 16].astype(F32)
                wide = ext[0:8] + ext[8:16]
                halves.append(
                    jnp.concatenate(
                        [wide[:, rows * b : rows * b + rows] for b in range(experts // 8)], axis=0
                    )
                )
            all_probs = jnp.concatenate(halves, axis=1)
            probs[p] = all_probs
            own = [
                jnp.sum(jnp.where(names == at_first + j, all_probs, 0.0), axis=0, keepdims=True)
                for j in range(mine)
            ]
            own = jnp.concatenate(own + [jnp.zeros((8 - mine, pair_rows), F32)], axis=0)
            local[p] = own[0:mine]
            taken = jnp.where(own > 0.0, 1.0, 0.0)
            rank = jnp.concatenate(
                [
                    nn(taken[:, 0:rows].astype(BF), before),
                    nn(taken[:, rows:].astype(BF), before) + float(cap),
                ],
                axis=1,
            )
            slot = jnp.where(taken > 0.0, rank, -1000.0)
            parts = []
            for j in range(mine):
                hit = slot_down == slot[j : j + 1, :]
                parts.append(jnp.where(hit, 1.0, 0.0))
                weight[j, pl.ds(pl.multiple_of(p * two, two), two), :] = jnp.sum(
                    jnp.where(hit, own[j : j + 1, :], 0.0), axis=1, keepdims=True
                )
            pick = jnp.concatenate(parts, axis=0).astype(BF)
            picks[p] = pick
            slot_t = jnp.transpose(slot)
            spread = jnp.zeros((pair_rows, slots), F32)
            for j in range(mine):
                spread = jnp.where(
                    slot_across == slot_t[:, j : j + 1] + float(j * two),
                    jnp.where(slot_t[:, j : j + 1] >= 0.0, 1.0, 0.0), spread
                )
            spreads[p] = spread.astype(BF)
            here = pl.ds(pl.multiple_of(p * two, two), two)
            got = nn(pick, pair_of(p, 0)).astype(BF)
            for j in range(mine):
                x_rows[j, here, :] = got[j * two : j * two + two]
            got = nn(pick, pair_of(p, rows)).astype(BF)
            for j in range(mine):
                u_rows[j, here, :] = got[j * two : j * two + two]

    x = x_rows[e]
    u = u_rows[e]
    pre_gate = nt(x, gate[0])
    pre_up = nt(x, up[0])
    raw = nt(u, down[0])
    g = weight[e]
    logistic = jax.nn.sigmoid(pre_gate)
    swished = pre_gate * logistic
    activated = swished * pre_up
    scores[e] = jnp.sum(activated * raw, axis=1, keepdims=True)
    act_grad = raw * g
    scaled = (activated * g).astype(BF)
    gate_back = (act_grad * pre_up * logistic * (1.0 + pre_gate * (1.0 - logistic))).astype(BF)
    up_back = (act_grad * swished).astype(BF)
    at = pl.ds(pl.multiple_of(e * two, two), two)
    made = nn(scaled, down[0]).astype(BF)
    back = (nn(gate_back, gate[0]) + nn(up_back, up[0])).astype(BF)
    for p in range(pairs):
        produced[p, at, :] = made[p * two : p * two + two]
        row_grads[p, at, :] = back[p * two : p * two + two]
    chunks = grads.shape[0]
    gate_grad = tn(gate_back, x)
    up_grad = tn(up_back, x)
    piece = gate_grad.shape[0] // chunks
    for d in range(chunks):
        cut = slice(d * piece, d * piece + piece)
        grads[(d % 2) * (chunks // 2) + d // 2, pl.ds(pl.multiple_of(e * 2 * piece, 2 * piece), 2 * piece), :] = jnp.concatenate(
            [gate_grad[cut], up_grad[cut]], axis=0
        ).astype(BF)
    down_grad = tn(scaled, u)

    @pl.when(e % 2 == 0)
    def _():
        down_kept[...] = down_grad

    @pl.when(e % 2 == 1)
    def _():
        base = mine * 2 * piece + (e // 2) * 2 * piece
        for d in range(chunks):
            cut = slice(d * piece, d * piece + piece)
            grads[(d % 2) * (chunks // 2) + d // 2, pl.ds(pl.multiple_of(base, 2 * piece), 2 * piece), :] = jnp.concatenate(
                [down_kept[cut], down_grad[cut]], axis=0
            ).astype(BF)

    @pl.when(e == mine - 1)
    def _():
        names = lax.broadcasted_iota(jnp.int32, (experts, pair_rows), 0)
        router_part[...] = jnp.zeros_like(router_part)

        @pl.loop(0, pairs)
        def _(p):
            spread = spreads[p]
            mix = nn(spread, produced[p]).astype(BF)
            out[2 * p, 0:rows] = mix[0:rows]
            out[2 * p + 1, 0:rows] = mix[rows:]
            pick = picks[p].astype(F32)
            own = local[p]
            total = jnp.zeros((1, pair_rows), F32)
            placed = jnp.zeros((experts, pair_rows), F32)
            for j in range(mine):
                score = scores[j, pl.ds(pl.multiple_of(p * two, two), two), :]
                grad = own[j : j + 1] * jnp.sum(
                    pick[j * two : j * two + two] * score, axis=0, keepdims=True
                )
                total = total + grad
                placed = jnp.where(names == at_first + j, grad, placed)
            logit_grad = placed - probs[p] * total
            high = logit_grad.astype(BF)
            low = (logit_grad - high.astype(F32)).astype(BF)
            both = nn(jnp.concatenate([high, low], axis=0), pair_of(p, 0))
            router_part[...] += both[0:experts] + both[experts:]
            back = (nn(spread, row_grads[p]) + tn(high, router[...])).astype(BF)
            out[2 * p, rows : 2 * rows] = back[0:rows]
            out[2 * p + 1, rows : 2 * rows] = back[rows:]

        half = width // 2
        end = grads.shape[1] - 16
        for d in range(chunks):
            part = router_part[8 * (d // 2) : 8 * (d // 2) + 8, half * (d % 2) : half * (d % 2 + 1)]
            high = part.astype(BF).astype(F32)
            split = jnp.concatenate([high, part - high], axis=1)
            grads[(d % 2) * (chunks // 2) + d // 2, end : end + 16] = jnp.concatenate(
                [split, jnp.zeros_like(split)], axis=0
            ).astype(BF)


def run_experts(first, payload, gate, up, down, router, cap, chunks):
    sources, payload_rows, width = payload.shape
    mine, hidden, _ = gate.shape
    experts = router.shape[0]
    rows = (payload_rows - 16) // 2
    pairs, slots, total = sources // 2, 2 * mine * cap, sources * cap
    whole = functools.partial(pl.BlockSpec, pipeline_mode=pl.Buffered(1))
    one = lambda: pl.BlockSpec((1, hidden, width), lambda e: (e, 0, 0))
    grad_rows = 3 * mine * hidden // chunks + 16
    return pl.pallas_call(
        functools.partial(expert_kernel, cap=cap),
        grid=(mine,),
        out_shape=(
            jax.ShapeDtypeStruct((sources, 2 * rows, width), BF),
            jax.ShapeDtypeStruct((chunks, grad_rows, width), BF),
        ),
        in_specs=[
            pl.BlockSpec(memory_space=pltpu.SMEM),
            whole((sources, payload_rows, width), lambda e: (0, 0, 0)),
            one(),
            one(),
            one(),
            whole((experts, width), lambda e: (0, 0)),
        ],
        out_specs=(
            whole((sources, 2 * rows, width), lambda e: (0, 0, 0)),
            whole((chunks, grad_rows, width), lambda e: (0, 0, 0)),
        ),
        scratch_shapes=[
            pltpu.VMEM((experts, width), F32),
            pltpu.VMEM((mine, total, width), BF),
            pltpu.VMEM((mine, total, width), BF),
            pltpu.VMEM((pairs, slots, 2 * rows), BF),
            pltpu.VMEM((pairs, 2 * rows, slots), BF),
            pltpu.VMEM((pairs, experts, 2 * rows), F32),
            pltpu.VMEM((pairs, mine, 2 * rows), F32),
            pltpu.VMEM((mine, total, 1), F32),
            pltpu.VMEM((mine, total, 1), F32),
            pltpu.VMEM((pairs, slots, width), BF),
            pltpu.VMEM((pairs, slots, width), BF),
            pltpu.VMEM((hidden, width), F32),
        ],
        compiler_params=pltpu.CompilerParams(vmem_limit_bytes=60 * 2**20),
        cost_estimate=pl.CostEstimate(
            flops=16 * 10**9, bytes_accessed=32 * 2**20, transcendentals=10**6
        ),
    )(first, payload, gate, up, down, router)


def swap(value, axis, step):
    size = lax.axis_size(axis)
    return lax.ppermute(value, axis, [(i, i ^ step) for i in range(size)])


def joined(value):
    half = value.shape[-1] // 2
    return value[..., 0:half].astype(F32) + value[..., half:].astype(F32)


def body(tokens, expert_ids, upstream, router_weight, gate_matrix, up_matrix, down_matrix):
    rows, width = tokens.shape
    top = expert_ids.shape[1]
    mine, hidden, _ = gate_matrix.shape
    peers = lax.axis_size(EXPERT)
    groups = lax.axis_size(DP)
    experts = peers * mine
    cap = rows * top * 3 // (2 * experts)
    router = router_weight.T
    payload = pl.pallas_call(
        pack_kernel,
        out_shape=jax.ShapeDtypeStruct((2 * rows + 16, width), BF),
    )(tokens, expert_ids.T, upstream, router)
    gathered = lax.all_gather(payload, EXPERT, axis=0, tiled=False)
    first = (lax.axis_index(EXPERT) * mine).reshape(1).astype(jnp.int32)
    out, grads = run_experts(
        first, gathered, gate_matrix, up_matrix, down_matrix, router, cap, groups
    )
    out = lax.psum_scatter(out, EXPERT, scatter_dimension=0, tiled=False)
    piece = hidden // groups
    end = 3 * mine * piece
    core = lax.axis_index("core")
    both = grads.reshape(2, groups // 2, end + 16, width)
    theirs = swap(lax.dynamic_index_in_dim(both, 1 - core, 0, keepdims=False), "core", 1)
    ours = lax.dynamic_index_in_dim(both, core, 0, keepdims=False)
    sums = (ours[:, 0:end].astype(F32) + theirs[:, 0:end].astype(F32)).astype(BF)
    part = joined(ours[:, end : end + 8]) + joined(theirs[:, end : end + 8])
    high = lax.reduce_precision(part, 8, 7)
    split = jnp.concatenate([high, part - high], axis=2).astype(BF)
    send = jnp.concatenate([sums, split, jnp.zeros_like(split)], axis=1)
    got = lax.all_to_all(send, ("x", "yh"), split_axis=0, concat_axis=0, tiled=True)
    total = jnp.sum(got[:, 0:end].astype(F32), axis=0)
    both = total[0 : 2 * mine * piece].reshape(mine, 2, piece, width)
    down_grad = total[2 * mine * piece :].reshape(mine, piece, width)
    part = jnp.sum(joined(got[:, end : end + 8]), axis=0)
    for axis, step in (("yl", 1), ("z", 1), ("z", 2), ("z", 4)):
        part = part + swap(part, axis, step)
    parts = lax.all_gather(part, DP, axis=0, tiled=False)
    parts = parts.reshape(groups // 2, 2, 8, width // 2).transpose(0, 2, 1, 3)
    router_grad = parts.reshape(experts, width).T
    return out[0:rows], out[rows:], router_grad, both[:, 0], both[:, 1], down_grad


def solution(mesh):
    shape = {"x": 4, "yh": 2, "core": 2, "yl": 2, "z": 8}
    fine = jax.sharding.Mesh(mesh.devices.reshape(tuple(shape.values())), tuple(shape))
    in_specs = (
        P(ALL, None),
        P(ALL, None),
        P(ALL, None),
        P(),
        P(EXPERT, None, None),
        P(EXPERT, None, None),
        P(EXPERT, None, None),
    )
    out_specs = (
        P(ALL, None),
        P(ALL, None),
        P(),
        P(EXPERT, DP, None),
        P(EXPERT, DP, None),
        P(EXPERT, DP, None),
    )
    return jax.shard_map(body, mesh=fine, in_specs=in_specs, out_specs=out_specs, check_vma=False)
```

```python
import functools

import jax
import jax.numpy as jnp
from jax import lax
from jax.experimental import pallas as pl
from jax.experimental.pallas import tpu as pltpu
from jax.sharding import PartitionSpec as P

BF = jnp.bfloat16
F32 = jnp.float32
EXPERT = ("yl", "z")
DP = ("x", "yh", "core")
ALL = DP + EXPERT


def nt(a, b):
    return lax.dot_general(a, b, (((1,), (1,)), ((), ())), preferred_element_type=F32)


def tn(a, b):
    return lax.dot_general(a, b, (((0,), (0,)), ((), ())), preferred_element_type=F32)


def nn(a, b):
    return jnp.dot(a, b, preferred_element_type=F32)


def pack_kernel(tokens, ids, upstream, router, packed):
    rows = tokens.shape[0]
    experts = router.shape[0]
    packed[0:rows] = upstream[...]
    logits = nt(router[...], tokens[...])
    names = lax.broadcasted_iota(jnp.int32, (experts, rows), 0)
    chosen = names == ids[0:1, :]
    for k in range(1, ids.shape[0]):
        chosen = chosen | (names == ids[k : k + 1, :])
    raised = jnp.where(chosen, jnp.exp(logits), 0.0)
    probs = raised / jnp.sum(raised, axis=0, keepdims=True)
    wide = jnp.concatenate([probs[8 * b : 8 * b + 8, :] for b in range(experts // 8)], axis=1)
    high = wide.astype(BF).astype(F32)
    packed[rows : rows + 16] = jnp.concatenate([high, wide - high], axis=0).astype(BF)


def expert_kernel(*refs, cap, counts):
    place = refs[0]
    token_refs = refs[1 : 1 + counts[0]]
    packed_refs = refs[1 + counts[0] : 1 + sum(counts)]
    gate, up, down, router, out, ours, theirs, router_part = refs[1 + sum(counts) : 9 + sum(counts)]
    (
        xs,
        us,
        grads,
        x_rows,
        u_rows,
        picks,
        spreads,
        probs,
        local,
        weight,
        scores,
        produced,
        row_grads,
        down_kept,
        sems,
        end_sems,
    ) = refs[9 + sum(counts) :]
    e = pl.program_id(0)
    width = xs.shape[2]
    mine = local.shape[1]
    pairs, slots, pair_rows = picks.shape
    rows = pair_rows // 2
    experts = router.shape[0]
    two = 2 * cap
    px, py, pc, pl_, pz = [place[i] for i in range(5)]
    at_first = (pl_ * pairs + pz) * mine

    def pair_of(p, start):
        if start == 0:
            return xs[p]
        return jnp.concatenate([us[p, 0, 0:rows], us[p, 1, 0:rows]], axis=0)

    def slot_of(d):
        x_off = lax.rem(d // 4 + 4 - px, 4)
        y_off = jnp.where(py == d // 2 % 2, 0, 1)
        return jnp.where(pc == d % 2, 0, 1), x_off * 2 + y_off

    @pl.when(e == 0)
    def _():
        copies = []
        for i in range(counts[0]):
            to = xs.at[i % pairs, pl.ds(i // pairs * rows, rows)]
            copies.append(pltpu.make_async_copy(token_refs[i], to, sems.at[len(copies)]))
        for i in range(counts[1]):
            to = us.at[i] if i < pairs // 2 else us.at[i + 1]
            if i >= pairs - 1:
                to = us.at[pairs // 2, i - (pairs - 1)]
            copies.append(pltpu.make_async_copy(packed_refs[i], to, sems.at[len(copies)]))
        for copy in copies:
            copy.start()
        for copy in copies:
            copy.wait()

    @pl.when(e == 0)
    def _():
        t_from = lax.broadcasted_iota(jnp.int32, (rows, rows), 0)
        t_to = lax.broadcasted_iota(jnp.int32, (rows, rows), 1)
        before = jnp.where(t_from < t_to, 1.0, 0.0).astype(BF)
        names = lax.broadcasted_iota(jnp.int32, (experts, pair_rows), 0)
        slot_down = lax.broadcasted_iota(jnp.int32, (two, pair_rows), 0).astype(F32)
        slot_across = lax.broadcasted_iota(jnp.int32, (pair_rows, slots), 1).astype(F32)

        @pl.loop(0, pairs)
        def _(p):
            halves = []
            for h in range(2):
                ext = us[p, h, rows : rows + 16].astype(F32)
                wide = ext[0:8] + ext[8:16]
                halves.append(
                    jnp.concatenate(
                        [wide[:, rows * b : rows * b + rows] for b in range(experts // 8)], axis=0
                    )
                )
            all_probs = jnp.concatenate(halves, axis=1)
            probs[p] = all_probs
            own = [
                jnp.sum(jnp.where(names == at_first + j, all_probs, 0.0), axis=0, keepdims=True)
                for j in range(mine)
            ]
            own = jnp.concatenate(own + [jnp.zeros((8 - mine, pair_rows), F32)], axis=0)
            local[p] = own[0:mine]
            taken = jnp.where(own > 0.0, 1.0, 0.0)
            rank = jnp.concatenate(
                [
                    nn(taken[:, 0:rows].astype(BF), before),
                    nn(taken[:, rows:].astype(BF), before) + float(cap),
                ],
                axis=1,
            )
            slot = jnp.where(taken > 0.0, rank, -1000.0)
            parts = []
            for j in range(mine):
                hit = slot_down == slot[j : j + 1, :]
                parts.append(jnp.where(hit, 1.0, 0.0))
                weight[j, pl.ds(pl.multiple_of(p * two, two), two), :] = jnp.sum(
                    jnp.where(hit, own[j : j + 1, :], 0.0), axis=1, keepdims=True
                )
            pick = jnp.concatenate(parts, axis=0).astype(BF)
            picks[p] = pick
            slot_t = jnp.transpose(slot)
            spread = jnp.zeros((pair_rows, slots), F32)
            for j in range(mine):
                spread = jnp.where(
                    slot_across == slot_t[:, j : j + 1] + float(j * two),
                    jnp.where(slot_t[:, j : j + 1] >= 0.0, 1.0, 0.0), spread
                )
            spreads[p] = spread.astype(BF)
            here = pl.ds(pl.multiple_of(p * two, two), two)
            got = nn(pick, pair_of(p, 0)).astype(BF)
            for j in range(mine):
                x_rows[j, here, :] = got[j * two : j * two + two]
            got = nn(pick, pair_of(p, rows)).astype(BF)
            for j in range(mine):
                u_rows[j, here, :] = got[j * two : j * two + two]

    x = x_rows[e]
    u = u_rows[e]
    pre_gate = nt(x, gate[0])
    pre_up = nt(x, up[0])
    raw = nt(u, down[0])
    g = weight[e]
    logistic = jax.nn.sigmoid(pre_gate)
    swished = pre_gate * logistic
    activated = swished * pre_up
    scores[e] = jnp.sum(activated * raw, axis=1, keepdims=True)
    act_grad = raw * g
    scaled = (activated * g).astype(BF)
    gate_back = (act_grad * pre_up * logistic * (1.0 + pre_gate * (1.0 - logistic))).astype(BF)
    up_back = (act_grad * swished).astype(BF)
    at = pl.ds(pl.multiple_of(e * two, two), two)
    made = nn(scaled, down[0]).astype(BF)
    back = (nn(gate_back, gate[0]) + nn(up_back, up[0])).astype(BF)
    for p in range(pairs):
        produced[p, at, :] = made[p * two : p * two + two]
        row_grads[p, at, :] = back[p * two : p * two + two]
    chunks = 2 * grads.shape[1]
    gate_grad = tn(gate_back, x)
    up_grad = tn(up_back, x)
    piece = gate_grad.shape[0] // chunks
    for d in range(chunks):
        cut = slice(d * piece, d * piece + piece)
        grads[*slot_of(d), pl.ds(pl.multiple_of(e * 2 * piece, 2 * piece), 2 * piece), :] = jnp.concatenate(
            [gate_grad[cut], up_grad[cut]], axis=0
        ).astype(BF)
    down_grad = tn(scaled, u)

    @pl.when(e % 2 == 0)
    def _():
        down_kept[...] = down_grad

    @pl.when(e % 2 == 1)
    def _():
        base = mine * 2 * piece + (e // 2) * 2 * piece
        for d in range(chunks):
            cut = slice(d * piece, d * piece + piece)
            grads[*slot_of(d), pl.ds(pl.multiple_of(base, 2 * piece), 2 * piece), :] = jnp.concatenate(
                [down_kept[cut], down_grad[cut]], axis=0
            ).astype(BF)

    @pl.when(e == mine - 1)
    def _():
        names = lax.broadcasted_iota(jnp.int32, (experts, pair_rows), 0)
        router_part[...] = jnp.zeros_like(router_part)

        @pl.loop(0, pairs)
        def _(p):
            spread = spreads[p]
            mix = nn(spread, produced[p]).astype(BF)
            to = lax.rem(pz + p, pairs)
            to = (pl_ * pairs + to, (1 - pl_) * pairs + to)
            for h in range(2):
                out[to[h], 0:rows] = mix[h * rows : h * rows + rows]
            pick = picks[p].astype(F32)
            own = local[p]
            total = jnp.zeros((1, pair_rows), F32)
            placed = jnp.zeros((experts, pair_rows), F32)
            for j in range(mine):
                score = scores[j, pl.ds(pl.multiple_of(p * two, two), two), :]
                grad = own[j : j + 1] * jnp.sum(
                    pick[j * two : j * two + two] * score, axis=0, keepdims=True
                )
                total = total + grad
                placed = jnp.where(names == at_first + j, grad, placed)
            logit_grad = placed - probs[p] * total
            high = logit_grad.astype(BF)
            low = (logit_grad - high.astype(F32)).astype(BF)
            both = nn(jnp.concatenate([high, low], axis=0), pair_of(p, 0))
            router_part[...] += both[0:experts] + both[experts:]
            back = (nn(spread, row_grads[p]) + tn(high, router[...])).astype(BF)
            for h in range(2):
                out[to[h], rows : 2 * rows] = back[h * rows : h * rows + rows]

        finals = (
            pltpu.make_async_copy(grads.at[0], ours, end_sems.at[0]),
            pltpu.make_async_copy(grads.at[1], theirs, end_sems.at[1]),
        )
        for copy in finals:
            copy.start()
        for copy in finals:
            copy.wait()


def run_experts(place, token_blocks, packed_blocks, gate, up, down, router, cap, chunks):
    rows, width = token_blocks[0].shape
    mine, hidden, _ = gate.shape
    experts = router.shape[0]
    sources = len(token_blocks)
    pairs, slots, total = sources // 2, 2 * mine * cap, sources * cap
    whole = functools.partial(pl.BlockSpec, pipeline_mode=pl.Buffered(1))
    one = lambda: pl.BlockSpec((1, hidden, width), lambda e: (e, 0, 0))
    anywhere = pl.BlockSpec(memory_space=pl.ANY)
    grad_rows = 3 * mine * hidden // chunks
    counts = (sources, len(packed_blocks))
    return pl.pallas_call(
        functools.partial(expert_kernel, cap=cap, counts=counts),
        grid=(mine,),
        out_shape=(
            jax.ShapeDtypeStruct((sources, 2 * rows, width), BF),
            jax.ShapeDtypeStruct((chunks // 2, grad_rows, width), BF),
            jax.ShapeDtypeStruct((chunks // 2, grad_rows, width), BF),
            jax.ShapeDtypeStruct((experts, width), F32),
        ),
        in_specs=[
            pl.BlockSpec(memory_space=pltpu.SMEM),
            *([anywhere] * sum(counts)),
            one(),
            one(),
            one(),
            whole((experts, width), lambda e: (0, 0)),
        ],
        out_specs=(
            whole((sources, 2 * rows, width), lambda e: (0, 0, 0)),
            anywhere,
            anywhere,
            whole((experts, width), lambda e: (0, 0)),
        ),
        scratch_shapes=[
            pltpu.VMEM((pairs, 2 * rows, width), BF),
            pltpu.VMEM((pairs, 2, rows + 16, width), BF),
            pltpu.VMEM((2, chunks // 2, grad_rows, width), BF),
            pltpu.VMEM((mine, total, width), BF),
            pltpu.VMEM((mine, total, width), BF),
            pltpu.VMEM((pairs, slots, 2 * rows), BF),
            pltpu.VMEM((pairs, 2 * rows, slots), BF),
            pltpu.VMEM((pairs, experts, 2 * rows), F32),
            pltpu.VMEM((pairs, mine, 2 * rows), F32),
            pltpu.VMEM((mine, total, 1), F32),
            pltpu.VMEM((mine, total, 1), F32),
            pltpu.VMEM((pairs, slots, width), BF),
            pltpu.VMEM((pairs, slots, width), BF),
            pltpu.VMEM((hidden, width), F32),
            pltpu.SemaphoreType.DMA((sum(counts),)),
            pltpu.SemaphoreType.DMA((2,)),
        ],
        compiler_params=pltpu.CompilerParams(vmem_limit_bytes=60 * 2**20),
        cost_estimate=pl.CostEstimate(
            flops=16 * 10**9, bytes_accessed=32 * 2**20, transcendentals=10**6
        ),
    )(place, *token_blocks, *packed_blocks, gate, up, down, router)


def swap(value, axis, step):
    size = lax.axis_size(axis)
    return lax.ppermute(value, axis, [(i, i ^ step) for i in range(size)])


def shift(value, axis, step):
    size = lax.axis_size(axis)
    return lax.ppermute(value, axis, [(i, (i + step) % size) for i in range(size)])


def gather_tokens(block):
    half = block.shape[0] // 2
    right = left = block
    found = {0: block}
    for k in range(1, 4):
        right, left = shift(right, "z", 1), shift(left, "z", -1)
        found[8 - k], found[k] = right, left
    found[4] = jnp.concatenate([shift(right[:half], "z", 1), shift(left[half:], "z", -1)], axis=0)
    return [found[i] for i in range(8)] + [swap(found[i], "yl", 1) for i in range(8)]


def gather_packed(block):
    both = jnp.stack([block, swap(block, "yl", 1)])
    right = left = both
    found = {0: both}
    for k in range(1, 4):
        right, left = shift(right, "z", 1), shift(left, "z", -1)
        found[8 - k], found[k] = right, left
    far = [shift(right[0], "z", 1), shift(left[1], "z", -1)]
    return [found[i] for i in (0, 1, 2, 3, 5, 6, 7)] + far


def added(*terms):
    total = terms[0].astype(F32)
    for term in terms[1:]:
        total = total + term.astype(F32)
    return total


def scatter_grads(ours, theirs):
    held = added(ours, swap(theirs, "core", 1)).astype(BF)
    held = held.reshape(4, 2, *held.shape[1:])
    up = shift(held[2, 0], "x", 1)
    down = shift(held[2, 1], "x", -1)
    up = jnp.stack([added(held[1, 0], up).astype(BF), held[1, 1]])
    down = jnp.stack([held[3, 0], added(held[3, 1], down).astype(BF)])
    up, down = shift(up, "x", 1), shift(down, "x", -1)
    away = added(held[0, 1], up[1], down[1]).astype(BF)
    return added(held[0, 0], up[0], down[0], swap(away, "yh", 1))


def sum_router(part):
    steps = (("core", 1), ("x", 1), ("x", 2), ("yh", 1))
    for axis, step in steps:
        low = lax.axis_index(axis) & step == 0
        half = part.shape[0] // 2
        away = jnp.where(low, part[half:], part[:half])
        part = jnp.where(low, part[:half], part[half:]) + swap(away, axis, step)
    for axis, step in (("yl", 1), ("z", 1), ("z", 2), ("z", 4)):
        part = part + swap(part, axis, step)
    for axis, step in reversed(steps):
        low = lax.axis_index(axis) & step == 0
        other = swap(part, axis, step)
        part = jnp.where(
            low, jnp.concatenate([part, other]), jnp.concatenate([other, part])
        )
    return part


def body(tokens, expert_ids, upstream, router_weight, gate_matrix, up_matrix, down_matrix):
    rows, width = tokens.shape
    top = expert_ids.shape[1]
    mine, hidden, _ = gate_matrix.shape
    peers = lax.axis_size(EXPERT)
    groups = lax.axis_size(DP)
    experts = peers * mine
    cap = rows * top * 3 // (2 * experts)
    router = router_weight.T
    token_blocks = gather_tokens(tokens)
    packed = pl.pallas_call(
        pack_kernel,
        out_shape=jax.ShapeDtypeStruct((rows + 16, width), BF),
    )(tokens, expert_ids.T, upstream, router)
    packed_blocks = gather_packed(packed)
    place = jnp.stack([lax.axis_index(axis) for axis in ALL]).astype(jnp.int32)
    out, ours, theirs, router_part = run_experts(
        place, token_blocks, packed_blocks, gate_matrix, up_matrix, down_matrix, router, cap, groups
    )
    out = lax.psum_scatter(out, EXPERT, scatter_dimension=0, tiled=False)
    router_grad = sum_router(router_part).T
    total = scatter_grads(ours, theirs)
    piece = hidden // groups
    both = total[0 : 2 * mine * piece].reshape(mine, 2, piece, width)
    down_grad = total[2 * mine * piece :].reshape(mine, piece, width)
    return out[0:rows], out[rows:], router_grad, both[:, 0], both[:, 1], down_grad


def solution(mesh):
    shape = {"x": 4, "yh": 2, "core": 2, "yl": 2, "z": 8}
    fine = jax.sharding.Mesh(mesh.devices.reshape(tuple(shape.values())), tuple(shape))
    in_specs = (
        P(ALL, None),
        P(ALL, None),
        P(ALL, None),
        P(),
        P(EXPERT, None, None),
        P(EXPERT, None, None),
        P(EXPERT, None, None),
    )
    out_specs = (
        P(ALL, None),
        P(ALL, None),
        P(),
        P(EXPERT, DP, None),
        P(EXPERT, DP, None),
        P(EXPERT, DP, None),
    )
    return jax.shard_map(body, mesh=fine, in_specs=in_specs, out_specs=out_specs, check_vma=False)
```

```python
import functools

import jax
import jax.numpy as jnp
from jax import lax
from jax.experimental import pallas as pl
from jax.experimental.pallas import tpu as pltpu
from jax.sharding import PartitionSpec as P

BF = jnp.bfloat16
F32 = jnp.float32
EXPERT = ("yl", "z")
DP = ("x", "yh", "core")
ALL = DP + EXPERT


def nt(a, b):
    return lax.dot_general(a, b, (((1,), (1,)), ((), ())), preferred_element_type=F32)


def tn(a, b):
    return lax.dot_general(a, b, (((0,), (0,)), ((), ())), preferred_element_type=F32)


def nn(a, b):
    return jnp.dot(a, b, preferred_element_type=F32)


def pack_kernel(tokens, ids, router, packed):
    rows = tokens.shape[0]
    experts = router.shape[0]
    packed[0:rows] = tokens[...]
    logits = nt(router[...], tokens[...])
    names = lax.broadcasted_iota(jnp.int32, (experts, rows), 0)
    chosen = names == ids[0:1, :]
    for k in range(1, ids.shape[0]):
        chosen = chosen | (names == ids[k : k + 1, :])
    raised = jnp.where(chosen, jnp.exp(logits), 0.0)
    probs = raised / jnp.sum(raised, axis=0, keepdims=True)
    wide = jnp.concatenate([probs[8 * b : 8 * b + 8, :] for b in range(experts // 8)], axis=1)
    high = wide.astype(BF).astype(F32)
    packed[rows : rows + 16] = jnp.concatenate([high, wide - high], axis=0).astype(BF)


def forward_kernel(*refs, cap, sources):
    place, tokens = refs[0], refs[1 : 1 + sources]
    gate, up, down = refs[1 + sources : 4 + sources]
    (mix, x_rows, pre_gates, pre_ups, picks, spreads, probs, local, weight) = refs[
        4 + sources : 13 + sources
    ]
    xs, produced, sems = refs[13 + sources :]
    e = pl.program_id(0)
    mine = local.shape[1]
    pairs, slots, pair_rows = picks.shape
    rows = pair_rows // 2
    experts = probs.shape[1]
    two = 2 * cap
    my_y, my_z = place[3], place[4]
    at_first = (my_y * pairs + my_z) * mine

    @pl.when(e == 0)
    def _():
        copies = [
            pltpu.make_async_copy(tokens[i], xs.at[i % pairs, i // pairs], sems.at[i])
            for i in range(sources)
        ]
        for copy in copies:
            copy.start()
        for copy in copies:
            copy.wait()
        t_from = lax.broadcasted_iota(jnp.int32, (rows, rows), 0)
        t_to = lax.broadcasted_iota(jnp.int32, (rows, rows), 1)
        before = jnp.where(t_from < t_to, 1.0, 0.0).astype(BF)
        names = lax.broadcasted_iota(jnp.int32, (experts, pair_rows), 0)
        slot_down = lax.broadcasted_iota(jnp.int32, (two, pair_rows), 0).astype(F32)
        slot_across = lax.broadcasted_iota(jnp.int32, (pair_rows, slots), 1).astype(F32)

        @pl.loop(0, pairs)
        def _(p):
            halves = []
            for h in range(2):
                ext = xs[p, h, rows : rows + 16].astype(F32)
                wide = ext[0:8] + ext[8:16]
                halves.append(
                    jnp.concatenate(
                        [wide[:, rows * b : rows * b + rows] for b in range(experts // 8)], axis=0
                    )
                )
            all_probs = jnp.concatenate(halves, axis=1)
            probs[p] = all_probs
            own = [
                jnp.sum(jnp.where(names == at_first + j, all_probs, 0.0), axis=0, keepdims=True)
                for j in range(mine)
            ]
            own = jnp.concatenate(own + [jnp.zeros((8 - mine, pair_rows), F32)], axis=0)
            local[p] = own[0:mine]
            taken = jnp.where(own > 0.0, 1.0, 0.0)
            rank = jnp.concatenate(
                [
                    nn(taken[:, 0:rows].astype(BF), before),
                    nn(taken[:, rows:].astype(BF), before) + float(cap),
                ],
                axis=1,
            )
            slot = jnp.where(taken > 0.0, rank, -1000.0)
            here = pl.ds(pl.multiple_of(p * two, two), two)
            parts = []
            for j in range(mine):
                hit = slot_down == slot[j : j + 1, :]
                parts.append(jnp.where(hit, 1.0, 0.0))
                weight[j, here, :] = jnp.sum(
                    jnp.where(hit, own[j : j + 1, :], 0.0), axis=1, keepdims=True
                )
            pick = jnp.concatenate(parts, axis=0).astype(BF)
            picks[p] = pick
            slot_t = jnp.transpose(slot)
            spread = jnp.zeros((pair_rows, slots), F32)
            for j in range(mine):
                column = slot_t[:, j : j + 1]
                spread = jnp.where(
                    slot_across == column + float(j * two),
                    jnp.where(column >= 0.0, 1.0, 0.0),
                    spread,
                )
            spreads[p] = spread.astype(BF)
            both = jnp.concatenate([xs[p, 0, 0:rows], xs[p, 1, 0:rows]], axis=0)
            got = nn(pick, both).astype(BF)
            for j in range(mine):
                x_rows[j, here, :] = got[j * two : j * two + two]

    x = x_rows[e]
    pre_gate = nt(x, gate[0])
    pre_up = nt(x, up[0])
    pre_gates[0] = pre_gate
    pre_ups[0] = pre_up
    scaled = (pre_gate * jax.nn.sigmoid(pre_gate) * pre_up * weight[e]).astype(BF)
    made = nn(scaled, down[0]).astype(BF)
    at = pl.ds(pl.multiple_of(e * two, two), two)
    for p in range(pairs):
        produced[p, at, :] = made[p * two : p * two + two]

    @pl.when(e == mine - 1)
    def _():
        @pl.loop(0, pairs)
        def _(p):
            got = nn(spreads[p], produced[p]).astype(BF)
            to = lax.rem(my_z + p, pairs)
            mix[my_y * pairs + to] = got[0:rows]
            mix[(1 - my_y) * pairs + to] = got[rows:]


def backward_kernel(*refs, cap, sources, blocks):
    place, tokens, cotangents = refs[0], refs[1 : 1 + sources], refs[1 + sources : 1 + sources + blocks]
    base = 1 + sources + blocks
    (
        gate,
        up,
        down,
        router,
        x_rows,
        pre_gates,
        pre_ups,
        picks,
        spreads,
        probs,
        local,
        weight,
        out,
        ours,
        theirs,
        router_part,
    ) = refs[base : base + 16]
    xs, us, u_rows, grads, scores, row_grads, down_kept, sems, end_sems = refs[base + 16 :]
    e = pl.program_id(0)
    mine = local.shape[1]
    pairs, slots, pair_rows = picks.shape
    rows = pair_rows // 2
    experts = router.shape[0]
    two = 2 * cap
    px, py, pc, my_y, my_z = [place[i] for i in range(5)]
    at_first = (my_y * pairs + my_z) * mine

    def slot_of(d):
        x_off = lax.rem(d // 4 + 4 - px, 4)
        y_off = jnp.where(py == d // 2 % 2, 0, 1)
        return jnp.where(pc == d % 2, 0, 1), x_off * 2 + y_off

    def token_copies():
        return [
            pltpu.make_async_copy(
                tokens[i].at[pl.ds(0, rows)],
                xs.at[i % pairs, pl.ds(i // pairs * rows, rows)],
                sems.at[i],
            )
            for i in range(sources)
        ]

    @pl.when(e == 0)
    def _():
        copies = []
        for i in range(blocks):
            to = us.at[i] if i < pairs // 2 else us.at[i + 1]
            if i >= pairs - 1:
                to = us.at[pairs // 2, i - (pairs - 1)]
            copies.append(pltpu.make_async_copy(cotangents[i], to, sems.at[sources + i]))
        for copy in copies:
            copy.start()
        for copy in copies:
            copy.wait()
        for copy in token_copies():
            copy.start()

        @pl.loop(0, pairs)
        def _(p):
            here = pl.ds(pl.multiple_of(p * two, two), two)
            got = nn(picks[p], jnp.concatenate([us[p, 0], us[p, 1]], axis=0)).astype(BF)
            for j in range(mine):
                u_rows[j, here, :] = got[j * two : j * two + two]

    x = x_rows[0]
    u = u_rows[e]
    pre_gate = pre_gates[0]
    pre_up = pre_ups[0]
    raw = nt(u, down[0])
    g = weight[0]
    logistic = jax.nn.sigmoid(pre_gate)
    swished = pre_gate * logistic
    activated = swished * pre_up
    scores[e] = jnp.sum(activated * raw, axis=1, keepdims=True)
    act_grad = raw * g
    scaled = (activated * g).astype(BF)
    gate_back = (act_grad * pre_up * logistic * (1.0 + pre_gate * (1.0 - logistic))).astype(BF)
    up_back = (act_grad * swished).astype(BF)
    at = pl.ds(pl.multiple_of(e * two, two), two)
    back = (nn(gate_back, gate[0]) + nn(up_back, up[0])).astype(BF)
    for p in range(pairs):
        row_grads[p, at, :] = back[p * two : p * two + two]
    chunks = 2 * grads.shape[1]
    gate_grad = tn(gate_back, x)
    up_grad = tn(up_back, x)
    piece = gate_grad.shape[0] // chunks
    for d in range(chunks):
        cut = slice(d * piece, d * piece + piece)
        grads[*slot_of(d), pl.ds(pl.multiple_of(e * 2 * piece, 2 * piece), 2 * piece), :] = (
            jnp.concatenate([gate_grad[cut], up_grad[cut]], axis=0).astype(BF)
        )
    down_grad = tn(scaled, u)

    @pl.when(e % 2 == 0)
    def _():
        down_kept[...] = down_grad

    @pl.when(e % 2 == 1)
    def _():
        start = mine * 2 * piece + (e // 2) * 2 * piece
        for d in range(chunks):
            cut = slice(d * piece, d * piece + piece)
            grads[*slot_of(d), pl.ds(pl.multiple_of(start, 2 * piece), 2 * piece), :] = (
                jnp.concatenate([down_kept[cut], down_grad[cut]], axis=0).astype(BF)
            )

    @pl.when(e == mine - 1)
    def _():
        finals = (
            pltpu.make_async_copy(grads.at[0], ours, end_sems.at[0]),
            pltpu.make_async_copy(grads.at[1], theirs, end_sems.at[1]),
        )
        for copy in finals:
            copy.start()
        for copy in token_copies():
            copy.wait()
        names = lax.broadcasted_iota(jnp.int32, (experts, pair_rows), 0)
        router_part[...] = jnp.zeros_like(router_part)

        @pl.loop(0, pairs)
        def _(p):
            pick = picks[p].astype(F32)
            own = local[p]
            total = jnp.zeros((1, pair_rows), F32)
            placed = jnp.zeros((experts, pair_rows), F32)
            for j in range(mine):
                score = scores[j, pl.ds(pl.multiple_of(p * two, two), two), :]
                grad = own[j : j + 1] * jnp.sum(
                    pick[j * two : j * two + two] * score, axis=0, keepdims=True
                )
                total = total + grad
                placed = jnp.where(names == at_first + j, grad, placed)
            logit_grad = placed - probs[p] * total
            high = logit_grad.astype(BF)
            low = (logit_grad - high.astype(F32)).astype(BF)
            both = nn(jnp.concatenate([high, low], axis=0), xs[p])
            router_part[...] += both[0:experts] + both[experts:]
            got = (nn(spreads[p], row_grads[p]) + tn(high, router[...])).astype(BF)
            out[p, 0] = got[0:rows]
            out[p, 1] = got[rows:]

        for copy in finals:
            copy.wait()


WHOLE = functools.partial(pl.BlockSpec, pipeline_mode=pl.Buffered(1))
ANYWHERE = pl.BlockSpec(memory_space=pl.ANY)


def whole(*shape):
    return WHOLE(shape, lambda e: (0,) * len(shape))


def each(*shape):
    return pl.BlockSpec((1, *shape), lambda e: (e, 0, 0))


def run_forward(place, tokens, gate, up, down, cap, experts):
    rows, width = tokens[0].shape
    rows = rows - 16
    mine, hidden, _ = gate.shape
    sources = len(tokens)
    pairs, slots, total = sources // 2, 2 * mine * cap, sources * cap
    shapes = (
        ((sources, rows, width), BF),
        ((mine, total, width), BF),
        ((mine, total, hidden), F32),
        ((mine, total, hidden), F32),
        ((pairs, slots, 2 * rows), BF),
        ((pairs, 2 * rows, slots), BF),
        ((pairs, experts, 2 * rows), F32),
        ((pairs, mine, 2 * rows), F32),
        ((mine, total, 1), F32),
    )
    specs = [whole(*shape) for shape, _ in shapes]
    specs[2] = specs[3] = each(total, hidden)
    return pl.pallas_call(
        functools.partial(forward_kernel, cap=cap, sources=sources),
        grid=(mine,),
        out_shape=tuple(jax.ShapeDtypeStruct(*one) for one in shapes),
        in_specs=[
            pl.BlockSpec(memory_space=pltpu.SMEM),
            *([ANYWHERE] * sources),
            *([each(hidden, width)] * 3),
        ],
        out_specs=tuple(specs),
        scratch_shapes=[
            pltpu.VMEM((pairs, 2, rows + 16, width), BF),
            pltpu.VMEM((pairs, slots, width), BF),
            pltpu.SemaphoreType.DMA((sources,)),
        ],
        compiler_params=pltpu.CompilerParams(vmem_limit_bytes=44 * 2**20),
        cost_estimate=pl.CostEstimate(
            flops=6 * 10**9, bytes_accessed=24 * 2**20, transcendentals=10**6
        ),
    )(place, *tokens, gate, up, down)


def run_backward(place, tokens, cotangents, gate, up, down, router, kept, cap, chunks):
    rows, width = tokens[0].shape
    rows = rows - 16
    mine, hidden, _ = gate.shape
    experts = router.shape[0]
    sources, blocks = len(tokens), len(cotangents)
    pairs, slots, total = sources // 2, 2 * mine * cap, sources * cap
    grad_rows = 3 * mine * hidden // chunks
    return pl.pallas_call(
        functools.partial(backward_kernel, cap=cap, sources=sources, blocks=blocks),
        grid=(mine,),
        out_shape=(
            jax.ShapeDtypeStruct((pairs, 2, rows, width), BF),
            jax.ShapeDtypeStruct((chunks // 2, grad_rows, width), BF),
            jax.ShapeDtypeStruct((chunks // 2, grad_rows, width), BF),
            jax.ShapeDtypeStruct((experts, width), F32),
        ),
        in_specs=[
            pl.BlockSpec(memory_space=pltpu.SMEM),
            *([ANYWHERE] * (sources + blocks)),
            *([each(hidden, width)] * 3),
            whole(experts, width),
            each(total, width),
            each(total, hidden),
            each(total, hidden),
            whole(pairs, slots, 2 * rows),
            whole(pairs, 2 * rows, slots),
            whole(pairs, experts, 2 * rows),
            whole(pairs, mine, 2 * rows),
            each(total, 1),
        ],
        out_specs=(
            whole(pairs, 2, rows, width),
            ANYWHERE,
            ANYWHERE,
            whole(experts, width),
        ),
        scratch_shapes=[
            pltpu.VMEM((pairs, 2 * rows, width), BF),
            pltpu.VMEM((pairs, 2, rows, width), BF),
            pltpu.VMEM((mine, total, width), BF),
            pltpu.VMEM((2, chunks // 2, grad_rows, width), BF),
            pltpu.VMEM((mine, total, 1), F32),
            pltpu.VMEM((pairs, slots, width), BF),
            pltpu.VMEM((hidden, width), F32),
            pltpu.SemaphoreType.DMA((sources + blocks,)),
            pltpu.SemaphoreType.DMA((2,)),
        ],
        compiler_params=pltpu.CompilerParams(vmem_limit_bytes=58 * 2**20),
        cost_estimate=pl.CostEstimate(
            flops=12 * 10**9, bytes_accessed=40 * 2**20, transcendentals=10**6
        ),
    )(place, *tokens, *cotangents, gate, up, down, router, *kept)


def swap(value, axis, step):
    size = lax.axis_size(axis)
    return lax.ppermute(value, axis, [(i, i ^ step) for i in range(size)])


def shift(value, axis, step):
    size = lax.axis_size(axis)
    return lax.ppermute(value, axis, [(i, (i + step) % size) for i in range(size)])


def after(value, *others):
    return lax.optimization_barrier((value, *others))[0]


def gather_group(block, other):
    half = block.shape[0] // 2
    both = jnp.stack([other, swap(other, "yl", 1)])
    right = left = block
    near, far = {0: block}, {0: swap(block, "yl", 1)}
    for k in range(1, 4):
        right, left = shift(right, "z", 1), shift(left, "z", -1)
        near[8 - k], near[k] = right, left
        far[8 - k], far[k] = swap(right, "yl", 1), swap(left, "yl", 1)
    ends = [shift(right[:half], "z", 1), shift(left[half:], "z", -1)]
    near[4] = jnp.concatenate(ends, axis=0)
    far[4] = swap(near[4], "yl", 1)
    right = left = after(both, *ends, far[0], far[1])
    found = {0: both}
    for k in range(1, 4):
        right, left = shift(right, "z", 1), shift(left, "z", -1)
        wait = ([far[7], far[2]], [far[6], far[3], far[4]], [far[5]])[k - 1]
        right, left = lax.optimization_barrier((right, left, *wait))[0:2]
        found[8 - k], found[k] = right, left
    last = [shift(right[0], "z", 1), shift(left[1], "z", -1)]
    blocks = [near[i] for i in range(8)] + [far[i] for i in range(8)]
    return blocks, [found[i] for i in (0, 1, 2, 3, 5, 6, 7)] + last


def added(*terms):
    total = terms[0].astype(F32)
    for term in terms[1:]:
        total = total + term.astype(F32)
    return total


def scatter_grads(ours, theirs, router_part):
    part, lows = router_part, []

    def halve(part, axis, step):
        low = lax.axis_index(axis) & step == 0
        half = part.shape[0] // 2
        away = jnp.where(low, part[half:], part[:half])
        lows.append((low, axis, step))
        return jnp.where(low, part[:half], part[half:]) + swap(away, axis, step)

    part = halve(part, "core", 1)
    part = halve(part, "x", 1)
    part = halve(part, "x", 2)
    held = added(ours, swap(theirs, "core", 1)).astype(BF)
    held = after(held, part)
    held = held.reshape(4, 2, *held.shape[1:])
    up = shift(held[2, 0], "x", 1)
    down = shift(held[2, 1], "x", -1)
    part = halve(part, "yh", 1)
    part = part + swap(part, "yl", 1)
    up = jnp.stack([added(held[1, 0], up).astype(BF), held[1, 1]])
    down = jnp.stack([held[3, 0], added(held[3, 1], down).astype(BF)])
    up, down = shift(up, "x", 1), shift(down, "x", -1)
    for step in (1, 2, 4):
        part = part + swap(part, "z", step)
    away = added(held[0, 1], up[1], down[1]).astype(BF)
    total = added(held[0, 0], up[0], down[0], swap(away, "yh", 1))
    part = after(part, away)
    for low, axis, step in reversed(lows):
        other = swap(part, axis, step)
        part = jnp.where(low, jnp.concatenate([part, other]), jnp.concatenate([other, part]))
    return total, part


def scatter_tokens(parts, mixture):
    right, left = shift(parts[4, 0], "z", 1), shift(parts[4, 1], "z", -1)
    right = jnp.stack([added(parts[3, 0], right).astype(BF), parts[3, 1]])
    left = jnp.stack([parts[5, 0], added(parts[5, 1], left).astype(BF)])
    for k in (2, 1, 0):
        if k == 1:
            right, left, mixture = lax.optimization_barrier((right, left, mixture))
        right, left = shift(right, "z", 1), shift(left, "z", -1)
        if k:
            right, left = added(parts[k], right).astype(BF), added(parts[8 - k], left).astype(BF)
    away = swap(added(parts[0, 1], right[1], left[1]).astype(BF), "yl", 1)
    return added(parts[0, 0], right[0], left[0], away).astype(BF), mixture


def body(tokens, expert_ids, upstream, router_weight, gate_matrix, up_matrix, down_matrix):
    rows, width = tokens.shape
    top = expert_ids.shape[1]
    mine, hidden, _ = gate_matrix.shape
    peers = lax.axis_size(EXPERT)
    groups = lax.axis_size(DP)
    experts = peers * mine
    cap = rows * top * 3 // (2 * experts)
    router = router_weight.T
    packed = pl.pallas_call(
        pack_kernel,
        out_shape=jax.ShapeDtypeStruct((rows + 16, width), BF),
    )(tokens, expert_ids.T, router)
    blocks, cotangents = gather_group(packed, upstream)
    place = jnp.stack([lax.axis_index(axis) for axis in ALL]).astype(jnp.int32)
    weights = (gate_matrix, up_matrix, down_matrix)
    mix, *kept = run_forward(place, blocks, *weights, cap, experts)
    mixture = lax.psum_scatter(mix, EXPERT, scatter_dimension=0, tiled=False)
    out, ours, theirs, router_part = run_backward(
        place, blocks, cotangents, *weights, router, kept, cap, groups
    )
    input_grad, mixture = scatter_tokens(out, mixture)
    total, router_grad = scatter_grads(ours, theirs, router_part)
    piece = hidden // groups
    both = total[0 : 2 * mine * piece].reshape(mine, 2, piece, width)
    down_grad = total[2 * mine * piece :].reshape(mine, piece, width)
    return mixture, input_grad, router_grad.T, both[:, 0], both[:, 1], down_grad


def solution(mesh):
    shape = {"x": 4, "yh": 2, "core": 2, "yl": 2, "z": 8}
    fine = jax.sharding.Mesh(mesh.devices.reshape(tuple(shape.values())), tuple(shape))
    in_specs = (
        P(ALL, None),
        P(ALL, None),
        P(ALL, None),
        P(),
        P(EXPERT, None, None),
        P(EXPERT, None, None),
        P(EXPERT, None, None),
    )
    out_specs = (
        P(ALL, None),
        P(ALL, None),
        P(),
        P(EXPERT, DP, None),
        P(EXPERT, DP, None),
        P(EXPERT, DP, None),
    )
    return jax.shard_map(body, mesh=fine, in_specs=in_specs, out_specs=out_specs, check_vma=False)
```

```python
import functools

import jax
import jax.numpy as jnp
from jax import lax
from jax.experimental import pallas as pl
from jax.experimental.pallas import tpu as pltpu
from jax.sharding import PartitionSpec as P

BF = jnp.bfloat16
F32 = jnp.float32
EXPERT = ("yl", "z")
DP = ("x", "yh", "core")
ALL = DP + EXPERT


def nt(a, b):
    return lax.dot_general(a, b, (((1,), (1,)), ((), ())), preferred_element_type=F32)


def tn(a, b):
    return lax.dot_general(a, b, (((0,), (0,)), ((), ())), preferred_element_type=F32)


def nn(a, b):
    return jnp.dot(a, b, preferred_element_type=F32)


def pack_kernel(tokens, ids, router, packed):
    rows = tokens.shape[0]
    experts = router.shape[0]
    packed[0:rows] = tokens[...]
    logits = nt(router[...], tokens[...])
    names = lax.broadcasted_iota(jnp.int32, (experts, rows), 0)
    chosen = names == ids[0:1, :]
    for k in range(1, ids.shape[0]):
        chosen = chosen | (names == ids[k : k + 1, :])
    raised = jnp.where(chosen, jnp.exp(logits), 0.0)
    probs = raised / jnp.sum(raised, axis=0, keepdims=True)
    wide = jnp.concatenate([probs[8 * b : 8 * b + 8, :] for b in range(experts // 8)], axis=1)
    high = wide.astype(BF).astype(F32)
    packed[rows : rows + 16] = jnp.concatenate([high, wide - high], axis=0).astype(BF)


def stacked(tokens, held, pairs, sems, start, rows):
    copies = []
    for i, block in enumerate(tokens):
        if i >= pairs - 1:
            to = held.at[pairs // 2, i - (pairs - 1)]
            block = block.at[pl.ds(0, rows)]
        else:
            to = held.at[i if i < pairs // 2 else i + 1]
            block = block.at[:, pl.ds(0, rows)]
        copies.append(pltpu.make_async_copy(block, to, sems.at[start + i]))
    return copies


def forward_kernel(*refs, cap, sources):
    place, tokens = refs[0], refs[1 : 1 + sources]
    gate, up, down = refs[1 + sources : 4 + sources]
    (mix, x_rows, pre_gates, pre_ups, picks, spreads, probs, local, weight) = refs[
        4 + sources : 13 + sources
    ]
    xs, produced, sems = refs[13 + sources :]
    e = pl.program_id(0)
    mine = local.shape[1]
    pairs, slots, pair_rows = picks.shape
    rows = pair_rows // 2
    experts = probs.shape[1]
    two = 2 * cap
    my_y, my_z = place[3], place[4]
    at_first = (my_y * pairs + my_z) * mine

    @pl.when(e == 0)
    def _():
        copies = stacked(tokens, xs, pairs, sems, 0, rows + 16)
        for copy in copies:
            copy.start()
        for copy in copies:
            copy.wait()
        t_from = lax.broadcasted_iota(jnp.int32, (rows, rows), 0)
        t_to = lax.broadcasted_iota(jnp.int32, (rows, rows), 1)
        before = jnp.where(t_from < t_to, 1.0, 0.0).astype(BF)
        names = lax.broadcasted_iota(jnp.int32, (experts, pair_rows), 0)
        slot_down = lax.broadcasted_iota(jnp.int32, (two, pair_rows), 0).astype(F32)
        slot_across = lax.broadcasted_iota(jnp.int32, (pair_rows, slots), 1).astype(F32)

        @pl.loop(0, pairs)
        def _(p):
            halves = []
            for h in range(2):
                ext = xs[p, h, rows : rows + 16].astype(F32)
                wide = ext[0:8] + ext[8:16]
                halves.append(
                    jnp.concatenate(
                        [wide[:, rows * b : rows * b + rows] for b in range(experts // 8)], axis=0
                    )
                )
            all_probs = jnp.concatenate(halves, axis=1)
            probs[p] = all_probs
            own = [
                jnp.sum(jnp.where(names == at_first + j, all_probs, 0.0), axis=0, keepdims=True)
                for j in range(mine)
            ]
            own = jnp.concatenate(own + [jnp.zeros((8 - mine, pair_rows), F32)], axis=0)
            local[p] = own[0:mine]
            taken = jnp.where(own > 0.0, 1.0, 0.0)
            rank = jnp.concatenate(
                [
                    nn(taken[:, 0:rows].astype(BF), before),
                    nn(taken[:, rows:].astype(BF), before) + float(cap),
                ],
                axis=1,
            )
            slot = jnp.where(taken > 0.0, rank, -1000.0)
            here = pl.ds(pl.multiple_of(p * two, two), two)
            parts = []
            for j in range(mine):
                hit = slot_down == slot[j : j + 1, :]
                parts.append(jnp.where(hit, 1.0, 0.0))
                weight[j, here, :] = jnp.sum(
                    jnp.where(hit, own[j : j + 1, :], 0.0), axis=1, keepdims=True
                )
            pick = jnp.concatenate(parts, axis=0).astype(BF)
            picks[p] = pick
            slot_t = jnp.transpose(slot)
            spread = jnp.zeros((pair_rows, slots), F32)
            for j in range(mine):
                column = slot_t[:, j : j + 1]
                spread = jnp.where(
                    slot_across == column + float(j * two),
                    jnp.where(column >= 0.0, 1.0, 0.0),
                    spread,
                )
            spreads[p] = spread.astype(BF)
            both = jnp.concatenate([xs[p, 0, 0:rows], xs[p, 1, 0:rows]], axis=0)
            got = nn(pick, both).astype(BF)
            for j in range(mine):
                x_rows[j, here, :] = got[j * two : j * two + two]

    x = x_rows[e]
    pre_gate = nt(x, gate[0])
    pre_up = nt(x, up[0])
    pre_gates[0] = pre_gate
    pre_ups[0] = pre_up
    scaled = (pre_gate * jax.nn.sigmoid(pre_gate) * pre_up * weight[e]).astype(BF)
    made = nn(scaled, down[0]).astype(BF)
    at = pl.ds(pl.multiple_of(e * two, two), two)
    for p in range(pairs):
        produced[p, at, :] = made[p * two : p * two + two]

    @pl.when(e == mine - 1)
    def _():
        @pl.loop(0, pairs)
        def _(p):
            got = nn(spreads[p], produced[p]).astype(BF)
            to = lax.rem(my_z + p, pairs)
            mix[my_y * pairs + to] = got[0:rows]
            mix[(1 - my_y) * pairs + to] = got[rows:]


def backward_kernel(*refs, cap, sources):
    place, tokens = refs[0], refs[1 : 1 + sources]
    (
        cotangents,
        down,
        x_rows,
        pre_gates,
        pre_ups,
        picks,
        probs,
        local,
        weight,
        ours,
        theirs,
        router_part,
        gate_backs,
        up_backs,
        logit_grads,
    ) = refs[1 + sources : 16 + sources]
    xs, us, u_rows, grads, scores, down_kept, sems, end_sems = refs[16 + sources :]
    e = pl.program_id(0)
    mine = local.shape[1]
    pairs, slots, pair_rows = picks.shape
    rows = pair_rows // 2
    experts = probs.shape[1]
    two = 2 * cap
    px, py, pc, my_y, my_z = [place[i] for i in range(5)]
    at_first = (my_y * pairs + my_z) * mine

    def slot_of(d):
        x_off = lax.rem(d // 4 + 4 - px, 4)
        y_off = jnp.where(py == d // 2 % 2, 0, 1)
        return jnp.where(pc == d % 2, 0, 1), x_off * 2 + y_off

    def token_copies():
        return stacked(tokens, xs, pairs, sems, 0, rows)

    @pl.when(e == 0)
    def _():
        copies = []
        for p in range(pairs):
            for h in range(2):
                at_y = my_y if h == 0 else 1 - my_y
                source = at_y * pairs + lax.rem(my_z + p, pairs)
                sem = sems.at[sources + len(copies)]
                copies.append(pltpu.make_async_copy(cotangents.at[source], us.at[p, h], sem))
        for copy in copies:
            copy.start()
        for copy in copies:
            copy.wait()
        for copy in token_copies():
            copy.start()

        @pl.loop(0, pairs)
        def _(p):
            here = pl.ds(pl.multiple_of(p * two, two), two)
            got = nn(picks[p], jnp.concatenate([us[p, 0], us[p, 1]], axis=0)).astype(BF)
            for j in range(mine):
                u_rows[j, here, :] = got[j * two : j * two + two]

    x = x_rows[0]
    u = u_rows[e]
    pre_gate = pre_gates[0]
    pre_up = pre_ups[0]
    raw = nt(u, down[0])
    g = weight[0]
    logistic = jax.nn.sigmoid(pre_gate)
    swished = pre_gate * logistic
    activated = swished * pre_up
    scores[e] = jnp.sum(activated * raw, axis=1, keepdims=True)
    act_grad = raw * g
    scaled = (activated * g).astype(BF)
    gate_back = (act_grad * pre_up * logistic * (1.0 + pre_gate * (1.0 - logistic))).astype(BF)
    up_back = (act_grad * swished).astype(BF)
    gate_backs[0] = gate_back
    up_backs[0] = up_back
    chunks = 2 * grads.shape[1]
    gate_grad = tn(gate_back, x)
    up_grad = tn(up_back, x)
    piece = gate_grad.shape[0] // chunks
    for d in range(chunks):
        cut = slice(d * piece, d * piece + piece)
        grads[*slot_of(d), pl.ds(pl.multiple_of(e * 2 * piece, 2 * piece), 2 * piece), :] = (
            jnp.concatenate([gate_grad[cut], up_grad[cut]], axis=0).astype(BF)
        )
    down_grad = tn(scaled, u)

    @pl.when(e % 2 == 0)
    def _():
        down_kept[...] = down_grad

    @pl.when(e % 2 == 1)
    def _():
        start = mine * 2 * piece + (e // 2) * 2 * piece
        for d in range(chunks):
            cut = slice(d * piece, d * piece + piece)
            grads[*slot_of(d), pl.ds(pl.multiple_of(start, 2 * piece), 2 * piece), :] = (
                jnp.concatenate([down_kept[cut], down_grad[cut]], axis=0).astype(BF)
            )

    @pl.when(e == mine - 1)
    def _():
        finals = (
            pltpu.make_async_copy(grads.at[0], ours, end_sems.at[0]),
            pltpu.make_async_copy(grads.at[1], theirs, end_sems.at[1]),
        )
        for copy in finals:
            copy.start()
        for copy in token_copies():
            copy.wait()
        names = lax.broadcasted_iota(jnp.int32, (experts, pair_rows), 0)
        router_part[...] = jnp.zeros_like(router_part)

        @pl.loop(0, pairs)
        def _(p):
            pick = picks[p].astype(F32)
            own = local[p]
            total = jnp.zeros((1, pair_rows), F32)
            placed = jnp.zeros((experts, pair_rows), F32)
            for j in range(mine):
                score = scores[j, pl.ds(pl.multiple_of(p * two, two), two), :]
                grad = own[j : j + 1] * jnp.sum(
                    pick[j * two : j * two + two] * score, axis=0, keepdims=True
                )
                total = total + grad
                placed = jnp.where(names == at_first + j, grad, placed)
            logit_grad = placed - probs[p] * total
            high = logit_grad.astype(BF)
            logit_grads[p] = high
            low = (logit_grad - high.astype(F32)).astype(BF)
            here = jnp.concatenate([xs[p, 0], xs[p, 1]], axis=0)
            both = nn(jnp.concatenate([high, low], axis=0), here)
            router_part[...] += both[0:experts] + both[experts:]

        for copy in finals:
            copy.wait()


def input_kernel(gate_backs, up_backs, gate, up, router, spreads, logit_grads, *rest, cap):
    outs, row_grads = rest[:-1], rest[-1]
    e = pl.program_id(0)
    pairs, pair_rows, _ = spreads.shape
    rows, two = pair_rows // 2, 2 * cap
    back = (nn(gate_backs[0], gate[0]) + nn(up_backs[0], up[0])).astype(BF)
    at = pl.ds(pl.multiple_of(e * two, two), two)
    for p in range(pairs):
        row_grads[p, at, :] = back[p * two : p * two + two]

    @pl.when(e == pl.num_programs(0) - 1)
    def _():
        for p in range(pairs):
            got = (nn(spreads[p], row_grads[p]) + tn(logit_grads[p], router[...])).astype(BF)
            for h in range(2):
                half = got[h * rows : h * rows + rows]
                if p == pairs // 2:
                    outs[pairs - 1 + h][...] = half
                else:
                    outs[p if p < pairs // 2 else p - 1][h] = half


WHOLE = functools.partial(pl.BlockSpec, pipeline_mode=pl.Buffered(1))
ANYWHERE = pl.BlockSpec(memory_space=pl.ANY)


def whole(*shape):
    return WHOLE(shape, lambda e: (0,) * len(shape))


def each(*shape):
    return pl.BlockSpec((1, *shape), lambda e: (e, 0, 0))


def run_forward(place, tokens, gate, up, down, cap, experts):
    rows, width = tokens[-1].shape
    rows = rows - 16
    mine, hidden, _ = gate.shape
    sources, pairs = len(tokens), len(tokens) - 1
    slots, total = 2 * mine * cap, 2 * pairs * cap
    shapes = (
        ((2 * pairs, rows, width), BF),
        ((mine, total, width), BF),
        ((mine, total, hidden), F32),
        ((mine, total, hidden), F32),
        ((pairs, slots, 2 * rows), BF),
        ((pairs, 2 * rows, slots), BF),
        ((pairs, experts, 2 * rows), F32),
        ((pairs, mine, 2 * rows), F32),
        ((mine, total, 1), F32),
    )
    specs = [whole(*shape) for shape, _ in shapes]
    specs[2] = specs[3] = each(total, hidden)
    return pl.pallas_call(
        functools.partial(forward_kernel, cap=cap, sources=sources),
        grid=(mine,),
        out_shape=tuple(jax.ShapeDtypeStruct(*one) for one in shapes),
        in_specs=[
            pl.BlockSpec(memory_space=pltpu.SMEM),
            *([ANYWHERE] * sources),
            *([each(hidden, width)] * 3),
        ],
        out_specs=tuple(specs),
        scratch_shapes=[
            pltpu.VMEM((pairs, 2, rows + 16, width), BF),
            pltpu.VMEM((pairs, slots, width), BF),
            pltpu.SemaphoreType.DMA((sources,)),
        ],
        compiler_params=pltpu.CompilerParams(vmem_limit_bytes=44 * 2**20),
        cost_estimate=pl.CostEstimate(
            flops=6 * 10**9, bytes_accessed=24 * 2**20, transcendentals=10**6
        ),
    )(place, *tokens, gate, up, down)


def run_backward(place, tokens, cotangents, down, kept, cap, chunks):
    x_rows, pre_gates, pre_ups, picks, probs, local, weight = kept
    rows, width = cotangents.shape[1:]
    mine, hidden, _ = down.shape
    sources, pairs = len(tokens), len(tokens) - 1
    slots, total = 2 * mine * cap, 2 * pairs * cap
    experts = probs.shape[1]
    grad_rows = 3 * mine * hidden // chunks
    return pl.pallas_call(
        functools.partial(backward_kernel, cap=cap, sources=sources),
        grid=(mine,),
        out_shape=(
            jax.ShapeDtypeStruct((chunks // 2, grad_rows, width), BF),
            jax.ShapeDtypeStruct((chunks // 2, grad_rows, width), BF),
            jax.ShapeDtypeStruct((experts, width), F32),
            jax.ShapeDtypeStruct((mine, total, hidden), BF),
            jax.ShapeDtypeStruct((mine, total, hidden), BF),
            jax.ShapeDtypeStruct((pairs, experts, 2 * rows), BF),
        ),
        in_specs=[
            pl.BlockSpec(memory_space=pltpu.SMEM),
            *([ANYWHERE] * (sources + 1)),
            each(hidden, width),
            each(total, width),
            each(total, hidden),
            each(total, hidden),
            whole(pairs, slots, 2 * rows),
            whole(pairs, experts, 2 * rows),
            whole(pairs, mine, 2 * rows),
            each(total, 1),
        ],
        out_specs=(
            ANYWHERE,
            ANYWHERE,
            whole(experts, width),
            each(total, hidden),
            each(total, hidden),
            whole(pairs, experts, 2 * rows),
        ),
        scratch_shapes=[
            pltpu.VMEM((pairs, 2, rows, width), BF),
            pltpu.VMEM((pairs, 2, rows, width), BF),
            pltpu.VMEM((mine, total, width), BF),
            pltpu.VMEM((2, chunks // 2, grad_rows, width), BF),
            pltpu.VMEM((mine, total, 1), F32),
            pltpu.VMEM((hidden, width), F32),
            pltpu.SemaphoreType.DMA((sources + 2 * pairs,)),
            pltpu.SemaphoreType.DMA((2,)),
        ],
        compiler_params=pltpu.CompilerParams(vmem_limit_bytes=52 * 2**20),
        cost_estimate=pl.CostEstimate(
            flops=8 * 10**9, bytes_accessed=40 * 2**20, transcendentals=10**6
        ),
    )(place, *tokens, cotangents, down, x_rows, pre_gates, pre_ups, picks, probs, local, weight)


def run_input(gate_backs, up_backs, gate, up, router, spreads, logit_grads, cap):
    mine, total, hidden = gate_backs.shape
    experts, width = router.shape
    pairs, pair_rows, slots = spreads.shape
    rows = pair_rows // 2
    shapes = [(2, rows, width)] * (pairs - 1) + [(rows, width)] * 2
    return pl.pallas_call(
        functools.partial(input_kernel, cap=cap),
        grid=(mine,),
        out_shape=tuple(jax.ShapeDtypeStruct(shape, BF) for shape in shapes),
        in_specs=[
            each(total, hidden),
            each(total, hidden),
            each(hidden, width),
            each(hidden, width),
            whole(experts, width),
            whole(pairs, pair_rows, slots),
            whole(pairs, experts, pair_rows),
        ],
        out_specs=tuple(whole(*shape) for shape in shapes),
        scratch_shapes=[pltpu.VMEM((pairs, slots, width), BF)],
        compiler_params=pltpu.CompilerParams(vmem_limit_bytes=32 * 2**20),
        cost_estimate=pl.CostEstimate(
            flops=5 * 10**9, bytes_accessed=20 * 2**20, transcendentals=0
        ),
    )(gate_backs, up_backs, gate, up, router, spreads, logit_grads)


def swap(value, axis, step):
    size = lax.axis_size(axis)
    return lax.ppermute(value, axis, [(i, i ^ step) for i in range(size)])


def shift(value, axis, step):
    size = lax.axis_size(axis)
    return lax.ppermute(value, axis, [(i, (i + step) % size) for i in range(size)])


def after(value, *others):
    return lax.optimization_barrier((value, *others))[0]


def gather_blocks(block):
    both = jnp.stack([block, swap(block, "yl", 1)])
    right = left = both
    found = {0: both}
    for k in range(1, 4):
        right, left = shift(right, "z", 1), shift(left, "z", -1)
        found[8 - k], found[k] = right, left
    last = [shift(right[0], "z", 1), shift(left[1], "z", -1)]
    return [found[i] for i in (0, 1, 2, 3, 5, 6, 7)] + last


def added(*terms):
    total = terms[0].astype(F32)
    for term in terms[1:]:
        total = total + term.astype(F32)
    return total


def scatter_grads(ours, theirs, router_part, *others):
    part, lows = router_part, []

    def halve(part, axis, step):
        low = lax.axis_index(axis) & step == 0
        half = part.shape[0] // 2
        away = jnp.where(low, part[half:], part[:half])
        lows.append((low, axis, step))
        return jnp.where(low, part[:half], part[half:]) + swap(away, axis, step)

    part = halve(part, "core", 1)
    part = halve(part, "x", 1)
    part = halve(part, "x", 2)
    held = added(ours, swap(theirs, "core", 1)).astype(BF)
    held = after(held, part, *others)
    held = held.reshape(4, 2, *held.shape[1:])
    up = shift(held[2, 0], "x", 1)
    down = shift(held[2, 1], "x", -1)
    part = halve(part, "yh", 1)
    part = part + swap(part, "yl", 1)
    up = jnp.stack([added(held[1, 0], up).astype(BF), held[1, 1]])
    down = jnp.stack([held[3, 0], added(held[3, 1], down).astype(BF)])
    up, down = shift(up, "x", 1), shift(down, "x", -1)
    for step in (1, 2, 4):
        part = part + swap(part, "z", step)
    away = added(held[0, 1], up[1], down[1]).astype(BF)
    total = added(held[0, 0], up[0], down[0], swap(away, "yh", 1))
    part = after(part, away)
    for low, axis, step in reversed(lows):
        other = swap(part, axis, step)
        part = jnp.where(low, jnp.concatenate([part, other]), jnp.concatenate([other, part]))
    return total, part


def scatter_tokens(outs, right, left, mixture):
    parts = dict(zip((0, 1, 2, 3, 5, 6, 7), outs))
    right = added(parts[3], jnp.stack([right, jnp.zeros_like(right)])).astype(BF)
    left = added(parts[5], jnp.stack([jnp.zeros_like(left), left])).astype(BF)
    for k in (2, 1, 0):
        if k == 0:
            right, left, mixture = lax.optimization_barrier((right, left, mixture))
        right, left = shift(right, "z", 1), shift(left, "z", -1)
        if k:
            right, left = added(parts[k], right).astype(BF), added(parts[8 - k], left).astype(BF)
    away = swap(added(parts[0][1], right[1], left[1]).astype(BF), "yl", 1)
    return added(parts[0][0], right[0], left[0], away).astype(BF), mixture


def body(tokens, expert_ids, upstream, router_weight, gate_matrix, up_matrix, down_matrix):
    rows, width = tokens.shape
    top = expert_ids.shape[1]
    mine, hidden, _ = gate_matrix.shape
    peers = lax.axis_size(EXPERT)
    groups = lax.axis_size(DP)
    experts = peers * mine
    cap = rows * top * 3 // (2 * experts)
    router = router_weight.T
    packed = pl.pallas_call(
        pack_kernel,
        out_shape=jax.ShapeDtypeStruct((rows + 16, width), BF),
    )(tokens, expert_ids.T, router)
    cotangents = lax.all_gather(upstream, EXPERT, axis=0, tiled=False)
    blocks = gather_blocks(packed)
    place = jnp.stack([lax.axis_index(axis) for axis in ALL]).astype(jnp.int32)
    mix, *kept = run_forward(place, blocks, gate_matrix, up_matrix, down_matrix, cap, experts)
    spreads = kept.pop(4)
    mixture = lax.psum_scatter(mix, EXPERT, scatter_dimension=0, tiled=False)
    ours, theirs, router_part, gate_backs, up_backs, logit_grads = run_backward(
        place, blocks, cotangents, down_matrix, kept, cap, groups
    )
    outs = run_input(
        gate_backs, up_backs, gate_matrix, up_matrix, router, spreads, logit_grads, cap
    )
    right, left = shift(outs[7], "z", 1), shift(outs[8], "z", -1)
    total, router_grad = scatter_grads(ours, theirs, router_part, right, left)
    input_grad, mixture = scatter_tokens(outs, right, left, mixture)
    piece = hidden // groups
    both = total[0 : 2 * mine * piece].reshape(mine, 2, piece, width)
    down_grad = total[2 * mine * piece :].reshape(mine, piece, width)
    return mixture, input_grad, router_grad.T, both[:, 0], both[:, 1], down_grad


def solution(mesh):
    shape = {"x": 4, "yh": 2, "core": 2, "yl": 2, "z": 8}
    fine = jax.sharding.Mesh(mesh.devices.reshape(tuple(shape.values())), tuple(shape))
    in_specs = (
        P(ALL, None),
        P(ALL, None),
        P(ALL, None),
        P(),
        P(EXPERT, None, None),
        P(EXPERT, None, None),
        P(EXPERT, None, None),
    )
    out_specs = (
        P(ALL, None),
        P(ALL, None),
        P(),
        P(EXPERT, DP, None),
        P(EXPERT, DP, None),
        P(EXPERT, DP, None),
    )
    return jax.shard_map(body, mesh=fine, in_specs=in_specs, out_specs=out_specs, check_vma=False)
```

```python
import functools

import jax
import jax.numpy as jnp
from jax import lax
from jax.experimental import pallas as pl
from jax.experimental.pallas import tpu as pltpu
from jax.sharding import PartitionSpec as P

BF = jnp.bfloat16
F32 = jnp.float32
EXPERT = ("yl", "z")
DP = ("x", "yh", "core")
ALL = DP + EXPERT


def nt(a, b):
    return lax.dot_general(a, b, (((1,), (1,)), ((), ())), preferred_element_type=F32)


def tn(a, b):
    return lax.dot_general(a, b, (((0,), (0,)), ((), ())), preferred_element_type=F32)


def nn(a, b):
    return jnp.dot(a, b, preferred_element_type=F32)


def pack_kernel(tokens, ids, router, packed):
    rows = tokens.shape[0]
    experts = router.shape[0]
    packed[0:rows] = tokens[...]
    logits = nt(router[...], tokens[...])
    names = lax.broadcasted_iota(jnp.int32, (experts, rows), 0)
    chosen = names == ids[0:1, :]
    for k in range(1, ids.shape[0]):
        chosen = chosen | (names == ids[k : k + 1, :])
    raised = jnp.where(chosen, jnp.exp(logits), 0.0)
    probs = raised / jnp.sum(raised, axis=0, keepdims=True)
    wide = jnp.concatenate([probs[8 * b : 8 * b + 8, :] for b in range(experts // 8)], axis=1)
    high = wide.astype(BF).astype(F32)
    packed[rows : rows + 16] = jnp.concatenate([high, wide - high], axis=0).astype(BF)


def stacked(tokens, held, sems, rows):
    pairs = held.shape[0]
    return [
        pltpu.make_async_copy(
            block.at[pl.ds(0, rows)], held.at[i % pairs, i // pairs], sems.at[i]
        )
        for i, block in enumerate(tokens)
    ]


def forward_kernel(*refs, cap, sources):
    place, tokens = refs[0], refs[1 : 1 + sources]
    gate, up, down = refs[1 + sources : 4 + sources]
    (mix, x_rows, pre_gates, pre_ups, picks, spreads, probs, local, weight) = refs[
        4 + sources : 13 + sources
    ]
    xs, produced, sems = refs[13 + sources :]
    e = pl.program_id(0)
    mine = local.shape[1]
    pairs, slots, pair_rows = picks.shape
    rows = pair_rows // 2
    experts = probs.shape[1]
    two = 2 * cap
    my_y, my_z = place[3], place[4]
    at_first = (my_y * pairs + my_z) * mine

    @pl.when(e == 0)
    def _():
        copies = stacked(tokens, xs, sems, rows + 16)
        for copy in copies:
            copy.start()
        for copy in copies:
            copy.wait()
        t_from = lax.broadcasted_iota(jnp.int32, (rows, rows), 0)
        t_to = lax.broadcasted_iota(jnp.int32, (rows, rows), 1)
        before = jnp.where(t_from < t_to, 1.0, 0.0).astype(BF)
        names = lax.broadcasted_iota(jnp.int32, (experts, pair_rows), 0)
        slot_down = lax.broadcasted_iota(jnp.int32, (two, pair_rows), 0).astype(F32)
        slot_across = lax.broadcasted_iota(jnp.int32, (pair_rows, slots), 1).astype(F32)

        @pl.loop(0, pairs)
        def _(p):
            halves = []
            for h in range(2):
                ext = xs[p, h, rows : rows + 16].astype(F32)
                wide = ext[0:8] + ext[8:16]
                halves.append(
                    jnp.concatenate(
                        [wide[:, rows * b : rows * b + rows] for b in range(experts // 8)], axis=0
                    )
                )
            all_probs = jnp.concatenate(halves, axis=1)
            probs[p] = all_probs
            own = [
                jnp.sum(jnp.where(names == at_first + j, all_probs, 0.0), axis=0, keepdims=True)
                for j in range(mine)
            ]
            own = jnp.concatenate(own + [jnp.zeros((8 - mine, pair_rows), F32)], axis=0)
            local[p] = own[0:mine]
            taken = jnp.where(own > 0.0, 1.0, 0.0)
            rank = jnp.concatenate(
                [
                    nn(taken[:, 0:rows].astype(BF), before),
                    nn(taken[:, rows:].astype(BF), before) + float(cap),
                ],
                axis=1,
            )
            slot = jnp.where(taken > 0.0, rank, -1000.0)
            here = pl.ds(pl.multiple_of(p * two, two), two)
            parts = []
            for j in range(mine):
                hit = slot_down == slot[j : j + 1, :]
                parts.append(jnp.where(hit, 1.0, 0.0))
                weight[j, here, :] = jnp.sum(
                    jnp.where(hit, own[j : j + 1, :], 0.0), axis=1, keepdims=True
                )
            pick = jnp.concatenate(parts, axis=0).astype(BF)
            picks[p] = pick
            slot_t = jnp.transpose(slot)
            spread = jnp.zeros((pair_rows, slots), F32)
            for j in range(mine):
                column = slot_t[:, j : j + 1]
                spread = jnp.where(
                    slot_across == column + float(j * two),
                    jnp.where(column >= 0.0, 1.0, 0.0),
                    spread,
                )
            spreads[p] = spread.astype(BF)
            both = jnp.concatenate([xs[p, 0, 0:rows], xs[p, 1, 0:rows]], axis=0)
            got = nn(pick, both).astype(BF)
            for j in range(mine):
                x_rows[j, here, :] = got[j * two : j * two + two]

    x = x_rows[e]
    pre_gate = nt(x, gate[0])
    pre_up = nt(x, up[0])
    pre_gates[0] = pre_gate
    pre_ups[0] = pre_up
    scaled = (pre_gate * jax.nn.sigmoid(pre_gate) * pre_up * weight[e]).astype(BF)
    made = nn(scaled, down[0]).astype(BF)
    at = pl.ds(pl.multiple_of(e * two, two), two)
    for p in range(pairs):
        produced[p, at, :] = made[p * two : p * two + two]

    @pl.when(e == mine - 1)
    def _():
        @pl.loop(0, pairs)
        def _(p):
            got = nn(spreads[p], produced[p]).astype(BF)
            to = lax.rem(my_z + p, pairs)
            mix[my_y * pairs + to] = got[0:rows]
            mix[(1 - my_y) * pairs + to] = got[rows:]


def backward_kernel(*refs, cap, sources):
    place, tokens = refs[0], refs[1 : 1 + sources]
    (
        cotangents,
        down,
        x_rows,
        pre_gates,
        pre_ups,
        picks,
        probs,
        local,
        weight,
        ours,
        theirs,
        router_part,
        gate_backs,
        up_backs,
        logit_grads,
    ) = refs[1 + sources : 16 + sources]
    xs, us, u_rows, grads, scores, down_kept, sems, end_sems = refs[16 + sources :]
    e = pl.program_id(0)
    mine = local.shape[1]
    pairs, slots, pair_rows = picks.shape
    rows = pair_rows // 2
    experts = probs.shape[1]
    two = 2 * cap
    px, py, pc, my_y, my_z = [place[i] for i in range(5)]
    at_first = (my_y * pairs + my_z) * mine

    def slot_of(d):
        x_off = lax.rem(d // 4 + 4 - px, 4)
        y_off = jnp.where(py == d // 2 % 2, 0, 1)
        return jnp.where(pc == d % 2, 0, 1), x_off * 2 + y_off

    def token_copies():
        return stacked(tokens, xs, sems, rows)

    @pl.when(e == 0)
    def _():
        copies = []
        for p in range(pairs):
            for h in range(2):
                at_y = my_y if h == 0 else 1 - my_y
                source = at_y * pairs + lax.rem(my_z + p, pairs)
                sem = sems.at[sources + len(copies)]
                copies.append(pltpu.make_async_copy(cotangents.at[source], us.at[p, h], sem))
        for copy in copies:
            copy.start()
        for copy in copies:
            copy.wait()
        for copy in token_copies():
            copy.start()

        @pl.loop(0, pairs)
        def _(p):
            here = pl.ds(pl.multiple_of(p * two, two), two)
            got = nn(picks[p], jnp.concatenate([us[p, 0], us[p, 1]], axis=0)).astype(BF)
            for j in range(mine):
                u_rows[j, here, :] = got[j * two : j * two + two]

    x = x_rows[0]
    u = u_rows[e]
    pre_gate = pre_gates[0]
    pre_up = pre_ups[0]
    raw = nt(u, down[0])
    g = weight[0]
    logistic = jax.nn.sigmoid(pre_gate)
    swished = pre_gate * logistic
    activated = swished * pre_up
    scores[e] = jnp.sum(activated * raw, axis=1, keepdims=True)
    act_grad = raw * g
    scaled = (activated * g).astype(BF)
    gate_back = (act_grad * pre_up * logistic * (1.0 + pre_gate * (1.0 - logistic))).astype(BF)
    up_back = (act_grad * swished).astype(BF)
    gate_backs[0] = gate_back
    up_backs[0] = up_back
    chunks = 2 * grads.shape[1]
    gate_grad = tn(gate_back, x)
    up_grad = tn(up_back, x)
    piece = gate_grad.shape[0] // chunks
    for d in range(chunks):
        cut = slice(d * piece, d * piece + piece)
        grads[*slot_of(d), pl.ds(pl.multiple_of(e * 2 * piece, 2 * piece), 2 * piece), :] = (
            jnp.concatenate([gate_grad[cut], up_grad[cut]], axis=0).astype(BF)
        )
    down_grad = tn(scaled, u)

    @pl.when(e % 2 == 0)
    def _():
        down_kept[...] = down_grad

    @pl.when(e % 2 == 1)
    def _():
        start = mine * 2 * piece + (e // 2) * 2 * piece
        for d in range(chunks):
            cut = slice(d * piece, d * piece + piece)
            grads[*slot_of(d), pl.ds(pl.multiple_of(start, 2 * piece), 2 * piece), :] = (
                jnp.concatenate([down_kept[cut], down_grad[cut]], axis=0).astype(BF)
            )

    @pl.when(e == mine - 1)
    def _():
        finals = (
            pltpu.make_async_copy(grads.at[0], ours, end_sems.at[0]),
            pltpu.make_async_copy(grads.at[1], theirs, end_sems.at[1]),
        )
        for copy in finals:
            copy.start()
        for copy in token_copies():
            copy.wait()
        names = lax.broadcasted_iota(jnp.int32, (experts, pair_rows), 0)
        router_part[...] = jnp.zeros_like(router_part)

        @pl.loop(0, pairs)
        def _(p):
            pick = picks[p].astype(F32)
            own = local[p]
            total = jnp.zeros((1, pair_rows), F32)
            placed = jnp.zeros((experts, pair_rows), F32)
            for j in range(mine):
                score = scores[j, pl.ds(pl.multiple_of(p * two, two), two), :]
                grad = own[j : j + 1] * jnp.sum(
                    pick[j * two : j * two + two] * score, axis=0, keepdims=True
                )
                total = total + grad
                placed = jnp.where(names == at_first + j, grad, placed)
            logit_grad = placed - probs[p] * total
            high = logit_grad.astype(BF)
            logit_grads[p] = high
            low = (logit_grad - high.astype(F32)).astype(BF)
            here = jnp.concatenate([xs[p, 0], xs[p, 1]], axis=0)
            both = nn(jnp.concatenate([high, low], axis=0), here)
            router_part[...] += both[0:experts] + both[experts:]

        for copy in finals:
            copy.wait()


def input_kernel(gate_backs, up_backs, gate, up, router, spreads, logit_grads, *rest, cap):
    outs, row_grads = rest[:-1], rest[-1]
    e = pl.program_id(0)
    pairs, pair_rows, _ = spreads.shape
    rows, two = pair_rows // 2, 2 * cap
    back = (nn(gate_backs[0], gate[0]) + nn(up_backs[0], up[0])).astype(BF)
    at = pl.ds(pl.multiple_of(e * two, two), two)
    for p in range(pairs):
        row_grads[p, at, :] = back[p * two : p * two + two]

    @pl.when(e == pl.num_programs(0) - 1)
    def _():
        for p in range(pairs):
            got = (nn(spreads[p], row_grads[p]) + tn(logit_grads[p], router[...])).astype(BF)
            for h in range(2):
                half = got[h * rows : h * rows + rows]
                if p == pairs // 2:
                    outs[pairs - 1 + h][...] = half
                else:
                    outs[p if p < pairs // 2 else p - 1][h] = half


WHOLE = functools.partial(pl.BlockSpec, pipeline_mode=pl.Buffered(1))
ANYWHERE = pl.BlockSpec(memory_space=pl.ANY)


def whole(*shape):
    return WHOLE(shape, lambda e: (0,) * len(shape))


def each(*shape):
    return pl.BlockSpec((1, *shape), lambda e: (e, 0, 0))


def run_forward(place, tokens, gate, up, down, cap, experts):
    rows, width = tokens[-1].shape
    rows = rows - 16
    mine, hidden, _ = gate.shape
    sources, pairs = len(tokens), len(tokens) // 2
    slots, total = 2 * mine * cap, 2 * pairs * cap
    shapes = (
        ((2 * pairs, rows, width), BF),
        ((mine, total, width), BF),
        ((mine, total, hidden), F32),
        ((mine, total, hidden), F32),
        ((pairs, slots, 2 * rows), BF),
        ((pairs, 2 * rows, slots), BF),
        ((pairs, experts, 2 * rows), F32),
        ((pairs, mine, 2 * rows), F32),
        ((mine, total, 1), F32),
    )
    specs = [whole(*shape) for shape, _ in shapes]
    specs[2] = specs[3] = each(total, hidden)
    return pl.pallas_call(
        functools.partial(forward_kernel, cap=cap, sources=sources),
        grid=(mine,),
        out_shape=tuple(jax.ShapeDtypeStruct(*one) for one in shapes),
        in_specs=[
            pl.BlockSpec(memory_space=pltpu.SMEM),
            *([ANYWHERE] * sources),
            *([each(hidden, width)] * 3),
        ],
        out_specs=tuple(specs),
        scratch_shapes=[
            pltpu.VMEM((pairs, 2, rows + 16, width), BF),
            pltpu.VMEM((pairs, slots, width), BF),
            pltpu.SemaphoreType.DMA((sources,)),
        ],
        compiler_params=pltpu.CompilerParams(vmem_limit_bytes=60 * 2**20),
        cost_estimate=pl.CostEstimate(
            flops=6 * 10**9, bytes_accessed=24 * 2**20, transcendentals=10**6
        ),
    )(place, *tokens, gate, up, down)


def run_backward(place, tokens, cotangents, down, kept, cap, chunks):
    x_rows, pre_gates, pre_ups, picks, probs, local, weight = kept
    rows, width = cotangents.shape[1:]
    mine, hidden, _ = down.shape
    sources, pairs = len(tokens), len(tokens) // 2
    slots, total = 2 * mine * cap, 2 * pairs * cap
    experts = probs.shape[1]
    grad_rows = 3 * mine * hidden // chunks
    return pl.pallas_call(
        functools.partial(backward_kernel, cap=cap, sources=sources),
        grid=(mine,),
        out_shape=(
            jax.ShapeDtypeStruct((chunks // 2, grad_rows, width), BF),
            jax.ShapeDtypeStruct((chunks // 2, grad_rows, width), BF),
            jax.ShapeDtypeStruct((experts, width), F32),
            jax.ShapeDtypeStruct((mine, total, hidden), BF),
            jax.ShapeDtypeStruct((mine, total, hidden), BF),
            jax.ShapeDtypeStruct((pairs, experts, 2 * rows), BF),
        ),
        in_specs=[
            pl.BlockSpec(memory_space=pltpu.SMEM),
            *([ANYWHERE] * (sources + 1)),
            each(hidden, width),
            each(total, width),
            each(total, hidden),
            each(total, hidden),
            whole(pairs, slots, 2 * rows),
            whole(pairs, experts, 2 * rows),
            whole(pairs, mine, 2 * rows),
            each(total, 1),
        ],
        out_specs=(
            ANYWHERE,
            ANYWHERE,
            whole(experts, width),
            each(total, hidden),
            each(total, hidden),
            whole(pairs, experts, 2 * rows),
        ),
        scratch_shapes=[
            pltpu.VMEM((pairs, 2, rows, width), BF),
            pltpu.VMEM((pairs, 2, rows, width), BF),
            pltpu.VMEM((mine, total, width), BF),
            pltpu.VMEM((2, chunks // 2, grad_rows, width), BF),
            pltpu.VMEM((mine, total, 1), F32),
            pltpu.VMEM((hidden, width), F32),
            pltpu.SemaphoreType.DMA((sources + 2 * pairs,)),
            pltpu.SemaphoreType.DMA((2,)),
        ],
        compiler_params=pltpu.CompilerParams(vmem_limit_bytes=60 * 2**20),
        cost_estimate=pl.CostEstimate(
            flops=8 * 10**9, bytes_accessed=40 * 2**20, transcendentals=10**6
        ),
    )(place, *tokens, cotangents, down, x_rows, pre_gates, pre_ups, picks, probs, local, weight)


def run_input(gate_backs, up_backs, gate, up, router, spreads, logit_grads, cap):
    mine, total, hidden = gate_backs.shape
    experts, width = router.shape
    pairs, pair_rows, slots = spreads.shape
    rows = pair_rows // 2
    shapes = [(2, rows, width)] * (pairs - 1) + [(rows, width)] * 2
    return pl.pallas_call(
        functools.partial(input_kernel, cap=cap),
        grid=(mine,),
        out_shape=tuple(jax.ShapeDtypeStruct(shape, BF) for shape in shapes),
        in_specs=[
            each(total, hidden),
            each(total, hidden),
            each(hidden, width),
            each(hidden, width),
            whole(experts, width),
            whole(pairs, pair_rows, slots),
            whole(pairs, experts, pair_rows),
        ],
        out_specs=tuple(whole(*shape) for shape in shapes),
        scratch_shapes=[pltpu.VMEM((pairs, slots, width), BF)],
        compiler_params=pltpu.CompilerParams(vmem_limit_bytes=60 * 2**20),
        cost_estimate=pl.CostEstimate(
            flops=5 * 10**9, bytes_accessed=20 * 2**20, transcendentals=0
        ),
    )(gate_backs, up_backs, gate, up, router, spreads, logit_grads)


def swap(value, axis, step):
    size = lax.axis_size(axis)
    return lax.ppermute(value, axis, [(i, i ^ step) for i in range(size)])


def shift(value, axis, step):
    size = lax.axis_size(axis)
    return lax.ppermute(value, axis, [(i, (i + step) % size) for i in range(size)])


def after(value, *others):
    return lax.optimization_barrier((value, *others))[0]


def gather_blocks(block):
    right = left = block
    near, far = {0: block}, {0: swap(block, "yl", 1)}
    for k in range(1, 4):
        right, left = shift(right, "z", 1), shift(left, "z", -1)
        near[8 - k], near[k] = right, left
        far[8 - k], far[k] = swap(right, "yl", 1), swap(left, "yl", 1)
        if k == 2:
            right, left, _ = lax.optimization_barrier((right, left, far[0]))
        if k == 3:
            right, _, _ = lax.optimization_barrier((right, far[1], far[7]))
    near[4] = shift(right, "z", 1)
    far[4] = swap(near[4], "yl", 1)
    return [near[i] for i in range(8)] + [far[i] for i in range(8)]


def added(*terms):
    total = terms[0].astype(F32)
    for term in terms[1:]:
        total = total + term.astype(F32)
    return total


def reduce_all(outs, mixture, ours, theirs, router_part):
    part, lows = router_part, []

    def halve(part, axis, step):
        low = lax.axis_index(axis) & step == 0
        half = part.shape[0] // 2
        away = jnp.where(low, part[half:], part[:half])
        lows.append((low, axis, step))
        return jnp.where(low, part[:half], part[half:]) + swap(away, axis, step)

    parts = dict(zip((0, 1, 2, 3, 5, 6, 7), outs))
    part = halve(part, "core", 1)
    part = halve(part, "x", 1)
    part = halve(part, "x", 2)
    right, left = shift(outs[7], "z", 1), shift(outs[8], "z", -1)
    held = added(ours, swap(theirs, "core", 1)).astype(BF)
    held = after(held, part, right, left)
    held = held.reshape(4, 2, *held.shape[1:])
    up = shift(held[2, 0], "x", 1)
    down = shift(held[2, 1], "x", -1)
    right = added(parts[3], jnp.stack([right, jnp.zeros_like(right)])).astype(BF)
    left = added(parts[5], jnp.stack([jnp.zeros_like(left), left])).astype(BF)
    right, left = shift(right, "z", 1), shift(left, "z", -1)
    part = halve(part, "yh", 1)
    part = part + swap(part, "yl", 1)
    up = jnp.stack([added(held[1, 0], up).astype(BF), held[1, 1]])
    down = jnp.stack([held[3, 0], added(held[3, 1], down).astype(BF)])
    up, down, part = lax.optimization_barrier((up, down, part))
    up, down = shift(up, "x", 1), shift(down, "x", -1)
    right, left = added(parts[2], right).astype(BF), added(parts[6], left).astype(BF)
    part = part + swap(part, "z", 1)
    right, left, part = lax.optimization_barrier((right, left, part))
    right, left = shift(right, "z", 1), shift(left, "z", -1)
    part = part + swap(part, "z", 2)
    part = part + swap(part, "z", 4)
    right, left = added(parts[1], right).astype(BF), added(parts[7], left).astype(BF)
    right, left, mixture, part = lax.optimization_barrier((right, left, mixture, part))
    right, left = shift(right, "z", 1), shift(left, "z", -1)
    away = added(held[0, 1], up[1], down[1]).astype(BF)
    away, part = lax.optimization_barrier((away, part))
    total = added(held[0, 0], up[0], down[0], swap(away, "yh", 1))
    for low, axis, step in reversed(lows):
        other = swap(part, axis, step)
        part = jnp.where(low, jnp.concatenate([part, other]), jnp.concatenate([other, part]))
    away = swap(added(parts[0][1], right[1], left[1]).astype(BF), "yl", 1)
    input_grad = added(parts[0][0], right[0], left[0], away).astype(BF)
    return mixture, input_grad, total, part


def body(tokens, expert_ids, upstream, router_weight, gate_matrix, up_matrix, down_matrix):
    rows, width = tokens.shape
    top = expert_ids.shape[1]
    mine, hidden, _ = gate_matrix.shape
    peers = lax.axis_size(EXPERT)
    groups = lax.axis_size(DP)
    experts = peers * mine
    cap = rows * top * 3 // (2 * experts)
    router = router_weight.T
    packed = pl.pallas_call(
        pack_kernel,
        out_shape=jax.ShapeDtypeStruct((rows + 16, width), BF),
    )(tokens, expert_ids.T, router)
    cotangents = lax.all_gather(upstream, EXPERT, axis=0, tiled=False)
    blocks = gather_blocks(packed)
    place = jnp.stack([lax.axis_index(axis) for axis in ALL]).astype(jnp.int32)
    mix, *kept = run_forward(place, blocks, gate_matrix, up_matrix, down_matrix, cap, experts)
    spreads = kept.pop(4)
    mixture = lax.psum_scatter(mix, EXPERT, scatter_dimension=0, tiled=False)
    ours, theirs, router_part, gate_backs, up_backs, logit_grads = run_backward(
        place, blocks, cotangents, down_matrix, kept, cap, groups
    )
    outs = run_input(
        gate_backs, up_backs, gate_matrix, up_matrix, router, spreads, logit_grads, cap
    )
    mixture, input_grad, total, router_grad = reduce_all(
        outs, mixture, ours, theirs, router_part
    )
    piece = hidden // groups
    both = total[0 : 2 * mine * piece].reshape(mine, 2, piece, width)
    down_grad = total[2 * mine * piece :].reshape(mine, piece, width)
    return mixture, input_grad, router_grad.T, both[:, 0], both[:, 1], down_grad


def solution(mesh):
    shape = {"x": 4, "yh": 2, "core": 2, "yl": 2, "z": 8}
    fine = jax.sharding.Mesh(mesh.devices.reshape(tuple(shape.values())), tuple(shape))
    in_specs = (
        P(ALL, None),
        P(ALL, None),
        P(ALL, None),
        P(),
        P(EXPERT, None, None),
        P(EXPERT, None, None),
        P(EXPERT, None, None),
    )
    out_specs = (
        P(ALL, None),
        P(ALL, None),
        P(),
        P(EXPERT, DP, None),
        P(EXPERT, DP, None),
        P(EXPERT, DP, None),
    )
    return jax.shard_map(body, mesh=fine, in_specs=in_specs, out_specs=out_specs, check_vma=False)
```

```python
import functools

import jax
import jax.numpy as jnp
from jax import lax
from jax.experimental import pallas as pl
from jax.experimental.pallas import tpu as pltpu
from jax.sharding import PartitionSpec as P

BF = jnp.bfloat16
F32 = jnp.float32
EXPERT = ("yl", "z")
DP = ("x", "yh", "core")
ALL = DP + EXPERT


def nt(a, b):
    return lax.dot_general(a, b, (((1,), (1,)), ((), ())), preferred_element_type=F32)


def tn(a, b):
    return lax.dot_general(a, b, (((0,), (0,)), ((), ())), preferred_element_type=F32)


def nn(a, b):
    return jnp.dot(a, b, preferred_element_type=F32)


def pack_kernel(tokens, ids, router, packed):
    rows = tokens.shape[0]
    experts = router.shape[0]
    packed[0:rows] = tokens[...]
    logits = nt(router[...], tokens[...])
    names = lax.broadcasted_iota(jnp.int32, (experts, rows), 0)
    chosen = names == ids[0:1, :]
    for k in range(1, ids.shape[0]):
        chosen = chosen | (names == ids[k : k + 1, :])
    raised = jnp.where(chosen, jnp.exp(logits), 0.0)
    probs = raised / jnp.sum(raised, axis=0, keepdims=True)
    wide = jnp.concatenate([probs[8 * b : 8 * b + 8, :] for b in range(experts // 8)], axis=1)
    high = wide.astype(BF).astype(F32)
    packed[rows : rows + 16] = jnp.concatenate([high, wide - high], axis=0).astype(BF)


def stacked(tokens, held, sems, rows):
    pairs = held.shape[0]
    return [
        pltpu.make_async_copy(
            block.at[pl.ds(0, rows)], held.at[i % pairs, i // pairs], sems.at[i]
        )
        for i, block in enumerate(tokens)
    ]


def forward_kernel(*refs, cap, sources):
    place, tokens = refs[0], refs[1 : 1 + sources]
    gate, up, down = refs[1 + sources : 4 + sources]
    (mix, x_rows, pre_gates, pre_ups, picks, spreads, probs, local, weight) = refs[
        4 + sources : 13 + sources
    ]
    xs, produced, sems = refs[13 + sources :]
    e = pl.program_id(0)
    mine = local.shape[1]
    pairs, slots, pair_rows = picks.shape
    rows = pair_rows // 2
    experts = probs.shape[1]
    two = 2 * cap
    my_y, my_z = place[3], place[4]
    at_first = (my_y * pairs + my_z) * mine

    @pl.when(e == 0)
    def _():
        copies = stacked(tokens, xs, sems, rows + 16)
        for copy in copies:
            copy.start()
        for copy in copies:
            copy.wait()
        t_from = lax.broadcasted_iota(jnp.int32, (rows, rows), 0)
        t_to = lax.broadcasted_iota(jnp.int32, (rows, rows), 1)
        before = jnp.where(t_from < t_to, 1.0, 0.0).astype(BF)
        names = lax.broadcasted_iota(jnp.int32, (experts, pair_rows), 0)
        slot_down = lax.broadcasted_iota(jnp.int32, (two, pair_rows), 0).astype(F32)
        slot_across = lax.broadcasted_iota(jnp.int32, (pair_rows, slots), 1).astype(F32)

        @pl.loop(0, pairs)
        def _(p):
            halves = []
            for h in range(2):
                ext = xs[p, h, rows : rows + 16].astype(F32)
                wide = ext[0:8] + ext[8:16]
                halves.append(
                    jnp.concatenate(
                        [wide[:, rows * b : rows * b + rows] for b in range(experts // 8)], axis=0
                    )
                )
            all_probs = jnp.concatenate(halves, axis=1)
            probs[p] = all_probs
            own = [
                jnp.sum(jnp.where(names == at_first + j, all_probs, 0.0), axis=0, keepdims=True)
                for j in range(mine)
            ]
            own = jnp.concatenate(own + [jnp.zeros((8 - mine, pair_rows), F32)], axis=0)
            local[p] = own[0:mine]
            taken = jnp.where(own > 0.0, 1.0, 0.0)
            rank = jnp.concatenate(
                [
                    nn(taken[:, 0:rows].astype(BF), before),
                    nn(taken[:, rows:].astype(BF), before) + float(cap),
                ],
                axis=1,
            )
            slot = jnp.where(taken > 0.0, rank, -1000.0)
            here = pl.ds(pl.multiple_of(p * two, two), two)
            parts = []
            for j in range(mine):
                hit = slot_down == slot[j : j + 1, :]
                parts.append(jnp.where(hit, 1.0, 0.0))
                weight[j, here, :] = jnp.sum(
                    jnp.where(hit, own[j : j + 1, :], 0.0), axis=1, keepdims=True
                )
            pick = jnp.concatenate(parts, axis=0).astype(BF)
            picks[p] = pick
            slot_t = jnp.transpose(slot)
            spread = jnp.zeros((pair_rows, slots), F32)
            for j in range(mine):
                column = slot_t[:, j : j + 1]
                spread = jnp.where(
                    slot_across == column + float(j * two),
                    jnp.where(column >= 0.0, 1.0, 0.0),
                    spread,
                )
            spreads[p] = spread.astype(BF)
            both = jnp.concatenate([xs[p, 0, 0:rows], xs[p, 1, 0:rows]], axis=0)
            got = nn(pick, both).astype(BF)
            for j in range(mine):
                x_rows[j, here, :] = got[j * two : j * two + two]

    x = x_rows[e]
    pre_gate = nt(x, gate[0])
    pre_up = nt(x, up[0])
    pre_gates[0] = pre_gate
    pre_ups[0] = pre_up
    scaled = (pre_gate * jax.nn.sigmoid(pre_gate) * pre_up * weight[e]).astype(BF)
    made = nn(scaled, down[0]).astype(BF)
    at = pl.ds(pl.multiple_of(e * two, two), two)
    for p in range(pairs):
        produced[p, at, :] = made[p * two : p * two + two]

    @pl.when(e == mine - 1)
    def _():
        @pl.loop(0, pairs)
        def _(p):
            got = nn(spreads[p], produced[p]).astype(BF)
            to = lax.rem(my_z + p, pairs)
            mix[my_y * pairs + to] = got[0:rows]
            mix[(1 - my_y) * pairs + to] = got[rows:]


def backward_kernel(*refs, cap, sources, stacks):
    place, tokens = refs[0], refs[1 : 1 + sources]
    cotangents = refs[1 + sources : 1 + sources + stacks]
    base = 1 + sources + stacks
    (
        down,
        x_rows,
        pre_gates,
        pre_ups,
        picks,
        probs,
        local,
        weight,
        ours,
        theirs,
        router_part,
        gate_backs,
        up_backs,
        logit_grads,
    ) = refs[base : base + 14]
    xs, us, u_rows, grads, scores, down_kept, sems, end_sems = refs[base + 14 :]
    e = pl.program_id(0)
    mine = local.shape[1]
    pairs, slots, pair_rows = picks.shape
    rows = pair_rows // 2
    experts = probs.shape[1]
    two = 2 * cap
    px, py, pc, my_y, my_z = [place[i] for i in range(5)]
    at_first = (my_y * pairs + my_z) * mine

    def slot_of(d):
        x_off = lax.rem(d // 4 + 4 - px, 4)
        y_off = jnp.where(py == d // 2 % 2, 0, 1)
        return jnp.where(pc == d % 2, 0, 1), x_off * 2 + y_off

    def token_copies():
        return stacked(tokens, xs, sems, rows)

    @pl.when(e == 0)
    def _():
        copies = []
        for i in range(stacks):
            to = us.at[i] if i < pairs // 2 else us.at[i + 1]
            if i >= pairs - 1:
                to = us.at[pairs // 2, i - (pairs - 1)]
            copies.append(pltpu.make_async_copy(cotangents[i], to, sems.at[sources + i]))
        for copy in copies:
            copy.start()
        for copy in copies:
            copy.wait()
        for copy in token_copies():
            copy.start()

        @pl.loop(0, pairs)
        def _(p):
            here = pl.ds(pl.multiple_of(p * two, two), two)
            got = nn(picks[p], jnp.concatenate([us[p, 0], us[p, 1]], axis=0)).astype(BF)
            for j in range(mine):
                u_rows[j, here, :] = got[j * two : j * two + two]

    x = x_rows[0]
    u = u_rows[e]
    pre_gate = pre_gates[0]
    pre_up = pre_ups[0]
    raw = nt(u, down[0])
    g = weight[0]
    logistic = jax.nn.sigmoid(pre_gate)
    swished = pre_gate * logistic
    activated = swished * pre_up
    scores[e] = jnp.sum(activated * raw, axis=1, keepdims=True)
    act_grad = raw * g
    scaled = (activated * g).astype(BF)
    gate_back = (act_grad * pre_up * logistic * (1.0 + pre_gate * (1.0 - logistic))).astype(BF)
    up_back = (act_grad * swished).astype(BF)
    gate_backs[0] = gate_back
    up_backs[0] = up_back
    chunks = 2 * grads.shape[1]
    gate_grad = tn(gate_back, x)
    up_grad = tn(up_back, x)
    piece = gate_grad.shape[0] // chunks
    for d in range(chunks):
        cut = slice(d * piece, d * piece + piece)
        grads[*slot_of(d), pl.ds(pl.multiple_of(e * 2 * piece, 2 * piece), 2 * piece), :] = (
            jnp.concatenate([gate_grad[cut], up_grad[cut]], axis=0).astype(BF)
        )
    down_grad = tn(scaled, u)

    @pl.when(e % 2 == 0)
    def _():
        down_kept[...] = down_grad

    @pl.when(e % 2 == 1)
    def _():
        start = mine * 2 * piece + (e // 2) * 2 * piece
        for d in range(chunks):
            cut = slice(d * piece, d * piece + piece)
            grads[*slot_of(d), pl.ds(pl.multiple_of(start, 2 * piece), 2 * piece), :] = (
                jnp.concatenate([down_kept[cut], down_grad[cut]], axis=0).astype(BF)
            )

    @pl.when(e == mine - 1)
    def _():
        finals = (
            pltpu.make_async_copy(grads.at[0], ours, end_sems.at[0]),
            pltpu.make_async_copy(grads.at[1], theirs, end_sems.at[1]),
        )
        for copy in finals:
            copy.start()
        for copy in token_copies():
            copy.wait()
        names = lax.broadcasted_iota(jnp.int32, (experts, pair_rows), 0)
        router_part[...] = jnp.zeros_like(router_part)

        @pl.loop(0, pairs)
        def _(p):
            pick = picks[p].astype(F32)
            own = local[p]
            total = jnp.zeros((1, pair_rows), F32)
            placed = jnp.zeros((experts, pair_rows), F32)
            for j in range(mine):
                score = scores[j, pl.ds(pl.multiple_of(p * two, two), two), :]
                grad = own[j : j + 1] * jnp.sum(
                    pick[j * two : j * two + two] * score, axis=0, keepdims=True
                )
                total = total + grad
                placed = jnp.where(names == at_first + j, grad, placed)
            logit_grad = placed - probs[p] * total
            high = logit_grad.astype(BF)
            logit_grads[p] = high
            low = (logit_grad - high.astype(F32)).astype(BF)
            here = jnp.concatenate([xs[p, 0], xs[p, 1]], axis=0)
            both = nn(jnp.concatenate([high, low], axis=0), here)
            router_part[...] += both[0:experts] + both[experts:]

        for copy in finals:
            copy.wait()


def input_kernel(gate_backs, up_backs, gate, up, router, spreads, logit_grads, *rest, cap):
    outs, row_grads = rest[:-1], rest[-1]
    e = pl.program_id(0)
    pairs, pair_rows, _ = spreads.shape
    rows, two = pair_rows // 2, 2 * cap
    back = (nn(gate_backs[0], gate[0]) + nn(up_backs[0], up[0])).astype(BF)
    at = pl.ds(pl.multiple_of(e * two, two), two)
    for p in range(pairs):
        row_grads[p, at, :] = back[p * two : p * two + two]

    @pl.when(e == pl.num_programs(0) - 1)
    def _():
        for p in range(pairs):
            got = (nn(spreads[p], row_grads[p]) + tn(logit_grads[p], router[...])).astype(BF)
            for h in range(2):
                half = got[h * rows : h * rows + rows]
                if p == pairs // 2:
                    outs[pairs - 1 + h][...] = half
                else:
                    outs[p if p < pairs // 2 else p - 1][h] = half


WHOLE = functools.partial(pl.BlockSpec, pipeline_mode=pl.Buffered(1))
ANYWHERE = pl.BlockSpec(memory_space=pl.ANY)


def whole(*shape):
    return WHOLE(shape, lambda e: (0,) * len(shape))


def each(*shape):
    return pl.BlockSpec((1, *shape), lambda e: (e, 0, 0))


def run_forward(place, tokens, gate, up, down, cap, experts):
    rows, width = tokens[-1].shape
    rows = rows - 16
    mine, hidden, _ = gate.shape
    sources, pairs = len(tokens), len(tokens) // 2
    slots, total = 2 * mine * cap, 2 * pairs * cap
    shapes = (
        ((2 * pairs, rows, width), BF),
        ((mine, total, width), BF),
        ((mine, total, hidden), F32),
        ((mine, total, hidden), F32),
        ((pairs, slots, 2 * rows), BF),
        ((pairs, 2 * rows, slots), BF),
        ((pairs, experts, 2 * rows), F32),
        ((pairs, mine, 2 * rows), F32),
        ((mine, total, 1), F32),
    )
    specs = [whole(*shape) for shape, _ in shapes]
    specs[2] = specs[3] = each(total, hidden)
    return pl.pallas_call(
        functools.partial(forward_kernel, cap=cap, sources=sources),
        grid=(mine,),
        out_shape=tuple(jax.ShapeDtypeStruct(*one) for one in shapes),
        in_specs=[
            pl.BlockSpec(memory_space=pltpu.SMEM),
            *([ANYWHERE] * sources),
            *([each(hidden, width)] * 3),
        ],
        out_specs=tuple(specs),
        scratch_shapes=[
            pltpu.VMEM((pairs, 2, rows + 16, width), BF),
            pltpu.VMEM((pairs, slots, width), BF),
            pltpu.SemaphoreType.DMA((sources,)),
        ],
        compiler_params=pltpu.CompilerParams(vmem_limit_bytes=60 * 2**20),
        cost_estimate=pl.CostEstimate(
            flops=6 * 10**9, bytes_accessed=24 * 2**20, transcendentals=10**6
        ),
    )(place, *tokens, gate, up, down)


def run_backward(place, tokens, cotangents, down, kept, cap, chunks):
    x_rows, pre_gates, pre_ups, picks, probs, local, weight = kept
    rows, width = cotangents[-1].shape
    stacks = len(cotangents)
    mine, hidden, _ = down.shape
    sources, pairs = len(tokens), len(tokens) // 2
    slots, total = 2 * mine * cap, 2 * pairs * cap
    experts = probs.shape[1]
    grad_rows = 3 * mine * hidden // chunks
    return pl.pallas_call(
        functools.partial(backward_kernel, cap=cap, sources=sources, stacks=stacks),
        grid=(mine,),
        out_shape=(
            jax.ShapeDtypeStruct((chunks // 2, grad_rows, width), BF),
            jax.ShapeDtypeStruct((chunks // 2, grad_rows, width), BF),
            jax.ShapeDtypeStruct((experts, width), F32),
            jax.ShapeDtypeStruct((mine, total, hidden), BF),
            jax.ShapeDtypeStruct((mine, total, hidden), BF),
            jax.ShapeDtypeStruct((pairs, experts, 2 * rows), BF),
        ),
        in_specs=[
            pl.BlockSpec(memory_space=pltpu.SMEM),
            *([ANYWHERE] * (sources + stacks)),
            each(hidden, width),
            each(total, width),
            each(total, hidden),
            each(total, hidden),
            whole(pairs, slots, 2 * rows),
            whole(pairs, experts, 2 * rows),
            whole(pairs, mine, 2 * rows),
            each(total, 1),
        ],
        out_specs=(
            ANYWHERE,
            ANYWHERE,
            whole(experts, width),
            each(total, hidden),
            each(total, hidden),
            whole(pairs, experts, 2 * rows),
        ),
        scratch_shapes=[
            pltpu.VMEM((pairs, 2, rows, width), BF),
            pltpu.VMEM((pairs, 2, rows, width), BF),
            pltpu.VMEM((mine, total, width), BF),
            pltpu.VMEM((2, chunks // 2, grad_rows, width), BF),
            pltpu.VMEM((mine, total, 1), F32),
            pltpu.VMEM((hidden, width), F32),
            pltpu.SemaphoreType.DMA((sources + stacks,)),
            pltpu.SemaphoreType.DMA((2,)),
        ],
        compiler_params=pltpu.CompilerParams(vmem_limit_bytes=60 * 2**20),
        cost_estimate=pl.CostEstimate(
            flops=8 * 10**9, bytes_accessed=40 * 2**20, transcendentals=10**6
        ),
    )(place, *tokens, *cotangents, down, x_rows, pre_gates, pre_ups, picks, probs, local, weight)


def run_input(gate_backs, up_backs, gate, up, router, spreads, logit_grads, cap):
    mine, total, hidden = gate_backs.shape
    experts, width = router.shape
    pairs, pair_rows, slots = spreads.shape
    rows = pair_rows // 2
    shapes = [(2, rows, width)] * (pairs - 1) + [(rows, width)] * 2
    return pl.pallas_call(
        functools.partial(input_kernel, cap=cap),
        grid=(mine,),
        out_shape=tuple(jax.ShapeDtypeStruct(shape, BF) for shape in shapes),
        in_specs=[
            each(total, hidden),
            each(total, hidden),
            each(hidden, width),
            each(hidden, width),
            whole(experts, width),
            whole(pairs, pair_rows, slots),
            whole(pairs, experts, pair_rows),
        ],
        out_specs=tuple(whole(*shape) for shape in shapes),
        scratch_shapes=[pltpu.VMEM((pairs, slots, width), BF)],
        compiler_params=pltpu.CompilerParams(vmem_limit_bytes=60 * 2**20),
        cost_estimate=pl.CostEstimate(
            flops=5 * 10**9, bytes_accessed=20 * 2**20, transcendentals=0
        ),
    )(gate_backs, up_backs, gate, up, router, spreads, logit_grads)


def swap(value, axis, step):
    size = lax.axis_size(axis)
    return lax.ppermute(value, axis, [(i, i ^ step) for i in range(size)])


def shift(value, axis, step):
    size = lax.axis_size(axis)
    return lax.ppermute(value, axis, [(i, (i + step) % size) for i in range(size)])


def after(value, *others):
    return lax.optimization_barrier((value, *others))[0]


def gather_group(block, other):
    hold = lax.optimization_barrier
    both = jnp.stack([other, swap(other, "yl", 1)])
    near, far = {0: block}, {0: swap(block, "yl", 1)}

    def cross(*distances):
        for k in distances:
            far[k] = swap(near[k], "yl", 1)

    near[7], near[1] = shift(block, "z", 1), shift(block, "z", -1)
    right, left, both = hold((near[7], near[1], both))
    near[6], near[2] = shift(right, "z", 1), shift(left, "z", -1)
    cross(1, 7)
    right, left, far[0] = hold((near[6], near[2], far[0]))
    near[5], near[3] = shift(right, "z", 1), shift(left, "z", -1)
    cross(2, 6)
    right, far[1] = hold((near[5], far[1]))
    near[4] = shift(right, "z", 1)
    cross(3, 5, 4)
    both, near[4], far[7] = hold((both, near[4], far[7]))
    found = {0: both}
    right, left = shift(both, "z", 1), shift(both, "z", -1)
    right, left, far[2], far[6] = hold((right, left, far[2], far[6]))
    found[7], found[1] = right, left
    right, left = shift(right, "z", 1), shift(left, "z", -1)
    right, left, far[3], far[5] = hold((right, left, far[3], far[5]))
    found[6], found[2] = right, left
    right, left = shift(right, "z", 1), shift(left, "z", -1)
    right, left, far[4] = hold((right, left, far[4]))
    found[5], found[3] = right, left
    last = [shift(right[0], "z", 1), shift(left[1], "z", -1)]
    blocks = [near[i] for i in range(8)] + [far[i] for i in range(8)]
    return blocks, [found[i] for i in (0, 1, 2, 3, 5, 6, 7)] + last


def added(*terms):
    total = terms[0].astype(F32)
    for term in terms[1:]:
        total = total + term.astype(F32)
    return total


def reduce_all(outs, mixture, ours, theirs, router_part):
    part, lows = router_part, []

    def halve(part, axis, step):
        low = lax.axis_index(axis) & step == 0
        half = part.shape[0] // 2
        away = jnp.where(low, part[half:], part[:half])
        lows.append((low, axis, step))
        return jnp.where(low, part[:half], part[half:]) + swap(away, axis, step)

    parts = dict(zip((0, 1, 2, 3, 5, 6, 7), outs))
    part = halve(part, "core", 1)
    part = halve(part, "x", 1)
    part = halve(part, "x", 2)
    right, left = shift(outs[7], "z", 1), shift(outs[8], "z", -1)
    held = added(ours, swap(theirs, "core", 1)).astype(BF)
    held = after(held, part)
    held = held.reshape(4, 2, *held.shape[1:])
    up = shift(held[2, 0], "x", 1)
    down = shift(held[2, 1], "x", -1)
    right = added(parts[3], jnp.stack([right, jnp.zeros_like(right)])).astype(BF)
    left = added(parts[5], jnp.stack([jnp.zeros_like(left), left])).astype(BF)
    right, left = shift(right, "z", 1), shift(left, "z", -1)
    part = halve(part, "yh", 1)
    part = part + swap(part, "yl", 1)
    up = jnp.stack([added(held[1, 0], up).astype(BF), held[1, 1]])
    down = jnp.stack([held[3, 0], added(held[3, 1], down).astype(BF)])
    up, down, part = lax.optimization_barrier((up, down, part))
    up, down = shift(up, "x", 1), shift(down, "x", -1)
    right, left = added(parts[2], right).astype(BF), added(parts[6], left).astype(BF)
    part = part + swap(part, "z", 1)
    right, left, part, mixture = lax.optimization_barrier((right, left, part, mixture))
    right, left = shift(right, "z", 1), shift(left, "z", -1)
    part = part + swap(part, "z", 2)
    part = part + swap(part, "z", 4)
    right, left = added(parts[1], right).astype(BF), added(parts[7], left).astype(BF)
    right, left, part = lax.optimization_barrier((right, left, part))
    right, left = shift(right, "z", 1), shift(left, "z", -1)
    away = added(held[0, 1], up[1], down[1]).astype(BF)
    away, part = lax.optimization_barrier((away, part))
    total = added(held[0, 0], up[0], down[0], swap(away, "yh", 1))
    for low, axis, step in reversed(lows):
        other = swap(part, axis, step)
        part = jnp.where(low, jnp.concatenate([part, other]), jnp.concatenate([other, part]))
    away = swap(added(parts[0][1], right[1], left[1]).astype(BF), "yl", 1)
    input_grad = added(parts[0][0], right[0], left[0], away).astype(BF)
    return mixture, input_grad, total, part


def body(tokens, expert_ids, upstream, router_weight, gate_matrix, up_matrix, down_matrix):
    rows, width = tokens.shape
    top = expert_ids.shape[1]
    mine, hidden, _ = gate_matrix.shape
    peers = lax.axis_size(EXPERT)
    groups = lax.axis_size(DP)
    experts = peers * mine
    cap = rows * top * 3 // (2 * experts)
    router = router_weight.T
    packed = pl.pallas_call(
        pack_kernel,
        out_shape=jax.ShapeDtypeStruct((rows + 16, width), BF),
    )(tokens, expert_ids.T, router)
    blocks, cotangents = gather_group(packed, upstream)
    place = jnp.stack([lax.axis_index(axis) for axis in ALL]).astype(jnp.int32)
    mix, *kept = run_forward(place, blocks, gate_matrix, up_matrix, down_matrix, cap, experts)
    spreads = kept.pop(4)
    mixture = lax.psum_scatter(mix, EXPERT, scatter_dimension=0, tiled=False)
    ours, theirs, router_part, gate_backs, up_backs, logit_grads = run_backward(
        place, blocks, cotangents, down_matrix, kept, cap, groups
    )
    outs = run_input(
        gate_backs, up_backs, gate_matrix, up_matrix, router, spreads, logit_grads, cap
    )
    mixture, input_grad, total, router_grad = reduce_all(
        outs, mixture, ours, theirs, router_part
    )
    piece = hidden // groups
    both = total[0 : 2 * mine * piece].reshape(mine, 2, piece, width)
    down_grad = total[2 * mine * piece :].reshape(mine, piece, width)
    return mixture, input_grad, router_grad.T, both[:, 0], both[:, 1], down_grad


def solution(mesh):
    shape = {"x": 4, "yh": 2, "core": 2, "yl": 2, "z": 8}
    fine = jax.sharding.Mesh(mesh.devices.reshape(tuple(shape.values())), tuple(shape))
    in_specs = (
        P(ALL, None),
        P(ALL, None),
        P(ALL, None),
        P(),
        P(EXPERT, None, None),
        P(EXPERT, None, None),
        P(EXPERT, None, None),
    )
    out_specs = (
        P(ALL, None),
        P(ALL, None),
        P(),
        P(EXPERT, DP, None),
        P(EXPERT, DP, None),
        P(EXPERT, DP, None),
    )
    return jax.shard_map(body, mesh=fine, in_specs=in_specs, out_specs=out_specs, check_vma=False)
```

```python
import functools

import jax
import jax.numpy as jnp
from jax import lax
from jax.experimental import pallas as pl
from jax.experimental.pallas import tpu as pltpu
from jax.sharding import PartitionSpec as P

BF = jnp.bfloat16
F32 = jnp.float32
EXPERT = ("yl", "z")
DP = ("x", "yh", "core")
ALL = DP + EXPERT


def nt(a, b):
    return lax.dot_general(a, b, (((1,), (1,)), ((), ())), preferred_element_type=F32)


def tn(a, b):
    return lax.dot_general(a, b, (((0,), (0,)), ((), ())), preferred_element_type=F32)


def nn(a, b):
    return jnp.dot(a, b, preferred_element_type=F32)


def pack_kernel(tokens, ids, router, packed):
    rows = tokens.shape[0]
    experts = router.shape[0]
    packed[0:rows] = tokens[...]
    logits = nt(router[...], tokens[...])
    names = lax.broadcasted_iota(jnp.int32, (experts, rows), 0)
    chosen = names == ids[0:1, :]
    for k in range(1, ids.shape[0]):
        chosen = chosen | (names == ids[k : k + 1, :])
    raised = jnp.where(chosen, jnp.exp(logits), 0.0)
    probs = raised / jnp.sum(raised, axis=0, keepdims=True)
    wide = jnp.concatenate([probs[8 * b : 8 * b + 8, :] for b in range(experts // 8)], axis=1)
    high = wide.astype(BF).astype(F32)
    packed[rows : rows + 16] = jnp.concatenate([high, wide - high], axis=0).astype(BF)


def stacked(tokens, held, sems, rows):
    pairs = held.shape[0]
    return [
        pltpu.make_async_copy(
            block.at[pl.ds(0, rows)], held.at[i % pairs, i // pairs], sems.at[i]
        )
        for i, block in enumerate(tokens)
    ]


def forward_kernel(*refs, cap, sources):
    place, tokens = refs[0], refs[1 : 1 + sources]
    gate, up, down = refs[1 + sources : 4 + sources]
    (mix, x_rows, pre_gates, pre_ups, picks, spreads, probs, local, weight) = refs[
        4 + sources : 13 + sources
    ]
    xs, produced, sems = refs[13 + sources :]
    e = pl.program_id(0)
    mine = local.shape[1]
    pairs, slots, pair_rows = picks.shape
    rows = pair_rows // 2
    experts = probs.shape[1]
    two = 2 * cap
    my_y, my_z = place[3], place[4]
    at_first = (my_y * pairs + my_z) * mine

    @pl.when(e == 0)
    def _():
        copies = stacked(tokens, xs, sems, rows + 16)
        for copy in copies:
            copy.start()
        for copy in copies:
            copy.wait()
        t_from = lax.broadcasted_iota(jnp.int32, (rows, rows), 0)
        t_to = lax.broadcasted_iota(jnp.int32, (rows, rows), 1)
        before = jnp.where(t_from < t_to, 1.0, 0.0).astype(BF)
        names = lax.broadcasted_iota(jnp.int32, (experts, pair_rows), 0)
        slot_down = lax.broadcasted_iota(jnp.int32, (two, pair_rows), 0).astype(F32)
        slot_across = lax.broadcasted_iota(jnp.int32, (pair_rows, slots), 1).astype(F32)

        @pl.loop(0, pairs, unroll=4)
        def _(p):
            halves = []
            for h in range(2):
                ext = xs[p, h, rows : rows + 16].astype(F32)
                wide = ext[0:8] + ext[8:16]
                halves.append(
                    jnp.concatenate(
                        [wide[:, rows * b : rows * b + rows] for b in range(experts // 8)], axis=0
                    )
                )
            all_probs = jnp.concatenate(halves, axis=1)
            probs[p] = all_probs
            own = [
                jnp.sum(jnp.where(names == at_first + j, all_probs, 0.0), axis=0, keepdims=True)
                for j in range(mine)
            ]
            own = jnp.concatenate(own + [jnp.zeros((8 - mine, pair_rows), F32)], axis=0)
            local[p] = own[0:mine]
            taken = jnp.where(own > 0.0, 1.0, 0.0)
            rank = jnp.concatenate(
                [
                    nn(taken[:, 0:rows].astype(BF), before),
                    nn(taken[:, rows:].astype(BF), before) + float(cap),
                ],
                axis=1,
            )
            slot = jnp.where(taken > 0.0, rank, -1000.0)
            here = pl.ds(pl.multiple_of(p * two, two), two)
            parts = []
            for j in range(mine):
                hit = slot_down == slot[j : j + 1, :]
                parts.append(jnp.where(hit, 1.0, 0.0))
                weight[j, here, :] = jnp.sum(
                    jnp.where(hit, own[j : j + 1, :], 0.0), axis=1, keepdims=True
                )
            pick = jnp.concatenate(parts, axis=0).astype(BF)
            picks[p] = pick
            slot_t = jnp.transpose(slot)
            spread = jnp.zeros((pair_rows, slots), F32)
            for j in range(mine):
                column = slot_t[:, j : j + 1]
                spread = jnp.where(
                    slot_across == column + float(j * two),
                    jnp.where(column >= 0.0, 1.0, 0.0),
                    spread,
                )
            spreads[p] = spread.astype(BF)
            both = jnp.concatenate([xs[p, 0, 0:rows], xs[p, 1, 0:rows]], axis=0)
            got = nn(pick, both).astype(BF)
            for j in range(mine):
                x_rows[j, here, :] = got[j * two : j * two + two]

    x = x_rows[e]
    pre_gate = nt(x, gate[0])
    pre_up = nt(x, up[0])
    pre_gates[0] = pre_gate
    pre_ups[0] = pre_up
    scaled = (pre_gate * jax.nn.sigmoid(pre_gate) * pre_up * weight[e]).astype(BF)
    made = nn(scaled, down[0]).astype(BF)
    at = pl.ds(pl.multiple_of(e * two, two), two)
    for p in range(pairs):
        produced[p, at, :] = made[p * two : p * two + two]

    @pl.when(e == mine - 1)
    def _():
        @pl.loop(0, pairs, unroll=4)
        def _(p):
            got = nn(spreads[p], produced[p]).astype(BF)
            to = lax.rem(my_z + p, pairs)
            mix[my_y * pairs + to] = got[0:rows]
            mix[(1 - my_y) * pairs + to] = got[rows:]


def backward_kernel(*refs, cap, sources, stacks):
    place, tokens = refs[0], refs[1 : 1 + sources]
    cotangents = refs[1 + sources : 1 + sources + stacks]
    base = 1 + sources + stacks
    (
        down,
        x_rows,
        pre_gates,
        pre_ups,
        picks,
        probs,
        local,
        weight,
        ours,
        theirs,
        router_part,
        gate_backs,
        up_backs,
        logit_grads,
    ) = refs[base : base + 14]
    xs, us, u_rows, grads, scores, down_kept, sems, end_sems = refs[base + 14 :]
    e = pl.program_id(0)
    mine = local.shape[1]
    pairs, slots, pair_rows = picks.shape
    rows = pair_rows // 2
    experts = probs.shape[1]
    two = 2 * cap
    px, py, pc, my_y, my_z = [place[i] for i in range(5)]
    at_first = (my_y * pairs + my_z) * mine

    def slot_of(d):
        x_off = lax.rem(d // 4 + 4 - px, 4)
        y_off = jnp.where(py == d // 2 % 2, 0, 1)
        return jnp.where(pc == d % 2, 0, 1), x_off * 2 + y_off

    def token_copies():
        return stacked(tokens, xs, sems, rows)

    @pl.when(e == 0)
    def _():
        copies = []
        for i in range(stacks):
            to = us.at[i] if i < pairs // 2 else us.at[i + 1]
            if i >= pairs - 1:
                to = us.at[pairs // 2, i - (pairs - 1)]
            copies.append(pltpu.make_async_copy(cotangents[i], to, sems.at[sources + i]))
        for copy in copies:
            copy.start()
        for copy in copies:
            copy.wait()
        for copy in token_copies():
            copy.start()

        @pl.loop(0, pairs, unroll=4)
        def _(p):
            here = pl.ds(pl.multiple_of(p * two, two), two)
            got = nn(picks[p], jnp.concatenate([us[p, 0], us[p, 1]], axis=0)).astype(BF)
            for j in range(mine):
                u_rows[j, here, :] = got[j * two : j * two + two]

    x = x_rows[0]
    u = u_rows[e]
    pre_gate = pre_gates[0]
    pre_up = pre_ups[0]
    raw = nt(u, down[0])
    g = weight[0]
    logistic = jax.nn.sigmoid(pre_gate)
    swished = pre_gate * logistic
    activated = swished * pre_up
    scores[e] = jnp.sum(activated * raw, axis=1, keepdims=True)
    act_grad = raw * g
    scaled = (activated * g).astype(BF)
    gate_back = (act_grad * pre_up * logistic * (1.0 + pre_gate * (1.0 - logistic))).astype(BF)
    up_back = (act_grad * swished).astype(BF)
    gate_backs[0] = gate_back
    up_backs[0] = up_back
    chunks = 2 * grads.shape[1]
    gate_grad = tn(gate_back, x)
    up_grad = tn(up_back, x)
    piece = gate_grad.shape[0] // chunks
    for d in range(chunks):
        cut = slice(d * piece, d * piece + piece)
        grads[*slot_of(d), pl.ds(pl.multiple_of(e * 2 * piece, 2 * piece), 2 * piece), :] = (
            jnp.concatenate([gate_grad[cut], up_grad[cut]], axis=0).astype(BF)
        )
    down_grad = tn(scaled, u)

    @pl.when(e % 2 == 0)
    def _():
        down_kept[...] = down_grad

    @pl.when(e % 2 == 1)
    def _():
        start = mine * 2 * piece + (e // 2) * 2 * piece
        for d in range(chunks):
            cut = slice(d * piece, d * piece + piece)
            grads[*slot_of(d), pl.ds(pl.multiple_of(start, 2 * piece), 2 * piece), :] = (
                jnp.concatenate([down_kept[cut], down_grad[cut]], axis=0).astype(BF)
            )

    @pl.when(e == mine - 1)
    def _():
        finals = (
            pltpu.make_async_copy(grads.at[0], ours, end_sems.at[0]),
            pltpu.make_async_copy(grads.at[1], theirs, end_sems.at[1]),
        )
        for copy in finals:
            copy.start()
        for copy in token_copies():
            copy.wait()
        names = lax.broadcasted_iota(jnp.int32, (experts, pair_rows), 0)
        router_part[...] = jnp.zeros_like(router_part)

        @pl.loop(0, pairs, unroll=4)
        def _(p):
            pick = picks[p].astype(F32)
            own = local[p]
            total = jnp.zeros((1, pair_rows), F32)
            placed = jnp.zeros((experts, pair_rows), F32)
            for j in range(mine):
                score = scores[j, pl.ds(pl.multiple_of(p * two, two), two), :]
                grad = own[j : j + 1] * jnp.sum(
                    pick[j * two : j * two + two] * score, axis=0, keepdims=True
                )
                total = total + grad
                placed = jnp.where(names == at_first + j, grad, placed)
            logit_grad = placed - probs[p] * total
            high = logit_grad.astype(BF)
            logit_grads[p] = high
            low = (logit_grad - high.astype(F32)).astype(BF)
            here = jnp.concatenate([xs[p, 0], xs[p, 1]], axis=0)
            both = nn(jnp.concatenate([high, low], axis=0), here)
            router_part[...] += both[0:experts] + both[experts:]

        for copy in finals:
            copy.wait()


def input_kernel(gate_backs, up_backs, gate, up, router, spreads, logit_grads, *rest, cap):
    outs, row_grads = rest[:-1], rest[-1]
    e = pl.program_id(0)
    pairs, pair_rows, _ = spreads.shape
    rows, two = pair_rows // 2, 2 * cap
    back = (nn(gate_backs[0], gate[0]) + nn(up_backs[0], up[0])).astype(BF)
    at = pl.ds(pl.multiple_of(e * two, two), two)
    for p in range(pairs):
        row_grads[p, at, :] = back[p * two : p * two + two]

    @pl.when(e == pl.num_programs(0) - 1)
    def _():
        for p in range(pairs):
            got = (nn(spreads[p], row_grads[p]) + tn(logit_grads[p], router[...])).astype(BF)
            for h in range(2):
                half = got[h * rows : h * rows + rows]
                if p == pairs // 2:
                    outs[pairs - 1 + h][...] = half
                else:
                    outs[p if p < pairs // 2 else p - 1][h] = half


WHOLE = functools.partial(pl.BlockSpec, pipeline_mode=pl.Buffered(1))
ANYWHERE = pl.BlockSpec(memory_space=pl.ANY)


def whole(*shape):
    return WHOLE(shape, lambda e: (0,) * len(shape))


def each(*shape):
    return pl.BlockSpec((1, *shape), lambda e: (e, 0, 0))


def run_forward(place, tokens, gate, up, down, cap, experts):
    rows, width = tokens[-1].shape
    rows = rows - 16
    mine, hidden, _ = gate.shape
    sources, pairs = len(tokens), len(tokens) // 2
    slots, total = 2 * mine * cap, 2 * pairs * cap
    shapes = (
        ((2 * pairs, rows, width), BF),
        ((mine, total, width), BF),
        ((mine, total, hidden), F32),
        ((mine, total, hidden), F32),
        ((pairs, slots, 2 * rows), BF),
        ((pairs, 2 * rows, slots), BF),
        ((pairs, experts, 2 * rows), F32),
        ((pairs, mine, 2 * rows), F32),
        ((mine, total, 1), F32),
    )
    specs = [whole(*shape) for shape, _ in shapes]
    specs[2] = specs[3] = each(total, hidden)
    return pl.pallas_call(
        functools.partial(forward_kernel, cap=cap, sources=sources),
        grid=(mine,),
        out_shape=tuple(jax.ShapeDtypeStruct(*one) for one in shapes),
        in_specs=[
            pl.BlockSpec(memory_space=pltpu.SMEM),
            *([ANYWHERE] * sources),
            *([each(hidden, width)] * 3),
        ],
        out_specs=tuple(specs),
        scratch_shapes=[
            pltpu.VMEM((pairs, 2, rows + 16, width), BF),
            pltpu.VMEM((pairs, slots, width), BF),
            pltpu.SemaphoreType.DMA((sources,)),
        ],
        compiler_params=pltpu.CompilerParams(vmem_limit_bytes=60 * 2**20),
        cost_estimate=pl.CostEstimate(
            flops=6 * 10**9, bytes_accessed=24 * 2**20, transcendentals=10**6
        ),
    )(place, *tokens, gate, up, down)


def run_backward(place, tokens, cotangents, down, kept, cap, chunks):
    x_rows, pre_gates, pre_ups, picks, probs, local, weight = kept
    rows, width = cotangents[-1].shape
    stacks = len(cotangents)
    mine, hidden, _ = down.shape
    sources, pairs = len(tokens), len(tokens) // 2
    slots, total = 2 * mine * cap, 2 * pairs * cap
    experts = probs.shape[1]
    grad_rows = 3 * mine * hidden // chunks
    return pl.pallas_call(
        functools.partial(backward_kernel, cap=cap, sources=sources, stacks=stacks),
        grid=(mine,),
        out_shape=(
            jax.ShapeDtypeStruct((chunks // 2, grad_rows, width), BF),
            jax.ShapeDtypeStruct((chunks // 2, grad_rows, width), BF),
            jax.ShapeDtypeStruct((experts, width), F32),
            jax.ShapeDtypeStruct((mine, total, hidden), BF),
            jax.ShapeDtypeStruct((mine, total, hidden), BF),
            jax.ShapeDtypeStruct((pairs, experts, 2 * rows), BF),
        ),
        in_specs=[
            pl.BlockSpec(memory_space=pltpu.SMEM),
            *([ANYWHERE] * (sources + stacks)),
            each(hidden, width),
            each(total, width),
            each(total, hidden),
            each(total, hidden),
            whole(pairs, slots, 2 * rows),
            whole(pairs, experts, 2 * rows),
            whole(pairs, mine, 2 * rows),
            each(total, 1),
        ],
        out_specs=(
            ANYWHERE,
            ANYWHERE,
            whole(experts, width),
            each(total, hidden),
            each(total, hidden),
            whole(pairs, experts, 2 * rows),
        ),
        scratch_shapes=[
            pltpu.VMEM((pairs, 2, rows, width), BF),
            pltpu.VMEM((pairs, 2, rows, width), BF),
            pltpu.VMEM((mine, total, width), BF),
            pltpu.VMEM((2, chunks // 2, grad_rows, width), BF),
            pltpu.VMEM((mine, total, 1), F32),
            pltpu.VMEM((hidden, width), F32),
            pltpu.SemaphoreType.DMA((sources + stacks,)),
            pltpu.SemaphoreType.DMA((2,)),
        ],
        compiler_params=pltpu.CompilerParams(vmem_limit_bytes=60 * 2**20),
        cost_estimate=pl.CostEstimate(
            flops=8 * 10**9, bytes_accessed=40 * 2**20, transcendentals=10**6
        ),
    )(place, *tokens, *cotangents, down, x_rows, pre_gates, pre_ups, picks, probs, local, weight)


def run_input(gate_backs, up_backs, gate, up, router, spreads, logit_grads, cap):
    mine, total, hidden = gate_backs.shape
    experts, width = router.shape
    pairs, pair_rows, slots = spreads.shape
    rows = pair_rows // 2
    shapes = [(2, rows, width)] * (pairs - 1) + [(rows, width)] * 2
    return pl.pallas_call(
        functools.partial(input_kernel, cap=cap),
        grid=(mine,),
        out_shape=tuple(jax.ShapeDtypeStruct(shape, BF) for shape in shapes),
        in_specs=[
            each(total, hidden),
            each(total, hidden),
            each(hidden, width),
            each(hidden, width),
            whole(experts, width),
            whole(pairs, pair_rows, slots),
            whole(pairs, experts, pair_rows),
        ],
        out_specs=tuple(whole(*shape) for shape in shapes),
        scratch_shapes=[pltpu.VMEM((pairs, slots, width), BF)],
        compiler_params=pltpu.CompilerParams(vmem_limit_bytes=60 * 2**20),
        cost_estimate=pl.CostEstimate(
            flops=5 * 10**9, bytes_accessed=20 * 2**20, transcendentals=0
        ),
    )(gate_backs, up_backs, gate, up, router, spreads, logit_grads)


def swap(value, axis, step):
    size = lax.axis_size(axis)
    return lax.ppermute(value, axis, [(i, i ^ step) for i in range(size)])


def shift(value, axis, step):
    size = lax.axis_size(axis)
    return lax.ppermute(value, axis, [(i, (i + step) % size) for i in range(size)])


def after(value, *others):
    return lax.optimization_barrier((value, *others))[0]


def gather_group(block, other):
    hold = lax.optimization_barrier
    both = jnp.stack([other, swap(other, "yl", 1)])
    near, far = {0: block}, {0: swap(block, "yl", 1)}

    def cross(*distances):
        for k in distances:
            far[k] = swap(near[k], "yl", 1)

    near[7], near[1] = shift(block, "z", 1), shift(block, "z", -1)
    right, left, both = hold((near[7], near[1], both))
    near[6], near[2] = shift(right, "z", 1), shift(left, "z", -1)
    cross(1, 7)
    right, left, far[0] = hold((near[6], near[2], far[0]))
    near[5], near[3] = shift(right, "z", 1), shift(left, "z", -1)
    cross(2, 6)
    right, far[1] = hold((near[5], far[1]))
    near[4] = shift(right, "z", 1)
    cross(3, 5, 4)
    both, near[4], far[7] = hold((both, near[4], far[7]))
    found = {0: both}
    right, left = shift(both, "z", 1), shift(both, "z", -1)
    right, left, far[2], far[6] = hold((right, left, far[2], far[6]))
    found[7], found[1] = right, left
    right, left = shift(right, "z", 1), shift(left, "z", -1)
    right, left, far[3], far[5] = hold((right, left, far[3], far[5]))
    found[6], found[2] = right, left
    right, left = shift(right, "z", 1), shift(left, "z", -1)
    right, left, far[4] = hold((right, left, far[4]))
    found[5], found[3] = right, left
    last = [shift(right[0], "z", 1), shift(left[1], "z", -1)]
    blocks = [near[i] for i in range(8)] + [far[i] for i in range(8)]
    return blocks, [found[i] for i in (0, 1, 2, 3, 5, 6, 7)] + last


def added(*terms):
    total = terms[0].astype(F32)
    for term in terms[1:]:
        total = total + term.astype(F32)
    return total


def reduce_all(outs, mixture, ours, theirs, router_part):
    part, lows = router_part, []

    def halve(part, axis, step):
        low = lax.axis_index(axis) & step == 0
        half = part.shape[0] // 2
        away = jnp.where(low, part[half:], part[:half])
        lows.append((low, axis, step))
        return jnp.where(low, part[:half], part[half:]) + swap(away, axis, step)

    parts = dict(zip((0, 1, 2, 3, 5, 6, 7), outs))
    part = after(halve(part, "core", 1), outs[7])
    part = halve(part, "x", 1)
    part = halve(part, "x", 2)
    right, left = shift(outs[7], "z", 1), shift(outs[8], "z", -1)
    held = added(ours, swap(theirs, "core", 1)).astype(BF)
    held = after(held, part)
    held = held.reshape(4, 2, *held.shape[1:])
    up = shift(held[2, 0], "x", 1)
    down = shift(held[2, 1], "x", -1)
    right = added(parts[3], jnp.stack([right, jnp.zeros_like(right)])).astype(BF)
    left = added(parts[5], jnp.stack([jnp.zeros_like(left), left])).astype(BF)
    right, left = shift(right, "z", 1), shift(left, "z", -1)
    part = halve(part, "yh", 1)
    part = part + swap(part, "yl", 1)
    up = jnp.stack([added(held[1, 0], up).astype(BF), held[1, 1]])
    down = jnp.stack([held[3, 0], added(held[3, 1], down).astype(BF)])
    up, down, part = lax.optimization_barrier((up, down, part))
    up, down = shift(up, "x", 1), shift(down, "x", -1)
    right, left = added(parts[2], right).astype(BF), added(parts[6], left).astype(BF)
    part = part + swap(part, "z", 1)
    right, left, part, mixture = lax.optimization_barrier((right, left, part, mixture))
    right, left = shift(right, "z", 1), shift(left, "z", -1)
    part = part + swap(part, "z", 2)
    part = part + swap(part, "z", 4)
    right, left = added(parts[1], right).astype(BF), added(parts[7], left).astype(BF)
    right, left = shift(right, "z", 1), shift(left, "z", -1)
    away = added(held[0, 1], up[1], down[1]).astype(BF)
    away, part = lax.optimization_barrier((away, part))
    away = swap(away, "yh", 1)
    for low, axis, step in reversed(lows):
        other = swap(part, axis, step)
        part = jnp.where(low, jnp.concatenate([part, other]), jnp.concatenate([other, part]))
        if axis == "yh":
            part, away = lax.optimization_barrier((part, away))
        elif axis == "x" and step == 2:
            part, right, left = lax.optimization_barrier((part, right, left))
    total = added(held[0, 0], up[0], down[0], away)
    away = swap(added(parts[0][1], right[1], left[1]).astype(BF), "yl", 1)
    input_grad = added(parts[0][0], right[0], left[0], away).astype(BF)
    return mixture, input_grad, total, part


def body(tokens, expert_ids, upstream, router_weight, gate_matrix, up_matrix, down_matrix):
    rows, width = tokens.shape
    top = expert_ids.shape[1]
    mine, hidden, _ = gate_matrix.shape
    peers = lax.axis_size(EXPERT)
    groups = lax.axis_size(DP)
    experts = peers * mine
    cap = rows * top * 3 // (2 * experts)
    router = router_weight.T
    packed = pl.pallas_call(
        pack_kernel,
        out_shape=jax.ShapeDtypeStruct((rows + 16, width), BF),
    )(tokens, expert_ids.T, router)
    blocks, cotangents = gather_group(packed, upstream)
    place = jnp.stack([lax.axis_index(axis) for axis in ALL]).astype(jnp.int32)
    mix, *kept = run_forward(place, blocks, gate_matrix, up_matrix, down_matrix, cap, experts)
    spreads = kept.pop(4)
    mixture = lax.psum_scatter(mix, EXPERT, scatter_dimension=0, tiled=False)
    ours, theirs, router_part, gate_backs, up_backs, logit_grads = run_backward(
        place, blocks, cotangents, down_matrix, kept, cap, groups
    )
    outs = run_input(
        gate_backs, up_backs, gate_matrix, up_matrix, router, spreads, logit_grads, cap
    )
    mixture, input_grad, total, router_grad = reduce_all(
        outs, mixture, ours, theirs, router_part
    )
    piece = hidden // groups
    both = total[0 : 2 * mine * piece].reshape(mine, 2, piece, width)
    down_grad = total[2 * mine * piece :].reshape(mine, piece, width)
    return mixture, input_grad, router_grad.T, both[:, 0], both[:, 1], down_grad


def solution(mesh):
    shape = {"x": 4, "yh": 2, "core": 2, "yl": 2, "z": 8}
    fine = jax.sharding.Mesh(mesh.devices.reshape(tuple(shape.values())), tuple(shape))
    in_specs = (
        P(ALL, None),
        P(ALL, None),
        P(ALL, None),
        P(),
        P(EXPERT, None, None),
        P(EXPERT, None, None),
        P(EXPERT, None, None),
    )
    out_specs = (
        P(ALL, None),
        P(ALL, None),
        P(),
        P(EXPERT, DP, None),
        P(EXPERT, DP, None),
        P(EXPERT, DP, None),
    )
    return jax.shard_map(body, mesh=fine, in_specs=in_specs, out_specs=out_specs, check_vma=False)
```

```python
import functools

import jax
import jax.numpy as jnp
from jax import lax
from jax.experimental import pallas as pl
from jax.experimental.pallas import tpu as pltpu
from jax.sharding import PartitionSpec as P

BF = jnp.bfloat16
F32 = jnp.float32
EXPERT = ("yl", "z")
DP = ("x", "yh", "core")
ALL = DP + EXPERT


def nt(a, b):
    return lax.dot_general(a, b, (((1,), (1,)), ((), ())), preferred_element_type=F32)


def tn(a, b):
    return lax.dot_general(a, b, (((0,), (0,)), ((), ())), preferred_element_type=F32)


def nn(a, b):
    return jnp.dot(a, b, preferred_element_type=F32)


def pack_kernel(tokens, ids, router, packed):
    rows = tokens.shape[0]
    experts = router.shape[0]
    packed[0:rows] = tokens[...]
    logits = nt(router[...], tokens[...])
    names = lax.broadcasted_iota(jnp.int32, (experts, rows), 0)
    chosen = names == ids[0:1, :]
    for k in range(1, ids.shape[0]):
        chosen = chosen | (names == ids[k : k + 1, :])
    raised = jnp.where(chosen, jnp.exp(logits), 0.0)
    probs = raised / jnp.sum(raised, axis=0, keepdims=True)
    wide = jnp.concatenate([probs[8 * b : 8 * b + 8, :] for b in range(experts // 8)], axis=1)
    high = wide.astype(BF).astype(F32)
    packed[rows : rows + 16] = jnp.concatenate([high, wide - high], axis=0).astype(BF)


def stacked(tokens, held, sems, rows):
    pairs = held.shape[0]
    return [
        pltpu.make_async_copy(
            block.at[pl.ds(0, rows)], held.at[i % pairs, i // pairs], sems.at[i]
        )
        for i, block in enumerate(tokens)
    ]


def forward_kernel(*refs, cap, sources):
    place, tokens = refs[0], refs[1 : 1 + sources]
    gate, up, down = refs[1 + sources : 4 + sources]
    (mix, x_rows, pre_gates, pre_ups, picks, spreads, probs, local, weight) = refs[
        4 + sources : 13 + sources
    ]
    xs, produced, sems = refs[13 + sources :]
    e = pl.program_id(0)
    mine = local.shape[1]
    pairs, slots, pair_rows = picks.shape
    rows = pair_rows // 2
    experts = probs.shape[1]
    two = 2 * cap
    my_y, my_z = place[3], place[4]
    at_first = (my_y * pairs + my_z) * mine

    @pl.when(e == 0)
    def _():
        copies = stacked(tokens, xs, sems, rows + 16)
        for copy in copies:
            copy.start()
        for copy in copies:
            copy.wait()
        t_from = lax.broadcasted_iota(jnp.int32, (rows, rows), 0)
        t_to = lax.broadcasted_iota(jnp.int32, (rows, rows), 1)
        before = jnp.where(t_from < t_to, 1.0, 0.0).astype(BF)
        names = lax.broadcasted_iota(jnp.int32, (experts, pair_rows), 0)
        slot_down = lax.broadcasted_iota(jnp.int32, (two, pair_rows), 0).astype(F32)
        slot_across = lax.broadcasted_iota(jnp.int32, (pair_rows, slots), 1).astype(F32)

        @pl.loop(0, pairs, unroll=4)
        def _(p):
            halves = []
            for h in range(2):
                ext = xs[p, h, rows : rows + 16].astype(F32)
                wide = ext[0:8] + ext[8:16]
                halves.append(
                    jnp.concatenate(
                        [wide[:, rows * b : rows * b + rows] for b in range(experts // 8)], axis=0
                    )
                )
            all_probs = jnp.concatenate(halves, axis=1)
            probs[p] = all_probs
            own = [
                jnp.sum(jnp.where(names == at_first + j, all_probs, 0.0), axis=0, keepdims=True)
                for j in range(mine)
            ]
            own = jnp.concatenate(own + [jnp.zeros((8 - mine, pair_rows), F32)], axis=0)
            local[p] = own[0:mine]
            taken = jnp.where(own > 0.0, 1.0, 0.0)
            rank = jnp.concatenate(
                [
                    nn(taken[:, 0:rows].astype(BF), before),
                    nn(taken[:, rows:].astype(BF), before) + float(cap),
                ],
                axis=1,
            )
            slot = jnp.where(taken > 0.0, rank, -1000.0)
            here = pl.ds(pl.multiple_of(p * two, two), two)
            parts = []
            for j in range(mine):
                hit = slot_down == slot[j : j + 1, :]
                parts.append(jnp.where(hit, 1.0, 0.0))
                weight[j, here, :] = jnp.sum(
                    jnp.where(hit, own[j : j + 1, :], 0.0), axis=1, keepdims=True
                )
            pick = jnp.concatenate(parts, axis=0).astype(BF)
            picks[p] = pick
            slot_t = jnp.transpose(slot)
            spread = jnp.zeros((pair_rows, slots), F32)
            for j in range(mine):
                column = slot_t[:, j : j + 1]
                spread = jnp.where(
                    slot_across == column + float(j * two),
                    jnp.where(column >= 0.0, 1.0, 0.0),
                    spread,
                )
            spreads[p] = spread.astype(BF)
            both = jnp.concatenate([xs[p, 0, 0:rows], xs[p, 1, 0:rows]], axis=0)
            got = nn(pick, both).astype(BF)
            for j in range(mine):
                x_rows[j, here, :] = got[j * two : j * two + two]

    x = x_rows[e]
    pre_gate = nt(x, gate[0])
    pre_up = nt(x, up[0])
    pre_gates[0] = pre_gate
    pre_ups[0] = pre_up
    scaled = (pre_gate * jax.nn.sigmoid(pre_gate) * pre_up * weight[e]).astype(BF)
    made = nn(scaled, down[0]).astype(BF)
    at = pl.ds(pl.multiple_of(e * two, two), two)
    for p in range(pairs):
        produced[p, at, :] = made[p * two : p * two + two]

    @pl.when(e == mine - 1)
    def _():
        @pl.loop(0, pairs, unroll=4)
        def _(p):
            got = nn(spreads[p], produced[p]).astype(BF)
            to = lax.rem(my_z + p, pairs)
            mix[my_y * pairs + to] = got[0:rows]
            mix[(1 - my_y) * pairs + to] = got[rows:]


def backward_kernel(*refs, cap, sources, stacks):
    place, tokens = refs[0], refs[1 : 1 + sources]
    cotangents = refs[1 + sources : 1 + sources + stacks]
    base = 1 + sources + stacks
    (
        down,
        x_rows,
        pre_gates,
        pre_ups,
        picks,
        probs,
        local,
        weight,
        ours,
        theirs,
        router_part,
        gate_backs,
        up_backs,
        logit_grads,
    ) = refs[base : base + 14]
    xs, us, u_rows, grads, scores, down_kept, sems, end_sems = refs[base + 14 :]
    e = pl.program_id(0)
    mine = local.shape[1]
    pairs, slots, pair_rows = picks.shape
    rows = pair_rows // 2
    experts = probs.shape[1]
    two = 2 * cap
    px, py, pc, my_y, my_z = [place[i] for i in range(5)]
    at_first = (my_y * pairs + my_z) * mine

    def slot_of(d):
        x_off = lax.rem(d // 4 + 4 - px, 4)
        y_off = jnp.where(py == d // 2 % 2, 0, 1)
        return jnp.where(pc == d % 2, 0, 1), x_off * 2 + y_off

    def token_copies():
        return stacked(tokens, xs, sems, rows)

    @pl.when(e == 0)
    def _():
        copies = []
        for i in range(stacks):
            to = us.at[i] if i < pairs // 2 else us.at[i + 1]
            if i >= pairs - 1:
                to = us.at[pairs // 2, i - (pairs - 1)]
            copies.append(pltpu.make_async_copy(cotangents[i], to, sems.at[sources + i]))
        for copy in copies:
            copy.start()
        for copy in copies:
            copy.wait()
        for copy in token_copies():
            copy.start()

        @pl.loop(0, pairs, unroll=4)
        def _(p):
            here = pl.ds(pl.multiple_of(p * two, two), two)
            got = nn(picks[p], jnp.concatenate([us[p, 0], us[p, 1]], axis=0)).astype(BF)
            for j in range(mine):
                u_rows[j, here, :] = got[j * two : j * two + two]

    x = x_rows[0]
    u = u_rows[e]
    pre_gate = pre_gates[0]
    pre_up = pre_ups[0]
    raw = nt(u, down[0])
    g = weight[0]
    logistic = jax.nn.sigmoid(pre_gate)
    swished = pre_gate * logistic
    activated = swished * pre_up
    scores[e] = jnp.sum(activated * raw, axis=1, keepdims=True)
    act_grad = raw * g
    scaled = (activated * g).astype(BF)
    gate_back = (act_grad * pre_up * logistic * (1.0 + pre_gate * (1.0 - logistic))).astype(BF)
    up_back = (act_grad * swished).astype(BF)
    gate_backs[0] = gate_back
    up_backs[0] = up_back
    chunks = 2 * grads.shape[1]
    gate_grad = tn(gate_back, x)
    up_grad = tn(up_back, x)
    piece = gate_grad.shape[0] // chunks
    for d in range(chunks):
        cut = slice(d * piece, d * piece + piece)
        grads[*slot_of(d), pl.ds(pl.multiple_of(e * 2 * piece, 2 * piece), 2 * piece), :] = (
            jnp.concatenate([gate_grad[cut], up_grad[cut]], axis=0).astype(BF)
        )
    down_grad = tn(scaled, u)

    @pl.when(e % 2 == 0)
    def _():
        down_kept[...] = down_grad

    @pl.when(e % 2 == 1)
    def _():
        start = mine * 2 * piece + (e // 2) * 2 * piece
        for d in range(chunks):
            cut = slice(d * piece, d * piece + piece)
            grads[*slot_of(d), pl.ds(pl.multiple_of(start, 2 * piece), 2 * piece), :] = (
                jnp.concatenate([down_kept[cut], down_grad[cut]], axis=0).astype(BF)
            )

    @pl.when(e == mine - 1)
    def _():
        finals = (
            pltpu.make_async_copy(grads.at[0], ours, end_sems.at[0]),
            pltpu.make_async_copy(grads.at[1], theirs, end_sems.at[1]),
        )
        for copy in finals:
            copy.start()
        for copy in token_copies():
            copy.wait()
        names = lax.broadcasted_iota(jnp.int32, (experts, pair_rows), 0)
        router_part[...] = jnp.zeros_like(router_part)

        @pl.loop(0, pairs, unroll=4)
        def _(p):
            pick = picks[p].astype(F32)
            own = local[p]
            total = jnp.zeros((1, pair_rows), F32)
            placed = jnp.zeros((experts, pair_rows), F32)
            for j in range(mine):
                score = scores[j, pl.ds(pl.multiple_of(p * two, two), two), :]
                grad = own[j : j + 1] * jnp.sum(
                    pick[j * two : j * two + two] * score, axis=0, keepdims=True
                )
                total = total + grad
                placed = jnp.where(names == at_first + j, grad, placed)
            logit_grad = placed - probs[p] * total
            high = logit_grad.astype(BF)
            logit_grads[p] = high
            low = (logit_grad - high.astype(F32)).astype(BF)
            here = jnp.concatenate([xs[p, 0], xs[p, 1]], axis=0)
            both = nn(jnp.concatenate([high, low], axis=0), here)
            router_part[...] += both[0:experts] + both[experts:]

        for copy in finals:
            copy.wait()


def input_kernel(gate_backs, up_backs, gate, up, router, spreads, logit_grads, *rest, cap):
    outs, row_grads = rest[:-1], rest[-1]
    e = pl.program_id(0)
    pairs, pair_rows, _ = spreads.shape
    rows, two = pair_rows // 2, 2 * cap
    back = (nn(gate_backs[0], gate[0]) + nn(up_backs[0], up[0])).astype(BF)
    at = pl.ds(pl.multiple_of(e * two, two), two)
    for p in range(pairs):
        row_grads[p, at, :] = back[p * two : p * two + two]

    @pl.when(e == pl.num_programs(0) - 1)
    def _():
        for p in range(pairs):
            got = (nn(spreads[p], row_grads[p]) + tn(logit_grads[p], router[...])).astype(BF)
            for h in range(2):
                half = got[h * rows : h * rows + rows]
                if p == pairs // 2:
                    outs[pairs - 1 + h][...] = half
                else:
                    outs[p if p < pairs // 2 else p - 1][h] = half


WHOLE = functools.partial(pl.BlockSpec, pipeline_mode=pl.Buffered(1))
ANYWHERE = pl.BlockSpec(memory_space=pl.ANY)


def whole(*shape):
    return WHOLE(shape, lambda e: (0,) * len(shape))


def each(*shape):
    return pl.BlockSpec((1, *shape), lambda e: (e, 0, 0))


def run_forward(place, tokens, gate, up, down, cap, experts):
    rows, width = tokens[-1].shape
    rows = rows - 16
    mine, hidden, _ = gate.shape
    sources, pairs = len(tokens), len(tokens) // 2
    slots, total = 2 * mine * cap, 2 * pairs * cap
    shapes = (
        ((2 * pairs, rows, width), BF),
        ((mine, total, width), BF),
        ((mine, total, hidden), F32),
        ((mine, total, hidden), F32),
        ((pairs, slots, 2 * rows), BF),
        ((pairs, 2 * rows, slots), BF),
        ((pairs, experts, 2 * rows), F32),
        ((pairs, mine, 2 * rows), F32),
        ((mine, total, 1), F32),
    )
    specs = [whole(*shape) for shape, _ in shapes]
    specs[2] = specs[3] = each(total, hidden)
    return pl.pallas_call(
        functools.partial(forward_kernel, cap=cap, sources=sources),
        grid=(mine,),
        out_shape=tuple(jax.ShapeDtypeStruct(*one) for one in shapes),
        in_specs=[
            pl.BlockSpec(memory_space=pltpu.SMEM),
            *([ANYWHERE] * sources),
            *([each(hidden, width)] * 3),
        ],
        out_specs=tuple(specs),
        scratch_shapes=[
            pltpu.VMEM((pairs, 2, rows + 16, width), BF),
            pltpu.VMEM((pairs, slots, width), BF),
            pltpu.SemaphoreType.DMA((sources,)),
        ],
        compiler_params=pltpu.CompilerParams(vmem_limit_bytes=60 * 2**20),
        cost_estimate=pl.CostEstimate(
            flops=6 * 10**9, bytes_accessed=24 * 2**20, transcendentals=10**6
        ),
    )(place, *tokens, gate, up, down)


def run_backward(place, tokens, cotangents, down, kept, cap, chunks):
    x_rows, pre_gates, pre_ups, picks, probs, local, weight = kept
    rows, width = cotangents[-1].shape
    stacks = len(cotangents)
    mine, hidden, _ = down.shape
    sources, pairs = len(tokens), len(tokens) // 2
    slots, total = 2 * mine * cap, 2 * pairs * cap
    experts = probs.shape[1]
    grad_rows = 3 * mine * hidden // chunks
    return pl.pallas_call(
        functools.partial(backward_kernel, cap=cap, sources=sources, stacks=stacks),
        grid=(mine,),
        out_shape=(
            jax.ShapeDtypeStruct((chunks // 2, grad_rows, width), BF),
            jax.ShapeDtypeStruct((chunks // 2, grad_rows, width), BF),
            jax.ShapeDtypeStruct((experts, width), F32),
            jax.ShapeDtypeStruct((mine, total, hidden), BF),
            jax.ShapeDtypeStruct((mine, total, hidden), BF),
            jax.ShapeDtypeStruct((pairs, experts, 2 * rows), BF),
        ),
        in_specs=[
            pl.BlockSpec(memory_space=pltpu.SMEM),
            *([ANYWHERE] * (sources + stacks)),
            each(hidden, width),
            each(total, width),
            each(total, hidden),
            each(total, hidden),
            whole(pairs, slots, 2 * rows),
            whole(pairs, experts, 2 * rows),
            whole(pairs, mine, 2 * rows),
            each(total, 1),
        ],
        out_specs=(
            ANYWHERE,
            ANYWHERE,
            whole(experts, width),
            each(total, hidden),
            each(total, hidden),
            whole(pairs, experts, 2 * rows),
        ),
        scratch_shapes=[
            pltpu.VMEM((pairs, 2, rows, width), BF),
            pltpu.VMEM((pairs, 2, rows, width), BF),
            pltpu.VMEM((mine, total, width), BF),
            pltpu.VMEM((2, chunks // 2, grad_rows, width), BF),
            pltpu.VMEM((mine, total, 1), F32),
            pltpu.VMEM((hidden, width), F32),
            pltpu.SemaphoreType.DMA((sources + stacks,)),
            pltpu.SemaphoreType.DMA((2,)),
        ],
        compiler_params=pltpu.CompilerParams(vmem_limit_bytes=60 * 2**20),
        cost_estimate=pl.CostEstimate(
            flops=8 * 10**9, bytes_accessed=40 * 2**20, transcendentals=10**6
        ),
    )(place, *tokens, *cotangents, down, x_rows, pre_gates, pre_ups, picks, probs, local, weight)


def run_input(gate_backs, up_backs, gate, up, router, spreads, logit_grads, cap):
    mine, total, hidden = gate_backs.shape
    experts, width = router.shape
    pairs, pair_rows, slots = spreads.shape
    rows = pair_rows // 2
    shapes = [(2, rows, width)] * (pairs - 1) + [(rows, width)] * 2
    return pl.pallas_call(
        functools.partial(input_kernel, cap=cap),
        grid=(mine,),
        out_shape=tuple(jax.ShapeDtypeStruct(shape, BF) for shape in shapes),
        in_specs=[
            each(total, hidden),
            each(total, hidden),
            each(hidden, width),
            each(hidden, width),
            whole(experts, width),
            whole(pairs, pair_rows, slots),
            whole(pairs, experts, pair_rows),
        ],
        out_specs=tuple(whole(*shape) for shape in shapes),
        scratch_shapes=[pltpu.VMEM((pairs, slots, width), BF)],
        compiler_params=pltpu.CompilerParams(vmem_limit_bytes=60 * 2**20),
        cost_estimate=pl.CostEstimate(
            flops=5 * 10**9, bytes_accessed=20 * 2**20, transcendentals=0
        ),
    )(gate_backs, up_backs, gate, up, router, spreads, logit_grads)


def swap(value, axis, step):
    size = lax.axis_size(axis)
    return lax.ppermute(value, axis, [(i, i ^ step) for i in range(size)])


def shift(value, axis, step):
    size = lax.axis_size(axis)
    return lax.ppermute(value, axis, [(i, (i + step) % size) for i in range(size)])


def after(value, *others):
    return lax.optimization_barrier((value, *others))[0]


def gather_group(block, other):
    hold = lax.optimization_barrier
    both = jnp.stack([other, swap(other, "yl", 1)])
    near, far = {0: block}, {0: swap(block, "yl", 1)}

    def cross(*distances):
        for k in distances:
            far[k] = swap(near[k], "yl", 1)

    near[7], near[1] = shift(block, "z", 1), shift(block, "z", -1)
    right, left, both = hold((near[7], near[1], both))
    near[6], near[2] = shift(right, "z", 1), shift(left, "z", -1)
    cross(1, 7)
    right, left, far[0] = hold((near[6], near[2], far[0]))
    near[5], near[3] = shift(right, "z", 1), shift(left, "z", -1)
    cross(2, 6)
    right, far[1] = hold((near[5], far[1]))
    near[4] = shift(right, "z", 1)
    cross(3, 5)
    both, near[5], near[3], far[7] = hold((both, near[5], near[3], far[7]))
    found = {0: both}
    right, left = shift(both, "z", 1), shift(both, "z", -1)
    right, left, far[2], far[6], near[4] = hold((right, left, far[2], far[6], near[4]))
    found[7], found[1] = right, left
    cross(4)
    right, left = shift(right, "z", 1), shift(left, "z", -1)
    right, left, far[3], far[5] = hold((right, left, far[3], far[5]))
    found[6], found[2] = right, left
    right, left = shift(right, "z", 1), shift(left, "z", -1)
    right, left, far[4] = hold((right, left, far[4]))
    found[5], found[3] = right, left
    last = [shift(right[0], "z", 1), shift(left[1], "z", -1)]
    blocks = [near[i] for i in range(8)] + [far[i] for i in range(8)]
    return blocks, [found[i] for i in (0, 1, 2, 3, 5, 6, 7)] + last


def added(*terms):
    total = terms[0].astype(F32)
    for term in terms[1:]:
        total = total + term.astype(F32)
    return total


def reduce_all(outs, mixture, ours, theirs, router_part):
    part, lows = router_part, []

    def halve(part, axis, step):
        low = lax.axis_index(axis) & step == 0
        half = part.shape[0] // 2
        away = jnp.where(low, part[half:], part[:half])
        lows.append((low, axis, step))
        return jnp.where(low, part[:half], part[half:]) + swap(away, axis, step)

    parts = dict(zip((0, 1, 2, 3, 5, 6, 7), outs))
    part = after(halve(part, "core", 1), outs[7])
    part = halve(part, "x", 1)
    part = halve(part, "x", 2)
    right, left = shift(outs[7], "z", 1), shift(outs[8], "z", -1)
    held = added(ours, swap(theirs, "core", 1)).astype(BF)
    held = after(held, part)
    held = held.reshape(4, 2, *held.shape[1:])
    up = shift(held[2, 0], "x", 1)
    down = shift(held[2, 1], "x", -1)
    right = added(parts[3], jnp.stack([right, jnp.zeros_like(right)])).astype(BF)
    left = added(parts[5], jnp.stack([jnp.zeros_like(left), left])).astype(BF)
    right, left = shift(right, "z", 1), shift(left, "z", -1)
    part = halve(part, "yh", 1)
    part = part + swap(part, "yl", 1)
    up = jnp.stack([added(held[1, 0], up).astype(BF), held[1, 1]])
    down = jnp.stack([held[3, 0], added(held[3, 1], down).astype(BF)])
    up, down, part = lax.optimization_barrier((up, down, part))
    up, down = shift(up, "x", 1), shift(down, "x", -1)
    right, left = added(parts[2], right).astype(BF), added(parts[6], left).astype(BF)
    part = part + swap(part, "z", 1)
    right, left, part, mixture = lax.optimization_barrier((right, left, part, mixture))
    right, left = shift(right, "z", 1), shift(left, "z", -1)
    part = part + swap(part, "z", 2)
    part = part + swap(part, "z", 4)
    right, left = added(parts[1], right).astype(BF), added(parts[7], left).astype(BF)
    right, left = shift(right, "z", 1), shift(left, "z", -1)
    away = added(held[0, 1], up[1], down[1]).astype(BF)
    away, part = lax.optimization_barrier((away, part))
    away = swap(away, "yh", 1)
    for low, axis, step in reversed(lows):
        other = swap(part, axis, step)
        part = jnp.where(low, jnp.concatenate([part, other]), jnp.concatenate([other, part]))
        if axis == "yh":
            part, away = lax.optimization_barrier((part, away))
        elif axis == "x" and step == 2:
            part, right, left = lax.optimization_barrier((part, right, left))
    total = added(held[0, 0], up[0], down[0], away)
    away = swap(added(parts[0][1], right[1], left[1]).astype(BF), "yl", 1)
    input_grad = added(parts[0][0], right[0], left[0], away).astype(BF)
    return mixture, input_grad, total, part


def body(tokens, expert_ids, upstream, router_weight, gate_matrix, up_matrix, down_matrix):
    rows, width = tokens.shape
    top = expert_ids.shape[1]
    mine, hidden, _ = gate_matrix.shape
    peers = lax.axis_size(EXPERT)
    groups = lax.axis_size(DP)
    experts = peers * mine
    cap = rows * top * 3 // (2 * experts)
    router = router_weight.T
    packed = pl.pallas_call(
        pack_kernel,
        out_shape=jax.ShapeDtypeStruct((rows + 16, width), BF),
    )(tokens, expert_ids.T, router)
    blocks, cotangents = gather_group(packed, upstream)
    place = jnp.stack([lax.axis_index(axis) for axis in ALL]).astype(jnp.int32)
    mix, *kept = run_forward(place, blocks, gate_matrix, up_matrix, down_matrix, cap, experts)
    spreads = kept.pop(4)
    mixture = lax.psum_scatter(mix, EXPERT, scatter_dimension=0, tiled=False)
    ours, theirs, router_part, gate_backs, up_backs, logit_grads = run_backward(
        place, blocks, cotangents, down_matrix, kept, cap, groups
    )
    outs = run_input(
        gate_backs, up_backs, gate_matrix, up_matrix, router, spreads, logit_grads, cap
    )
    mixture, input_grad, total, router_grad = reduce_all(
        outs, mixture, ours, theirs, router_part
    )
    piece = hidden // groups
    both = total[0 : 2 * mine * piece].reshape(mine, 2, piece, width)
    down_grad = total[2 * mine * piece :].reshape(mine, piece, width)
    return mixture, input_grad, router_grad.T, both[:, 0], both[:, 1], down_grad


def solution(mesh):
    shape = {"x": 4, "yh": 2, "core": 2, "yl": 2, "z": 8}
    fine = jax.sharding.Mesh(mesh.devices.reshape(tuple(shape.values())), tuple(shape))
    in_specs = (
        P(ALL, None),
        P(ALL, None),
        P(ALL, None),
        P(),
        P(EXPERT, None, None),
        P(EXPERT, None, None),
        P(EXPERT, None, None),
    )
    out_specs = (
        P(ALL, None),
        P(ALL, None),
        P(),
        P(EXPERT, DP, None),
        P(EXPERT, DP, None),
        P(EXPERT, DP, None),
    )
    return jax.shard_map(body, mesh=fine, in_specs=in_specs, out_specs=out_specs, check_vma=False)
```
